32 devices in a mesh: row: 2 (over core), col: 16 (over z, y, x).
Axes of the slice: x: 2, y: 2, z: 4, core: 2. Of those that a mesh axis runs over, the one named last changes fastest.
Arguments:
- tokens: bfloat16 [272, 8192], P('row', 'col'), may hold values from -6 to 6
- w_in: bfloat16 [8192, 24576], P(None, 'col'), may hold values from -0.0625 to 0.0625
- short_filter: float32 [3, 24576], P(None, 'col'), may hold values from -3.5 to 3.5
- mr_filter: float32 [512, 128], P('col'), may hold values from -0.5 to 0.5
- skip: float32 [8192], P('col'), may hold values from 0.5 to 1.5
- w_out: bfloat16 [8192, 8192], P(None, 'col'), may hold values from -0.0625 to 0.0625
- grad_out: bfloat16 [272, 8192], P('row', 'col'), may hold values from -0.119628906 to 0.119628906
Outputs:
- block_out: bfloat16 [272, 8192], P('row', 'col')
- filter_grad: float32 [512, 128], P('col')
- skip_grad: float32 [8192], P('col')
The draws below stay inside these ranges and needn't reach their ends.
All inputs are finite; a program needn't handle non-finite values.
Results may differ from the reference program's by a relative error of at most 0.0085.
Values may be sent and summed in bfloat16 or wider, within the bound.
No kernel may reach another device: no remote copies, remote signals or barrier semaphores. Data moves between devices by JAX's collectives and lax.ppermute only.
A program may use at most 128 MiB of HBM per device.

```python
import jax
import jax.numpy as jnp
from jax import lax

D = 8192
GSIZE = 16
TAPS = 128
GROUPS = 512
SEQ = 272


def level_of(stream_key, extent, cuts, least, top_value):
    def one(axis_at, blocks):
        heights = jax.random.uniform(jax.random.fold_in(jax.random.fold_in(stream_key, 6), axis_at), (blocks,), jnp.float32, least / len(cuts), top_value / len(cuts))
        return jnp.repeat(jnp.exp(heights), extent[axis_at] // blocks).reshape((-1,) + (1,) * (len(extent) - axis_at - 1))

    level = one(*cuts[0])
    for cut in cuts[1:]:
        level = level * one(*cut)
    return level


def normal_values(stream_key, extent, spread, limit, shards=(), held_as=jnp.bfloat16):
    entries = spread * jax.random.normal(stream_key, extent, jnp.float32)
    if shards:
        entries = entries * level_of(stream_key, extent, shards, -0.22, 0.18)
    return jnp.clip(entries, -limit, limit).astype(held_as)


def setup_inputs(seed: int = 0) -> dict:
    key_of = jax.random.split(jax.random.key(seed), 8)
    tokens = normal_values(key_of[0], (SEQ, D), 1.0, 6.0, ((0, 2), (1, 16)))
    w_in = normal_values(key_of[1], (D, 3 * D), D ** -0.5, 0.0625, ((1, 16),))
    short_filter = normal_values(key_of[2], (3, 3 * D), 3 ** -0.5, 3.5, ((1, 16),), jnp.float32)
    mr_filter = normal_values(key_of[3], (GROUPS, TAPS), TAPS ** -0.5, 0.5, ((0, 16),), jnp.float32)
    skip = jnp.clip(0.5 + 1.0 * jax.random.uniform(key_of[4], (D,), jnp.float32) ** level_of(key_of[4], (D,), ((0, 16),), -0.2, 0.2), 0.5, 1.5)
    w_out = normal_values(key_of[5], (D, D), D ** -0.5, 0.0625, ((1, 16),))
    grad_out = normal_values(key_of[6], (SEQ, D), 0.02, 0.119628906, ((0, 2), (1, 16)))
    return dict(tokens=tokens, w_in=w_in, short_filter=short_filter, mr_filter=mr_filter, skip=skip, w_out=w_out, grad_out=grad_out)


def reference(tokens, w_in, short_filter, mr_filter, skip, w_out, grad_out):
    seq_len = tokens.shape[0]
    projected = jnp.dot(tokens, w_in, preferred_element_type=jnp.float32).astype(jnp.bfloat16)
    projected = lax.optimization_barrier(projected).astype(jnp.float32)
    padded = jnp.pad(projected, ((2, 0), (0, 0)))
    short = short_filter[0] * padded[2:] + short_filter[1] * padded[1:-1] + short_filter[2] * padded[:-2]
    branches = short.reshape(seq_len, GROUPS, 3, GSIZE)
    query = branches[:, :, 0, :].reshape(seq_len, D)
    mixed = (branches[:, :, 1, :] * branches[:, :, 2, :]).reshape(seq_len, D)
    mixed_pad = jnp.pad(mixed, ((TAPS - 1, 0), (0, 0)))
    tap_table = jnp.repeat(mr_filter, GSIZE, axis=0).T

    def add_tap(step, running):
        window = lax.dynamic_slice_in_dim(mixed_pad, TAPS - 1 - step, seq_len, 0)
        return running + tap_table[step] * window
    longconv = lax.fori_loop(0, TAPS, add_tap, jnp.zeros((seq_len, D), jnp.float32))
    gated = (query * (longconv + skip * mixed)).astype(jnp.bfloat16)
    block_out = jnp.dot(gated, w_out, preferred_element_type=jnp.float32).astype(jnp.bfloat16)
    grad_gated = jnp.dot(grad_out, w_out.T, preferred_element_type=jnp.float32)
    weighted = grad_gated * query

    def tap_grad(step):
        window = lax.dynamic_slice_in_dim(mixed_pad, TAPS - 1 - step, seq_len, 0)
        return lax.optimization_barrier(jnp.sum((weighted * window).reshape(seq_len, GROUPS, GSIZE), axis=(0, 2)))
    filter_grad = lax.map(tap_grad, jnp.arange(TAPS, dtype=jnp.int32)).T
    skip_grad = lax.optimization_barrier(jnp.sum(weighted * mixed, axis=0))
    return (block_out, filter_grad, skip_grad)
```

```python
import functools

import jax
import jax.numpy as jnp
from jax import lax
from jax.experimental import pallas as pl
from jax.experimental.pallas import tpu as pltpu
from jax.sharding import PartitionSpec as P

F32 = jnp.float32
BF16 = jnp.bfloat16
VMEM_SPEC = pl.BlockSpec(memory_space=pltpu.VMEM)
SMEM_SPEC = pl.BlockSpec(memory_space=pltpu.SMEM)
ANY_SPEC = pl.BlockSpec(memory_space=pl.ANY)
WEIGHT_SLOTS = 4
VMEM_LIMIT = 24 * 2**20


def split_axis(size):
    low = 1
    while low * low < size and size % (low * 2) == 0:
        low *= 2
    return size // low, low


def swap_low(block, high, low, k):
    route = [(h * low + l, h * low + (l ^ k)) for h in range(high) for l in range(low)]
    return lax.ppermute(block, "col", route)


def shift_high(block, high, low, k):
    route = [(h * low + l, ((h + k) % high) * low + l) for h in range(high) for l in range(low)]
    return lax.ppermute(block, "col", route)


def spread(block, high, low):
    near = [swap_low(block, high, low, k) for k in range(1, low)]
    line = [shift_high(block, high, low, j) for j in range(1, high)]
    stacked = jnp.stack(line)
    far = [swap_low(stacked, high, low, k) for k in range(1, low)]
    return near, line, far


def owners_of(high, low):
    me = lax.axis_index("col")
    h, l = me // low, me % low
    near = [h * low + (l ^ k) for k in range(1, low)]
    line = [((h - j + high) % high) * low + l for j in range(1, high)]
    far = [[((h - j + high) % high) * low + (l ^ k) for j in range(1, high)] for k in range(1, low)]
    return me, near, line, far


def accumulate_kernel(counts, has_total, width, owners, *refs):
    pieces = refs[: len(counts)]
    refs = refs[len(counts) :]
    total = None
    if has_total:
        total, refs = refs[0], refs[1:]
    weights, out, sums, held, sems = refs
    order = [(p, i) for p, count in enumerate(counts) for i in range(count or 1)]
    depth = held.shape[1]

    def fetch(step):
        start = pl.multiple_of(owners[step] * depth, depth)
        slot = step % WEIGHT_SLOTS
        return pltpu.make_async_copy(
            weights.at[pl.ds(start, depth), :], held.at[slot], sems.at[slot]
        )

    for step in range(min(WEIGHT_SLOTS, len(order))):
        fetch(step).start()
    for step, (p, i) in enumerate(order):
        fetch(step).wait()
        slot = step % WEIGHT_SLOTS
        rows = pieces[p][i] if counts[p] else pieces[p][...]
        for at in range(0, held.shape[2], width):
            cols = slice(at, at + width)
            term = jnp.dot(rows, held[slot, :, cols], preferred_element_type=F32)
            if step == 0 and total is not None:
                term = term + total[:, cols]
            if step:
                term = term + sums[:, cols]
            if step + 1 == len(order):
                out[:, cols] = term.astype(out.dtype)
            else:
                sums[:, cols] = term
        if step + WEIGHT_SLOTS < len(order):
            fetch(step + WEIGHT_SLOTS).start()


def accumulate(total, pieces, owners, weights, out_type, name):
    counts = tuple(0 if piece.ndim == 2 else piece.shape[0] for piece in pieces)
    rows, depth = pieces[0].shape[-2:]
    columns = weights.shape[1]
    width = next(w for w in (512, 256, 128, columns) if columns % w == 0)
    steps = len(owners)
    operands = [jnp.stack(owners).astype(jnp.int32), *pieces]
    if total is not None:
        operands.append(total)
    return pl.pallas_call(
        functools.partial(accumulate_kernel, counts, total is not None, width),
        out_shape=jax.ShapeDtypeStruct((rows, columns), out_type),
        in_specs=[SMEM_SPEC] + [VMEM_SPEC] * (len(operands) - 1) + [ANY_SPEC],
        out_specs=VMEM_SPEC,
        scratch_shapes=[
            pltpu.VMEM((rows, columns), F32),
            pltpu.VMEM((WEIGHT_SLOTS, depth, columns), weights.dtype),
            pltpu.SemaphoreType.DMA((WEIGHT_SLOTS,)),
        ],
        compiler_params=pltpu.CompilerParams(vmem_limit_bytes=VMEM_LIMIT),
        cost_estimate=pl.CostEstimate(
            flops=2 * steps * rows * depth * columns,
            bytes_accessed=steps * depth * columns * 2 + rows * columns * 8,
            transcendentals=0,
        ),
        name=name,
    )(*operands, weights)


def partials_kernel(owners, grads, weights, *refs):
    outs, (held, sems) = refs[:-2], refs[-2:]
    order = [(o, i) for o, out in enumerate(outs) for i in range(out.shape[0])]
    depth = held.shape[1]

    def fetch(step):
        start = pl.multiple_of(owners[step] * depth, depth)
        slot = step % WEIGHT_SLOTS
        return pltpu.make_async_copy(
            weights.at[pl.ds(start, depth), :], held.at[slot], sems.at[slot]
        )

    for step in range(min(WEIGHT_SLOTS, len(order))):
        fetch(step).start()
    for step, (o, i) in enumerate(order):
        fetch(step).wait()
        term = lax.dot_general(
            grads[...],
            held[step % WEIGHT_SLOTS],
            (((1,), (1,)), ((), ())),
            preferred_element_type=F32,
        )
        outs[o][i] = term.astype(outs[o].dtype)
        if step + WEIGHT_SLOTS < len(order):
            fetch(step + WEIGHT_SLOTS).start()


def partials(grads, weights, high, low):
    me = lax.axis_index("col")
    h, l = me // low, me % low
    owners = [((h + j) % high) * low + (l ^ k) for k in range(low) for j in range(high)]
    rows, features = grads.shape
    depth = weights.shape[0] // (high * low)
    shape = jax.ShapeDtypeStruct((high, rows, depth), BF16)
    return pl.pallas_call(
        partials_kernel,
        out_shape=[shape] * low,
        in_specs=[SMEM_SPEC, VMEM_SPEC, ANY_SPEC],
        out_specs=[VMEM_SPEC] * low,
        scratch_shapes=[
            pltpu.VMEM((WEIGHT_SLOTS, depth, features), weights.dtype),
            pltpu.SemaphoreType.DMA((WEIGHT_SLOTS,)),
        ],
        compiler_params=pltpu.CompilerParams(vmem_limit_bytes=VMEM_LIMIT),
        cost_estimate=pl.CostEstimate(
            flops=2 * rows * features * weights.shape[0],
            bytes_accessed=2 * weights.shape[0] * (features + rows),
            transcendentals=0,
        ),
        name="grad_partials",
    )(jnp.stack(owners).astype(jnp.int32), grads, weights)


def halves(value):
    top = value.astype(BF16)
    return top, (value - top.astype(F32)).astype(BF16)


def band_kernel(taps, top, rest):
    rows, span = top.shape[1:]
    for g in range(top.shape[0]):
        spreadout = jnp.broadcast_to(taps[g : g + 1, :], (rows, span))
        band = pltpu.roll(spreadout, 0, 1, stride=1, stride_axis=0)
        top[g], rest[g] = halves(band)


def band_table(mr_filter):
    groups, taps = mr_filter.shape
    first = jnp.concatenate(
        [jnp.zeros((groups, 1), F32), mr_filter[:, ::-1], jnp.zeros((groups, taps - 1), F32)], 1
    )
    shape = jax.ShapeDtypeStruct((groups, taps, 2 * taps), BF16)
    return pl.pallas_call(
        band_kernel,
        out_shape=[shape, shape],
        in_specs=[VMEM_SPEC],
        out_specs=[VMEM_SPEC] * 2,
        compiler_params=pltpu.CompilerParams(vmem_limit_bytes=VMEM_LIMIT),
        name="band_table",
    )(first)


def mixing_kernel(groups, earlier, projected, order, filters, top, rest, skip, gated, query, mixed):
    rows = projected.shape[0]
    channels = skip.shape[1]
    taps = top.shape[1]
    span = 2 * taps
    extended = jnp.concatenate([earlier[...].astype(F32), projected[...].astype(F32)], 0).astype(BF16)
    lines = jnp.dot(extended, order[...], preferred_element_type=F32)
    short = (
        filters[0:1, :] * lines
        + filters[1:2, :] * pltpu.roll(lines, 1, 0)
        + filters[2:3, :] * pltpu.roll(lines, 2, 0)
    )
    own_query = short[rows:, :channels]
    both = short[:, channels : 2 * channels] * short[:, 2 * channels :]
    query[...] = own_query
    mixed[...] = both
    both_top, both_rest = halves(both)
    pair = jnp.concatenate([both_top, both_rest], 1)
    lane_group = lax.broadcasted_iota(jnp.int32, (taps, channels), 1) // (channels // groups)
    spare = rows - taps
    first = rows - taps
    body = jnp.zeros((taps, channels), F32)
    tail = jnp.zeros((spare, channels), F32)
    for g in range(groups):
        here = jnp.dot(top[g], pair[first : first + span], preferred_element_type=F32)
        here = here[:, :channels] + here[:, channels:]
        here = here + jnp.dot(rest[g], both_top[first : first + span], preferred_element_type=F32)
        body = jnp.where(lane_group == g, here, body)
        last_top, last_rest = top[g, taps - spare :], rest[g, taps - spare :]
        after = jnp.dot(last_top, pair[2 * first :], preferred_element_type=F32)
        after = after[:, :channels] + after[:, channels:]
        after = after + jnp.dot(last_rest, both_top[2 * first :], preferred_element_type=F32)
        tail = jnp.where(lane_group[:spare] == g, after, tail)
    longconv = jnp.concatenate([body, tail], 0)
    gated[...] = (own_query * (longconv + skip[...] * both[rows:])).astype(gated.dtype)


def mixing(earlier, projected, order, filters, bands, skip, groups):
    rows, columns = projected.shape
    channels = columns // 3
    block = order.shape[0] // 3
    steps = channels // block
    per_step = groups // steps
    taps = bands[0].shape[1]
    ext = 2 * rows
    table = pl.BlockSpec((per_step, taps, 2 * taps), lambda i: (i, 0, 0))
    return pl.pallas_call(
        functools.partial(mixing_kernel, per_step),
        grid=(steps,),
        out_shape=[
            jax.ShapeDtypeStruct((rows, channels), BF16),
            jax.ShapeDtypeStruct((rows, channels), F32),
            jax.ShapeDtypeStruct((ext, channels), F32),
        ],
        in_specs=[
            pl.BlockSpec((rows, 3 * block), lambda i: (0, i)),
            pl.BlockSpec((rows, 3 * block), lambda i: (0, i)),
            pl.BlockSpec((3 * block, 3 * block), lambda i: (0, 0)),
            pl.BlockSpec((3, 3 * block), lambda i: (0, i)),
            table,
            table,
            pl.BlockSpec((1, block), lambda i: (0, i)),
        ],
        out_specs=[
            pl.BlockSpec((rows, block), lambda i: (0, i)),
            pl.BlockSpec((rows, block), lambda i: (0, i)),
            pl.BlockSpec((ext, block), lambda i: (0, i)),
        ],
        compiler_params=pltpu.CompilerParams(vmem_limit_bytes=VMEM_LIMIT),
        cost_estimate=pl.CostEstimate(
            flops=2 * 2 * groups * rows * 2 * taps * 2 * block,
            bytes_accessed=4 * ext * channels + 6 * ext * channels + 8 * groups * taps * taps,
            transcendentals=0,
        ),
        name="mixing",
    )(earlier, projected, order, filters, *bands, skip)


def tap_grad_kernel(groups, pieces, *refs):
    grads, (query, mixed, flip, taps_out, skip_out) = refs[:pieces], refs[pieces:]
    total = grads[0][...].astype(F32)
    for piece in grads[1:]:
        total = total + piece[...].astype(F32)
    weighted = total * query[...]
    rows, channels = weighted.shape
    taps = taps_out.shape[1]
    span = 2 * taps
    first = rows - taps
    spare = rows - taps
    both = mixed[...]
    skip_out[...] = jnp.sum(weighted * both[rows:], axis=0, keepdims=True)
    both_top, both_rest = halves(both)

    def backwards(start):
        ends = [
            jnp.dot(flip[...], part[start : start + span], preferred_element_type=F32).astype(BF16)
            for part in (both_top, both_rest)
        ]
        return jnp.concatenate([ends[0], ends[0], ends[1]], 1)

    near, far = backwards(first), backwards(2 * first)
    parts = halves(weighted)
    lane_group = lax.broadcasted_iota(jnp.int32, (rows, channels), 1) // (channels // groups)
    contract = (((1,), (1,)), ((), ()))
    for g in range(groups):
        top, rest = [jnp.where(lane_group == g, part.astype(F32), 0.0).astype(BF16) for part in parts]
        sides = jnp.concatenate([top, rest, top], 1)
        body = lax.dot_general(sides[:taps], near, contract, preferred_element_type=F32)
        tail = lax.dot_general(sides[taps:], far, contract, preferred_element_type=F32)
        body = jnp.concatenate([body[: taps - spare], body[taps - spare :] + tail], 0)
        skewed = pltpu.roll(body, 0, 1, stride=1, stride_axis=0)
        line = jnp.sum(skewed, axis=0, keepdims=True)
        taps_out[g : g + 1, :] = pltpu.roll(line, span - (taps - 1), 1)[:, :taps]


def tap_grad(grads, query, mixed, groups, taps):
    rows, channels = query.shape
    ext = mixed.shape[0]
    block = 128 if channels % 128 == 0 else channels
    steps = channels // block
    per_step = groups // steps
    span = 2 * taps
    flip = jnp.eye(span, dtype=BF16)[::-1]
    one = pl.BlockSpec((rows, block), lambda i: (0, i))
    return pl.pallas_call(
        functools.partial(tap_grad_kernel, per_step, len(grads)),
        grid=(steps,),
        out_shape=[
            jax.ShapeDtypeStruct((groups, taps), F32),
            jax.ShapeDtypeStruct((1, channels), F32),
        ],
        in_specs=[one] * (len(grads) + 1)
        + [pl.BlockSpec((ext, block), lambda i: (0, i)), pl.BlockSpec((span, span), lambda i: (0, 0))],
        out_specs=[
            pl.BlockSpec((per_step, taps), lambda i: (i, 0)),
            pl.BlockSpec((1, block), lambda i: (0, i)),
        ],
        compiler_params=pltpu.CompilerParams(vmem_limit_bytes=VMEM_LIMIT),
        cost_estimate=pl.CostEstimate(
            flops=2 * groups * rows * span * 3 * block,
            bytes_accessed=4 * ext * channels + 6 * rows * channels,
            transcendentals=0,
        ),
        name="tap_grad",
    )(*grads, query, mixed, flip)


def branch_order(block, width):
    to = jnp.arange(3 * block)
    branch, channel = to // block, to % block
    source = 3 * width * (channel // width) + width * branch + channel % width
    return (jnp.arange(3 * block)[:, None] == source[None, :]).astype(BF16)


def local(tokens, w_in, short_filter, mr_filter, skip, w_out, grad_out):
    high, low = split_axis(lax.axis_size("col"))
    row_size = lax.axis_size("row")
    channels = tokens.shape[1]
    groups, taps = mr_filter.shape
    width = channels // groups
    block = 128 if channels % 128 == 0 else channels
    me, near_own, line_own, far_own = owners_of(high, low)
    far_first, far_last = far_own[:-1], far_own[-1:]

    def contract(gathered, weights, out_type, name):
        own, (near, line, far) = gathered
        total = accumulate(
            None, [own, *near, *line], [me, *near_own, *line_own], weights, F32, name + "_near"
        )
        if far_first:
            owners = [o for each in far_first for o in each]
            total = accumulate(total, far[:-1], owners, weights, F32, name + "_far")
        return accumulate(total, far[-1:], far_last[0], weights, out_type, name + "_last")

    order = branch_order(block, width)
    filters = short_filter.reshape(3, channels // block, block // width, 3, width)
    filters = filters.transpose(0, 1, 3, 2, 4).reshape(3, 3 * channels)
    bands = band_table(mr_filter)

    projected = contract((tokens, spread(tokens, high, low)), w_in, BF16, "project")
    earlier = lax.ppermute(projected, "row", [(r, r + 1) for r in range(row_size - 1)])

    kept, *sent = partials(grad_out, w_out, high, low)
    arrived = [swap_low(part, high, low, k + 1) for k, part in enumerate(sent)]
    sums = [
        functools.reduce(jnp.add, [part[j].astype(F32) for part in (kept, *arrived)]).astype(BF16)
        for j in range(high)
    ]
    grads = [sums[0]] + [shift_high(sums[j], high, low, j) for j in range(1, high)]

    gated, query, mixed = mixing(earlier, projected, order, filters, bands, skip[None], groups)
    block_out = contract((gated, spread(gated, high, low)), w_out, BF16, "output")

    tap_part, skip_part = tap_grad(grads, query, mixed, groups, taps)
    if row_size == 2:
        flat = jnp.concatenate([tap_part.reshape(-1), skip_part.reshape(-1)])
        flat = flat + lax.ppermute(flat, "row", [(0, 1), (1, 0)])
        filter_grad = flat[: groups * taps].reshape(groups, taps)
        skip_grad = flat[groups * taps :]
    else:
        filter_grad, skip_grad = lax.psum((tap_part, skip_part.reshape(-1)), "row")
    return (block_out, filter_grad, skip_grad)


def solution(mesh):
    in_specs = (
        P("row", "col"),
        P(None, "col"),
        P(None, "col"),
        P("col", None),
        P("col"),
        P(None, "col"),
        P("row", "col"),
    )
    out_specs = (P("row", "col"), P("col", None), P("col"))
    return jax.shard_map(local, mesh=mesh, in_specs=in_specs, out_specs=out_specs, check_vma=False)
```

```python
import functools

import jax
import jax.numpy as jnp
from jax import lax
from jax.experimental import pallas as pl
from jax.experimental.pallas import tpu as pltpu
from jax.sharding import PartitionSpec as P

F32 = jnp.float32
BF16 = jnp.bfloat16
VMEM_SPEC = pl.BlockSpec(memory_space=pltpu.VMEM)
SMEM_SPEC = pl.BlockSpec(memory_space=pltpu.SMEM)
HBM_SPEC = pl.BlockSpec(memory_space=pltpu.HBM)
WEIGHT_SLOTS = 4
VMEM_LIMIT = 47 * 2**20


def split_axis(size):
    low = 1
    while low * low < size and size % (low * 2) == 0:
        low *= 2
    return size // low, low


def low_masks(low, parity):
    bits = [1 << i for i in range(low.bit_length() - 1)]
    return bits[::-1] if parity else bits


def swap_low(block, high, low, step):
    rows = lax.axis_size("row")
    size = high * low
    route = []
    for r in range(rows):
        mask = low_masks(low, r % 2)[step]
        route += [(r * size + c, r * size + (c ^ mask)) for c in range(size)]
    return lax.ppermute(block, ("row", "col"), route)


def shift_high(block, high, low, k):
    route = [(h * low + l, ((h + k) % high) * low + l) for h in range(high) for l in range(low)]
    return lax.ppermute(block, "col", route)


def flipped_low(low):
    parity = lax.axis_index("row") % 2
    forward, backward = low_masks(low, 0), low_masks(low, 1)
    flips = [0]
    for one, other in zip(forward, backward):
        mask = jnp.where(parity == 0, one, other)
        flips += [flip + mask for flip in flips]
    return flips


def shift_groups(high):
    order = []
    for k in range(1, high // 2 + 1):
        order += [k] if 2 * k == high else [k, high - k]
    return [group for group in (order[:2], order[2:]) if group]


def spread(block, high, low):
    me = lax.axis_index("col")
    h, l = me // low, me % low
    flips = flipped_low(low)
    moved = {k: shift_high(block, high, low, k) for group in shift_groups(high) for k in group}

    def plane(item):
        items = [item]
        for step in range(low.bit_length() - 1):
            items += [swap_low(each, high, low, step) for each in items]
        return items[1:]

    stages = [([block, *plane(block)], [[h * low + (l ^ flip)] for flip in flips])]
    for group in shift_groups(high):
        item = moved[group[0]] if len(group) == 1 else jnp.stack([moved[k] for k in group])
        from_high = [(h - k + high) % high for k in group]
        stages[0][0].append(item)
        stages[0][1].append([f * low + l for f in from_high])
        owners = [[f * low + (l ^ flip) for f in from_high] for flip in flips[1:]]
        stages.append((plane(item), owners))
    return [(items, [o for each in owners for o in each]) for items, owners in stages]


def accumulate_kernel(counts, has_total, width, owners, *refs):
    pieces = refs[: len(counts)]
    refs = refs[len(counts) :]
    total = None
    if has_total:
        total, refs = refs[0], refs[1:]
    weights, out, sums, held, sems = refs
    order = [(p, i) for p, count in enumerate(counts) for i in range(count or 1)]
    depth = held.shape[1]

    def fetch(step):
        start = pl.multiple_of(owners[step] * depth, depth)
        slot = step % WEIGHT_SLOTS
        return pltpu.make_async_copy(
            weights.at[pl.ds(start, depth), :], held.at[slot], sems.at[slot]
        )

    for step in range(min(WEIGHT_SLOTS, len(order))):
        fetch(step).start()
    for step, (p, i) in enumerate(order):
        fetch(step).wait()
        slot = step % WEIGHT_SLOTS
        rows = pieces[p][i] if counts[p] else pieces[p][...]
        for at in range(0, held.shape[2], width):
            cols = slice(at, at + width)
            term = jnp.dot(rows, held[slot, :, cols], preferred_element_type=F32)
            if step == 0 and total is not None:
                term = term + total[:, cols]
            if step:
                term = term + sums[:, cols]
            if step + 1 == len(order):
                out[:, cols] = term.astype(out.dtype)
            else:
                sums[:, cols] = term
        if step + WEIGHT_SLOTS < len(order):
            fetch(step + WEIGHT_SLOTS).start()


def accumulate(total, pieces, owners, weights, out_type, name):
    counts = tuple(0 if piece.ndim == 2 else piece.shape[0] for piece in pieces)
    rows, depth = pieces[0].shape[-2:]
    columns = weights.shape[1]
    width = next(w for w in (512, 256, 128, columns) if columns % w == 0)
    steps = len(owners)
    operands = [jnp.stack(owners).astype(jnp.int32), *pieces]
    if total is not None:
        operands.append(total)
    return pl.pallas_call(
        functools.partial(accumulate_kernel, counts, total is not None, width),
        out_shape=jax.ShapeDtypeStruct((rows, columns), out_type),
        in_specs=[SMEM_SPEC] + [VMEM_SPEC] * (len(operands) - 1) + [HBM_SPEC],
        out_specs=VMEM_SPEC,
        scratch_shapes=[
            pltpu.VMEM((rows, columns), F32),
            pltpu.VMEM((WEIGHT_SLOTS, depth, columns), weights.dtype),
            pltpu.SemaphoreType.DMA((WEIGHT_SLOTS,)),
        ],
        compiler_params=pltpu.CompilerParams(vmem_limit_bytes=VMEM_LIMIT),
        cost_estimate=pl.CostEstimate(
            flops=2 * steps * rows * depth * columns,
            bytes_accessed=steps * depth * columns * 2 + rows * columns * 8,
            transcendentals=0,
        ),
        name=name,
    )(*operands, weights)


def partials_kernel(owners, grads, weights, *refs):
    outs, (held, sems) = refs[:-2], refs[-2:]
    order = [(o, i) for o, out in enumerate(outs) for i in range(out.shape[0])]
    depth = held.shape[1]

    def fetch(step):
        start = pl.multiple_of(owners[step] * depth, depth)
        slot = step % WEIGHT_SLOTS
        return pltpu.make_async_copy(
            weights.at[pl.ds(start, depth), :], held.at[slot], sems.at[slot]
        )

    for step in range(min(WEIGHT_SLOTS, len(order))):
        fetch(step).start()
    for step, (o, i) in enumerate(order):
        fetch(step).wait()
        term = lax.dot_general(
            grads[...],
            held[step % WEIGHT_SLOTS],
            (((1,), (1,)), ((), ())),
            preferred_element_type=F32,
        )
        outs[o][i] = term.astype(outs[o].dtype)
        if step + WEIGHT_SLOTS < len(order):
            fetch(step + WEIGHT_SLOTS).start()


def partials(grads, weights, high, low):
    me = lax.axis_index("col")
    h, l = me // low, me % low
    owners = [((h + j) % high) * low + (l ^ flip) for flip in flipped_low(low) for j in range(high)]
    rows, features = grads.shape
    depth = weights.shape[0] // (high * low)
    shape = jax.ShapeDtypeStruct((high, rows, depth), BF16)
    return pl.pallas_call(
        partials_kernel,
        out_shape=[shape] * low,
        in_specs=[SMEM_SPEC, VMEM_SPEC, HBM_SPEC],
        out_specs=[VMEM_SPEC] * low,
        scratch_shapes=[
            pltpu.VMEM((WEIGHT_SLOTS, depth, features), weights.dtype),
            pltpu.SemaphoreType.DMA((WEIGHT_SLOTS,)),
        ],
        compiler_params=pltpu.CompilerParams(vmem_limit_bytes=VMEM_LIMIT),
        cost_estimate=pl.CostEstimate(
            flops=2 * rows * features * weights.shape[0],
            bytes_accessed=2 * weights.shape[0] * (features + rows),
            transcendentals=0,
        ),
        name="grad_partials",
    )(jnp.stack(owners).astype(jnp.int32), grads, weights)


def halves(value):
    top = value.astype(BF16)
    return top, (value - top.astype(F32)).astype(BF16)


def band_kernel(taps, table):
    rows, span = table.shape[1:]
    for g in range(table.shape[0]):
        spreadout = jnp.broadcast_to(taps[g : g + 1, :], (rows, span))
        band = pltpu.roll(spreadout, 0, 1, stride=1, stride_axis=0)
        table[g] = band.astype(table.dtype)


def band_table(mr_filter):
    groups, taps = mr_filter.shape
    first = jnp.concatenate(
        [jnp.zeros((groups, 1), F32), mr_filter[:, ::-1], jnp.zeros((groups, taps - 1), F32)], 1
    )
    shape = jax.ShapeDtypeStruct((groups, taps, 2 * taps), BF16)
    return pl.pallas_call(
        band_kernel,
        out_shape=shape,
        in_specs=[VMEM_SPEC],
        out_specs=VMEM_SPEC,
        compiler_params=pltpu.CompilerParams(vmem_limit_bytes=VMEM_LIMIT),
        name="band_table",
    )(first)


def mixing_kernel(groups, earlier, projected, order, filters, bands, skip, gated, query, mixed):
    rows = projected.shape[0]
    channels = skip.shape[1]
    taps = bands.shape[1]
    span = 2 * taps
    extended = jnp.concatenate([earlier[...].astype(F32), projected[...].astype(F32)], 0).astype(BF16)
    lines = jnp.dot(extended, order[...], preferred_element_type=F32)
    short = (
        filters[0:1, :] * lines
        + filters[1:2, :] * pltpu.roll(lines, 1, 0)
        + filters[2:3, :] * pltpu.roll(lines, 2, 0)
    )
    own_query = short[rows:, :channels]
    both = short[:, channels : 2 * channels] * short[:, 2 * channels :]
    query[...] = own_query
    mixed[...] = both
    both_top, both_rest = halves(both)
    pair = jnp.concatenate([both_top, both_rest], 1)
    lane_group = lax.broadcasted_iota(jnp.int32, (taps, channels), 1) // (channels // groups)
    spare = rows - taps
    first = rows - taps
    body = jnp.zeros((taps, channels), F32)
    tail = jnp.zeros((spare, channels), F32)
    for g in range(groups):
        here = jnp.dot(bands[g], pair[first : first + span], preferred_element_type=F32)
        here = here[:, :channels] + here[:, channels:]
        body = jnp.where(lane_group == g, here, body)
        last = bands[g, taps - spare :]
        after = jnp.dot(last, pair[2 * first :], preferred_element_type=F32)
        after = after[:, :channels] + after[:, channels:]
        tail = jnp.where(lane_group[:spare] == g, after, tail)
    longconv = jnp.concatenate([body, tail], 0)
    gated[...] = (own_query * (longconv + skip[...] * both[rows:])).astype(gated.dtype)


def mixing(earlier, projected, order, filters, bands, skip, groups):
    rows, columns = projected.shape
    channels = columns // 3
    block = order.shape[0] // 3
    steps = channels // block
    per_step = groups // steps
    taps = bands.shape[1]
    ext = 2 * rows
    table = pl.BlockSpec((per_step, taps, 2 * taps), lambda i: (i, 0, 0))
    return pl.pallas_call(
        functools.partial(mixing_kernel, per_step),
        grid=(steps,),
        out_shape=[
            jax.ShapeDtypeStruct((rows, channels), BF16),
            jax.ShapeDtypeStruct((rows, channels), F32),
            jax.ShapeDtypeStruct((ext, channels), F32),
        ],
        in_specs=[
            pl.BlockSpec((rows, 3 * block), lambda i: (0, i)),
            pl.BlockSpec((rows, 3 * block), lambda i: (0, i)),
            pl.BlockSpec((3 * block, 3 * block), lambda i: (0, 0)),
            pl.BlockSpec((3, 3 * block), lambda i: (0, i)),
            table,
            pl.BlockSpec((1, block), lambda i: (0, i)),
        ],
        out_specs=[
            pl.BlockSpec((rows, block), lambda i: (0, i)),
            pl.BlockSpec((rows, block), lambda i: (0, i)),
            pl.BlockSpec((ext, block), lambda i: (0, i)),
        ],
        compiler_params=pltpu.CompilerParams(vmem_limit_bytes=VMEM_LIMIT),
        cost_estimate=pl.CostEstimate(
            flops=2 * 2 * groups * rows * 2 * taps * 2 * block,
            bytes_accessed=4 * ext * channels + 6 * ext * channels + 4 * groups * taps * taps,
            transcendentals=0,
        ),
        name="mixing",
    )(earlier, projected, order, filters, bands, skip)


def tap_grad_kernel(groups, pieces, *refs):
    grads, (query, mixed, taps_out, skip_out) = refs[:pieces], refs[pieces:]
    total = grads[0][...].astype(F32)
    for piece in grads[1:]:
        total = total + piece[...].astype(F32)
    weighted = total * query[...]
    rows, channels = weighted.shape
    taps = taps_out.shape[1]
    span = 2 * taps
    first = rows - taps
    spare = rows - taps
    both = mixed[...]
    skip_out[...] = jnp.sum(weighted * both[rows:], axis=0, keepdims=True)
    both_top = both.astype(BF16)
    flip = jnp.where(
        lax.broadcasted_iota(jnp.int32, (span, span), 0)
        + lax.broadcasted_iota(jnp.int32, (span, span), 1)
        == span - 1,
        1.0,
        0.0,
    ).astype(BF16)

    def backwards(start):
        end = jnp.dot(flip, both_top[start : start + span], preferred_element_type=F32)
        return jnp.concatenate([end.astype(BF16)] * 2, 1)

    near, far = backwards(first), backwards(2 * first)
    parts = jnp.concatenate(halves(weighted), 1)
    lane_group = (lax.broadcasted_iota(jnp.int32, (1, 2 * channels), 1) % channels) // (
        channels // groups
    )
    contract = (((1,), (1,)), ((), ()))
    for g in range(groups):
        sides = parts * jnp.where(lane_group == g, 1.0, 0.0).astype(BF16)
        body = lax.dot_general(sides[:taps], near, contract, preferred_element_type=F32)
        tail = lax.dot_general(sides[taps:], far, contract, preferred_element_type=F32)
        body = jnp.concatenate([body[: taps - spare], body[taps - spare :] + tail], 0)
        skewed = pltpu.roll(body, 0, 1, stride=1, stride_axis=0)
        line = jnp.sum(skewed, axis=0, keepdims=True)
        taps_out[g : g + 1, :] = pltpu.roll(line, span - (taps - 1), 1)[:, :taps]


def tap_grad(grads, query, mixed, groups, taps):
    rows, channels = query.shape
    ext = mixed.shape[0]
    block = 128 if channels % 128 == 0 else channels
    steps = channels // block
    per_step = groups // steps
    span = 2 * taps
    one = pl.BlockSpec((rows, block), lambda i: (0, i))
    return pl.pallas_call(
        functools.partial(tap_grad_kernel, per_step, len(grads)),
        grid=(steps,),
        out_shape=[
            jax.ShapeDtypeStruct((groups, taps), F32),
            jax.ShapeDtypeStruct((1, channels), F32),
        ],
        in_specs=[one] * (len(grads) + 1)
        + [pl.BlockSpec((ext, block), lambda i: (0, i))],
        out_specs=[
            pl.BlockSpec((per_step, taps), lambda i: (i, 0)),
            pl.BlockSpec((1, block), lambda i: (0, i)),
        ],
        compiler_params=pltpu.CompilerParams(vmem_limit_bytes=VMEM_LIMIT),
        cost_estimate=pl.CostEstimate(
            flops=2 * groups * rows * span * 2 * block,
            bytes_accessed=4 * ext * channels + 6 * rows * channels,
            transcendentals=0,
        ),
        name="tap_grad",
    )(*grads, query, mixed)


def branch_order(block, width):
    to = jnp.arange(3 * block)
    branch, channel = to // block, to % block
    source = 3 * width * (channel // width) + width * branch + channel % width
    return (jnp.arange(3 * block)[:, None] == source[None, :]).astype(BF16)


def local(tokens, w_in, short_filter, mr_filter, skip, w_out, grad_out):
    high, low = split_axis(lax.axis_size("col"))
    row_size = lax.axis_size("row")
    channels = tokens.shape[1]
    groups, taps = mr_filter.shape
    width = channels // groups
    block = 128 if channels % 128 == 0 else channels

    def contract(stages, weights, out_type, name):
        total = None
        for at, (pieces, owners) in enumerate(stages):
            last = at + 1 == len(stages)
            total = accumulate(
                total, pieces, owners, weights, out_type if last else F32, f"{name}_{at}"
            )
        return total

    order = branch_order(block, width)
    filters = short_filter.reshape(3, channels // block, block // width, 3, width)
    filters = filters.transpose(0, 1, 3, 2, 4).reshape(3, 3 * channels)
    bands = band_table(mr_filter)
    grad_out, order, filters, bands = lax.optimization_barrier((grad_out, order, filters, bands))

    stages = spread(tokens, high, low)
    parts = partials(grad_out, w_out, high, low)
    parts, stages[-1][0][-1] = lax.optimization_barrier((parts, stages[-1][0][-1]))
    for step in reversed(range(low.bit_length() - 1)):
        half = 1 << step
        moved = [swap_low(part, high, low, step) for part in parts[half:]]
        sums = [part.astype(F32) + more.astype(F32) for part, more in zip(parts, moved)]
        parts = [part.astype(BF16) for part in sums] if step else sums
    sums = [parts[0][j].astype(BF16) for j in range(high)]
    grads = [sums[0]] + [shift_high(sums[j], high, low, j) for j in range(1, high)]

    projected = contract(stages, w_in, BF16, "project")
    earlier = lax.ppermute(projected, "row", [(r, r + 1) for r in range(row_size - 1)])

    gated, query, mixed = mixing(earlier, projected, order, filters, bands, skip[None], groups)
    block_out = contract(spread(gated, high, low), w_out, BF16, "output")

    tap_part, skip_part = tap_grad(grads, query, mixed, groups, taps)
    if row_size == 2:
        flat = jnp.concatenate([tap_part.reshape(-1), skip_part.reshape(-1)])
        flat = flat + lax.ppermute(flat, "row", [(0, 1), (1, 0)])
        filter_grad = flat[: groups * taps].reshape(groups, taps)
        skip_grad = flat[groups * taps :]
    else:
        filter_grad, skip_grad = lax.psum((tap_part, skip_part.reshape(-1)), "row")
    return (block_out, filter_grad, skip_grad)


def solution(mesh):
    in_specs = (
        P("row", "col"),
        P(None, "col"),
        P(None, "col"),
        P("col", None),
        P("col"),
        P(None, "col"),
        P("row", "col"),
    )
    out_specs = (P("row", "col"), P("col", None), P("col"))
    return jax.shard_map(local, mesh=mesh, in_specs=in_specs, out_specs=out_specs, check_vma=False)
```

```python
import functools

import jax
import jax.numpy as jnp
from jax import lax
from jax.experimental import pallas as pl
from jax.experimental.pallas import tpu as pltpu
from jax.sharding import PartitionSpec as P

F32 = jnp.float32
BF16 = jnp.bfloat16
VMEM_SPEC = pl.BlockSpec(memory_space=pltpu.VMEM)
SMEM_SPEC = pl.BlockSpec(memory_space=pltpu.SMEM)
HBM_SPEC = pl.BlockSpec(memory_space=pltpu.HBM)
WEIGHT_SLOTS = 4
VMEM_LIMIT = 47 * 2**20


def split_axis(size):
    low = 1
    while low * low < size and size % (low * 2) == 0:
        low *= 2
    return size // low, low


def low_masks(low, parity):
    bits = [1 << i for i in range(low.bit_length() - 1)]
    return bits[::-1] if parity else bits


def swap_low(block, high, low, step):
    rows = lax.axis_size("row")
    size = high * low
    route = []
    for r in range(rows):
        mask = low_masks(low, r % 2)[step]
        route += [(r * size + c, r * size + (c ^ mask)) for c in range(size)]
    return lax.ppermute(block, ("row", "col"), route)


def shift_high(block, high, low, k):
    route = [(h * low + l, ((h + k) % high) * low + l) for h in range(high) for l in range(low)]
    return lax.ppermute(block, "col", route)


def flipped_low(low):
    parity = lax.axis_index("row") % 2
    forward, backward = low_masks(low, 0), low_masks(low, 1)
    flips = [0]
    for one, other in zip(forward, backward):
        mask = jnp.where(parity == 0, one, other)
        flips += [flip + mask for flip in flips]
    return flips


def spread(block, high, low):
    me = lax.axis_index("col")
    h, l = me // low, me % low
    flips = flipped_low(low)
    shifts = [k for k in range(1, high) if 2 * k != high] + [k for k in (high // 2,) if 2 * k == high]
    line = [shift_high(block, high, low, k) for k in shifts]
    from_high = [(h - k + high) % high for k in shifts]

    def plane(item):
        items = [item]
        for step in range(low.bit_length() - 1):
            items += [swap_low(each, high, low, step) for each in items]
        return items[1:]

    near = plane(block)
    line, near[:2] = lax.optimization_barrier((line, near[:2]))
    far = plane(jnp.stack(line))
    owners = [[h * low + (l ^ flip)] for flip in flips]
    first = ([block, *near], owners)
    owners = [[f * low + (l ^ flip) for f in from_high] for flip in flips]
    cut = max(1, len(far) - 1)
    second = ([*line, *far[:cut]], owners[: 1 + cut])
    stages = [first, second, (far[cut:], owners[1 + cut :])]
    return [(items, [o for each in owns for o in each]) for items, owns in stages if items]


def accumulate_kernel(counts, has_total, loads, width, owners, *refs):
    refs = list(refs)
    pieces = [refs.pop(0) for _ in counts]
    total = refs.pop(0) if has_total else None
    weights, out = refs[:2]
    refs = refs[2:]
    ahead = refs.pop(0) if loads else None
    sums, held, sems, ahead_sems = refs
    order = [(p, i) for p, count in enumerate(counts) for i in range(count or 1)]
    resident = len(weights.shape) == 3
    depth = weights.shape[1] if resident else held.shape[1]

    def rows_of(step):
        return weights.at[pl.ds(pl.multiple_of(owners[step] * depth, depth), depth), :]

    def fetch(step):
        slot = step % WEIGHT_SLOTS
        return pltpu.make_async_copy(rows_of(step), held.at[slot], sems.at[slot])

    def load(at):
        return pltpu.make_async_copy(rows_of(len(order) + at), ahead.at[at], ahead_sems.at[at])

    if not resident:
        for step in range(min(WEIGHT_SLOTS, len(order))):
            fetch(step).start()
    for step, (p, i) in enumerate(order):
        if not resident:
            fetch(step).wait()
        slot = step % WEIGHT_SLOTS
        rows = pieces[p][i] if counts[p] else pieces[p][...]
        for at in range(0, out.shape[1], width):
            cols = slice(at, at + width)
            part = weights[step, :, cols] if resident else held[slot, :, cols]
            term = jnp.dot(rows, part, preferred_element_type=F32)
            if step == 0 and total is not None:
                term = term + total[:, cols]
            if step:
                term = term + sums[:, cols]
            if step + 1 == len(order):
                out[:, cols] = term.astype(out.dtype)
            else:
                sums[:, cols] = term
        if not resident and step + WEIGHT_SLOTS < len(order):
            fetch(step + WEIGHT_SLOTS).start()
        if step == max(0, len(order) - 1 - WEIGHT_SLOTS):
            for at in range(loads):
                load(at).start()
    for at in range(loads):
        load(at).wait()


def accumulate(total, pieces, owners, weights, out_type, loads, limit, name):
    counts = tuple(0 if piece.ndim == 2 else piece.shape[0] for piece in pieces)
    rows, depth = pieces[0].shape[-2:]
    columns = weights.shape[-1]
    width = next(w for w in (512, 256, 128, columns) if columns % w == 0)
    resident = weights.ndim == 3
    steps = sum(count or 1 for count in counts)
    operands = [jnp.stack(owners).astype(jnp.int32), *pieces]
    if total is not None:
        operands.append(total)
    out_shape = [jax.ShapeDtypeStruct((rows, columns), out_type)]
    if loads:
        out_shape.append(jax.ShapeDtypeStruct((loads, depth, columns), weights.dtype))
    slots = 1 if resident else WEIGHT_SLOTS
    return pl.pallas_call(
        functools.partial(accumulate_kernel, counts, total is not None, loads, width),
        out_shape=out_shape,
        in_specs=[SMEM_SPEC]
        + [VMEM_SPEC] * (len(operands) - 1)
        + [VMEM_SPEC if resident else HBM_SPEC],
        out_specs=[VMEM_SPEC] * len(out_shape),
        scratch_shapes=[
            pltpu.VMEM((rows, columns), F32),
            pltpu.VMEM((slots, 8 if resident else depth, columns), weights.dtype),
            pltpu.SemaphoreType.DMA((slots,)),
            pltpu.SemaphoreType.DMA((max(1, loads),)),
        ],
        compiler_params=pltpu.CompilerParams(vmem_limit_bytes=limit),
        cost_estimate=pl.CostEstimate(
            flops=2 * steps * rows * depth * columns,
            bytes_accessed=(steps + loads) * depth * columns * 2 + rows * columns * 8,
            transcendentals=0,
        ),
        name=name,
    )(*operands, weights)


def partials_kernel(grads, weights, out, held, sems):
    low, high = out.shape[:2]
    order = [(l, h) for l in range(low) for h in range(high)]
    depth = held.shape[1]

    def fetch(step):
        l, h = order[step]
        slot = step % WEIGHT_SLOTS
        rows = weights.at[pl.ds((h * low + l) * depth, depth), :]
        return pltpu.make_async_copy(rows, held.at[slot], sems.at[slot])

    for step in range(min(WEIGHT_SLOTS, len(order))):
        fetch(step).start()
    for step, (l, h) in enumerate(order):
        fetch(step).wait()
        term = lax.dot_general(
            grads[...],
            held[step % WEIGHT_SLOTS],
            (((1,), (1,)), ((), ())),
            preferred_element_type=F32,
        )
        out[l, h] = term.astype(out.dtype)
        if step + WEIGHT_SLOTS < len(order):
            fetch(step + WEIGHT_SLOTS).start()


def partials(grads, weights, high, low):
    rows, features = grads.shape
    depth = weights.shape[0] // (high * low)
    return pl.pallas_call(
        partials_kernel,
        out_shape=jax.ShapeDtypeStruct((low, high, rows, depth), BF16),
        in_specs=[VMEM_SPEC, HBM_SPEC],
        out_specs=VMEM_SPEC,
        scratch_shapes=[
            pltpu.VMEM((WEIGHT_SLOTS, depth, features), weights.dtype),
            pltpu.SemaphoreType.DMA((WEIGHT_SLOTS,)),
        ],
        compiler_params=pltpu.CompilerParams(vmem_limit_bytes=VMEM_LIMIT),
        cost_estimate=pl.CostEstimate(
            flops=2 * rows * features * weights.shape[0],
            bytes_accessed=2 * weights.shape[0] * (features + rows),
            transcendentals=0,
        ),
        name="grad_partials",
    )(grads, weights)


def halves(value):
    top = value.astype(BF16)
    return top, (value - top.astype(F32)).astype(BF16)


def band_kernel(taps, table):
    rows, span = table.shape[1:]
    for g in range(table.shape[0]):
        spreadout = jnp.broadcast_to(taps[g : g + 1, :], (rows, span))
        band = pltpu.roll(spreadout, 0, 1, stride=1, stride_axis=0)
        table[g] = band.astype(table.dtype)


def band_table(mr_filter):
    groups, taps = mr_filter.shape
    first = jnp.concatenate(
        [jnp.zeros((groups, 1), F32), mr_filter[:, ::-1], jnp.zeros((groups, taps - 1), F32)], 1
    )
    shape = jax.ShapeDtypeStruct((groups, taps, 2 * taps), BF16)
    return pl.pallas_call(
        band_kernel,
        out_shape=shape,
        in_specs=[VMEM_SPEC],
        out_specs=VMEM_SPEC,
        compiler_params=pltpu.CompilerParams(vmem_limit_bytes=VMEM_LIMIT),
        name="band_table",
    )(first)


def mixing_kernel(groups, earlier, projected, order, filters, bands, skip, gated, query, mixed):
    rows = projected.shape[0]
    channels = skip.shape[1]
    taps = bands.shape[1]
    span = 2 * taps
    extended = jnp.concatenate([earlier[...].astype(F32), projected[...].astype(F32)], 0).astype(BF16)
    lines = jnp.dot(extended, order[...], preferred_element_type=F32)
    short = (
        filters[0:1, :] * lines
        + filters[1:2, :] * pltpu.roll(lines, 1, 0)
        + filters[2:3, :] * pltpu.roll(lines, 2, 0)
    )
    own_query = short[rows:, :channels]
    both = short[:, channels : 2 * channels] * short[:, 2 * channels :]
    query[...] = own_query
    mixed[...] = both
    both_top, both_rest = halves(both)
    pair = jnp.concatenate([both_top, both_rest], 1)
    lane_group = lax.broadcasted_iota(jnp.int32, (taps, channels), 1) // (channels // groups)
    spare = rows - taps
    first = rows - taps
    body = jnp.zeros((taps, channels), F32)
    tail = jnp.zeros((spare, channels), F32)
    for g in range(groups):
        here = jnp.dot(bands[g], pair[first : first + span], preferred_element_type=F32)
        here = here[:, :channels] + here[:, channels:]
        body = jnp.where(lane_group == g, here, body)
        last = bands[g, taps - spare :]
        after = jnp.dot(last, pair[2 * first :], preferred_element_type=F32)
        after = after[:, :channels] + after[:, channels:]
        tail = jnp.where(lane_group[:spare] == g, after, tail)
    longconv = jnp.concatenate([body, tail], 0)
    gated[...] = (own_query * (longconv + skip[...] * both[rows:])).astype(gated.dtype)


def mixing(earlier, projected, order, filters, bands, skip, groups):
    rows, columns = projected.shape
    channels = columns // 3
    block = order.shape[0] // 3
    steps = channels // block
    per_step = groups // steps
    taps = bands.shape[1]
    ext = 2 * rows
    table = pl.BlockSpec((per_step, taps, 2 * taps), lambda i: (i, 0, 0))
    return pl.pallas_call(
        functools.partial(mixing_kernel, per_step),
        grid=(steps,),
        out_shape=[
            jax.ShapeDtypeStruct((rows, channels), BF16),
            jax.ShapeDtypeStruct((rows, channels), F32),
            jax.ShapeDtypeStruct((ext, channels), F32),
        ],
        in_specs=[
            pl.BlockSpec((rows, 3 * block), lambda i: (0, i)),
            pl.BlockSpec((rows, 3 * block), lambda i: (0, i)),
            pl.BlockSpec((3 * block, 3 * block), lambda i: (0, 0)),
            pl.BlockSpec((3, 3 * block), lambda i: (0, i)),
            table,
            pl.BlockSpec((1, block), lambda i: (0, i)),
        ],
        out_specs=[
            pl.BlockSpec((rows, block), lambda i: (0, i)),
            pl.BlockSpec((rows, block), lambda i: (0, i)),
            pl.BlockSpec((ext, block), lambda i: (0, i)),
        ],
        compiler_params=pltpu.CompilerParams(vmem_limit_bytes=VMEM_LIMIT),
        cost_estimate=pl.CostEstimate(
            flops=2 * 2 * groups * rows * 2 * taps * 2 * block,
            bytes_accessed=4 * ext * channels + 6 * ext * channels + 4 * groups * taps * taps,
            transcendentals=0,
        ),
        name="mixing",
    )(earlier, projected, order, filters, bands, skip)


def tap_grad_kernel(groups, grads, query, mixed, taps_out, skip_out):
    total = grads[0].astype(F32)
    for at in range(1, grads.shape[0]):
        total = total + grads[at].astype(F32)
    weighted = total * query[...]
    rows, channels = weighted.shape
    taps = taps_out.shape[1]
    span = 2 * taps
    first = rows - taps
    spare = rows - taps
    both = mixed[...]
    skip_out[...] = jnp.sum(weighted * both[rows:], axis=0, keepdims=True)
    both_top = both.astype(BF16)
    flip = jnp.where(
        lax.broadcasted_iota(jnp.int32, (span, span), 0)
        + lax.broadcasted_iota(jnp.int32, (span, span), 1)
        == span - 1,
        1.0,
        0.0,
    ).astype(BF16)

    def backwards(start):
        end = jnp.dot(flip, both_top[start : start + span], preferred_element_type=F32)
        return jnp.concatenate([end.astype(BF16)] * 2, 1)

    near, far = backwards(first), backwards(2 * first)
    parts = jnp.concatenate(halves(weighted), 1)
    lane_group = (lax.broadcasted_iota(jnp.int32, (1, 2 * channels), 1) % channels) // (
        channels // groups
    )
    contract = (((1,), (1,)), ((), ()))
    for g in range(groups):
        sides = parts * jnp.where(lane_group == g, 1.0, 0.0).astype(BF16)
        body = lax.dot_general(sides[:taps], near, contract, preferred_element_type=F32)
        tail = lax.dot_general(sides[taps:], far, contract, preferred_element_type=F32)
        body = jnp.concatenate([body[: taps - spare], body[taps - spare :] + tail], 0)
        skewed = pltpu.roll(body, 0, 1, stride=1, stride_axis=0)
        line = jnp.sum(skewed, axis=0, keepdims=True)
        taps_out[g : g + 1, :] = pltpu.roll(line, span - (taps - 1), 1)[:, :taps]


def tap_grad(grads, query, mixed, groups, taps):
    rows, channels = query.shape
    ext = mixed.shape[0]
    block = 128 if channels % 128 == 0 else channels
    steps = channels // block
    per_step = groups // steps
    span = 2 * taps
    one = pl.BlockSpec((rows, block), lambda i: (0, i))
    return pl.pallas_call(
        functools.partial(tap_grad_kernel, per_step),
        grid=(steps,),
        out_shape=[
            jax.ShapeDtypeStruct((groups, taps), F32),
            jax.ShapeDtypeStruct((1, channels), F32),
        ],
        in_specs=[
            pl.BlockSpec((grads.shape[0], rows, block), lambda i: (0, 0, i)),
            one,
            pl.BlockSpec((ext, block), lambda i: (0, i)),
        ],
        out_specs=[
            pl.BlockSpec((per_step, taps), lambda i: (i, 0)),
            pl.BlockSpec((1, block), lambda i: (0, i)),
        ],
        compiler_params=pltpu.CompilerParams(vmem_limit_bytes=VMEM_LIMIT),
        cost_estimate=pl.CostEstimate(
            flops=2 * groups * rows * span * 2 * block,
            bytes_accessed=4 * ext * channels + 6 * rows * channels,
            transcendentals=0,
        ),
        name="tap_grad",
    )(grads, query, mixed)


def branch_order(block, width):
    to = jnp.arange(3 * block)
    branch, channel = to // block, to % block
    source = 3 * width * (channel // width) + width * branch + channel % width
    return (jnp.arange(3 * block)[:, None] == source[None, :]).astype(BF16)


def local(tokens, w_in, short_filter, mr_filter, skip, w_out, grad_out):
    high, low = split_axis(lax.axis_size("col"))
    row_size = lax.axis_size("row")
    channels = tokens.shape[1]
    groups, taps = mr_filter.shape
    width = channels // groups
    block = 128 if channels % 128 == 0 else channels

    def contract(stages, weights, out_type, name):
        total, rows = None, weights
        for at, (pieces, owners) in enumerate(stages):
            left = len(stages) - 1 - at
            loads = len(stages[-1][1]) if left == 1 else 0
            total, *ahead = accumulate(
                total,
                pieces,
                owners + (stages[-1][1] if loads else []),
                rows,
                F32 if left else out_type,
                loads,
                VMEM_LIMIT if weights.size < 2**23 else 40 * 2**20,
                f"{name}_{at}",
            )
            rows = ahead[0] if loads else rows
        return total

    order = branch_order(block, width)
    filters = short_filter.reshape(3, channels // block, block // width, 3, width)
    filters = filters.transpose(0, 1, 3, 2, 4).reshape(3, 3 * channels)
    bands = band_table(mr_filter)
    grad_out, order, filters, bands = lax.optimization_barrier((grad_out, order, filters, bands))

    stages = spread(tokens, high, low)
    parts = partials(grad_out, w_out, high, low)
    parts, stages[-1][0][-1] = lax.optimization_barrier((parts, stages[-1][0][-1]))
    planes = [[h * low + l for l in range(low)] for h in range(high)]
    lines = [[h * low + l for h in range(high)] for l in range(low)]
    parts = lax.all_to_all(parts, "col", 0, 0, axis_index_groups=planes, tiled=True)
    parts = jnp.sum(parts.astype(F32), axis=0).astype(BF16)

    projected = contract(stages, w_in, BF16, "project")
    earlier = lax.ppermute(projected, "row", [(r, r + 1) for r in range(row_size - 1)])

    gated, query, mixed = mixing(earlier, projected, order, filters, bands, skip[None], groups)
    stages = spread(gated, high, low)
    parts, stages[1][0][0] = lax.optimization_barrier((parts, stages[1][0][0]))
    grads = lax.all_to_all(parts, "col", 0, 0, axis_index_groups=lines, tiled=True)
    block_out = contract(stages, w_out, BF16, "output")

    tap_part, skip_part = tap_grad(grads, query, mixed, groups, taps)
    if row_size == 2:
        flat = jnp.concatenate([tap_part.reshape(-1), skip_part.reshape(-1)])
        flat = flat + lax.ppermute(flat, "row", [(0, 1), (1, 0)])
        filter_grad = flat[: groups * taps].reshape(groups, taps)
        skip_grad = flat[groups * taps :]
    else:
        filter_grad, skip_grad = lax.psum((tap_part, skip_part.reshape(-1)), "row")
    return (block_out, filter_grad, skip_grad)


def solution(mesh):
    in_specs = (
        P("row", "col"),
        P(None, "col"),
        P(None, "col"),
        P("col", None),
        P("col"),
        P(None, "col"),
        P("row", "col"),
    )
    out_specs = (P("row", "col"), P("col", None), P("col"))
    return jax.shard_map(local, mesh=mesh, in_specs=in_specs, out_specs=out_specs, check_vma=False)
```

```python
import functools

import jax
import jax.numpy as jnp
from jax import lax
from jax.experimental import pallas as pl
from jax.experimental.pallas import tpu as pltpu
from jax.sharding import PartitionSpec as P

F32 = jnp.float32
BF16 = jnp.bfloat16
VMEM_SPEC = pl.BlockSpec(memory_space=pltpu.VMEM)
SMEM_SPEC = pl.BlockSpec(memory_space=pltpu.SMEM)
HBM_SPEC = pl.BlockSpec(memory_space=pltpu.HBM)
WEIGHT_SLOTS = 4
VMEM_LIMIT = 47 * 2**20
SMALL_LIMIT = 16 * 2**20


def split_axis(size):
    low = 1
    while low * low < size and size % (low * 2) == 0:
        low *= 2
    return size // low, low


def low_masks(low, parity):
    bits = [1 << i for i in range(low.bit_length() - 1)]
    return bits[::-1] if parity else bits


def swap_low(block, high, low, step):
    rows = lax.axis_size("row")
    size = high * low
    route = []
    for r in range(rows):
        mask = low_masks(low, r % 2)[step]
        route += [(r * size + c, r * size + (c ^ mask)) for c in range(size)]
    return lax.ppermute(block, ("row", "col"), route)


def shift_high(block, high, low, k):
    route = [(h * low + l, ((h + k) % high) * low + l) for h in range(high) for l in range(low)]
    return lax.ppermute(block, "col", route)


def flipped_low(low):
    parity = lax.axis_index("row") % 2
    forward, backward = low_masks(low, 0), low_masks(low, 1)
    flips = [0]
    for one, other in zip(forward, backward):
        mask = jnp.where(parity == 0, one, other)
        flips += [flip + mask for flip in flips]
    return flips


def after(values, *others):
    return lax.optimization_barrier((values, others))[0]


class Gather:
    def __init__(self, block, high, low, line_first):
        self.high, self.low, self.block = high, low, block
        self.bits = low.bit_length() - 1
        shifts = [k for k in range(1, high) if 2 * k != high]
        shifts += [k for k in (high // 2,) if 2 * k == high]
        self.shifts = shifts
        self.line = [shift_high(block, high, low, k) for k in shifts]
        self.near = self.plane([after(block, self.line[0]) if line_first else block], self.bits)[1:]

    def plane(self, items, steps):
        for step in range(steps):
            items = items + [swap_low(each, self.high, self.low, step) for each in items]
        return items

    def pass_on(self, *others):
        self.line = after(self.line, self.near[:2], others)
        items = self.plane([jnp.stack(self.line)], self.bits - 1)
        self.half = len(items)
        self.far = items + [swap_low(items[0], self.high, self.low, self.bits - 1)]

    def finish(self, weights, out_type, name):
        high, low = self.high, self.low
        me = lax.axis_index("col")
        h, l = me // low, me % low
        flips = flipped_low(low)
        from_high = [(h - k + high) % high for k in self.shifts]
        limit = VMEM_LIMIT if weights.size < 2**23 else 40 * 2**20

        owners = [h * low + (l ^ flip) for flip in flips]
        owners, late_owners = owners[:3], owners[3:]
        owners += [f * low + l for f in from_high]
        pieces = [self.block, *self.near[:2], *self.line]
        total, = accumulate(None, pieces, owners, weights, F32, 0, limit, name + "_0")
        hop = after(self.far[1 : self.half], total)
        last = [swap_low(each, high, low, self.bits - 1) for each in hop]
        owners = late_owners + [f * low + (l ^ flip) for flip in flips[1:] for f in from_high]
        final = len(last) * len(self.line)
        pieces = [*self.near[2:], *self.far[1:]]
        total, ahead = accumulate(total, pieces, owners, weights, F32, final, limit, name + "_1")
        self.total = total
        owners = owners[len(owners) - final :]
        return accumulate(total, last, owners, ahead, out_type, 0, limit, name + "_2")[0]


def accumulate_kernel(counts, has_total, loads, width, owners, *refs):
    refs = list(refs)
    pieces = [refs.pop(0) for _ in counts]
    total = refs.pop(0) if has_total else None
    weights, out = refs[:2]
    refs = refs[2:]
    ahead = refs.pop(0) if loads else None
    sums, held, sems, ahead_sems = refs
    order = [(p, i) for p, count in enumerate(counts) for i in range(count or 1)]
    resident = len(weights.shape) == 3
    depth = weights.shape[1] if resident else held.shape[1]

    def rows_of(step):
        return weights.at[pl.ds(pl.multiple_of(owners[step] * depth, depth), depth), :]

    def fetch(step):
        slot = step % WEIGHT_SLOTS
        return pltpu.make_async_copy(rows_of(step), held.at[slot], sems.at[slot])

    def load(at):
        return pltpu.make_async_copy(rows_of(len(order) + at), ahead.at[at], ahead_sems.at[at])

    if not resident:
        for step in range(min(WEIGHT_SLOTS, len(order))):
            fetch(step).start()
    for step, (p, i) in enumerate(order):
        if not resident:
            fetch(step).wait()
        slot = step % WEIGHT_SLOTS
        rows = pieces[p][i] if counts[p] else pieces[p][...]
        for at in range(0, out.shape[1], width):
            cols = slice(at, at + width)
            part = weights[step, :, cols] if resident else held[slot, :, cols]
            term = jnp.dot(rows, part, preferred_element_type=F32)
            if step == 0 and total is not None:
                term = term + total[:, cols]
            if step:
                term = term + sums[:, cols]
            if step + 1 == len(order):
                out[:, cols] = term.astype(out.dtype)
            else:
                sums[:, cols] = term
        if not resident and step + WEIGHT_SLOTS < len(order):
            fetch(step + WEIGHT_SLOTS).start()
        if step == max(0, len(order) - 1 - WEIGHT_SLOTS):
            for at in range(loads):
                load(at).start()
    for at in range(loads):
        load(at).wait()


def accumulate(total, pieces, owners, weights, out_type, loads, limit, name):
    counts = tuple(0 if piece.ndim == 2 else piece.shape[0] for piece in pieces)
    rows, depth = pieces[0].shape[-2:]
    columns = weights.shape[-1]
    width = next(w for w in (512, 256, 128, columns) if columns % w == 0)
    resident = weights.ndim == 3
    steps = sum(count or 1 for count in counts)
    operands = [jnp.stack(owners).astype(jnp.int32), *pieces]
    if total is not None:
        operands.append(total)
    out_shape = [jax.ShapeDtypeStruct((rows, columns), out_type)]
    if loads:
        out_shape.append(jax.ShapeDtypeStruct((loads, depth, columns), weights.dtype))
    slots = 1 if resident else WEIGHT_SLOTS
    return pl.pallas_call(
        functools.partial(accumulate_kernel, counts, total is not None, loads, width),
        out_shape=out_shape,
        in_specs=[SMEM_SPEC]
        + [VMEM_SPEC] * (len(operands) - 1)
        + [VMEM_SPEC if resident else HBM_SPEC],
        out_specs=[VMEM_SPEC] * len(out_shape),
        scratch_shapes=[
            pltpu.VMEM((rows, columns), F32),
            pltpu.VMEM((slots, 8 if resident else depth, columns), weights.dtype),
            pltpu.SemaphoreType.DMA((slots,)),
            pltpu.SemaphoreType.DMA((max(1, loads),)),
        ],
        compiler_params=pltpu.CompilerParams(vmem_limit_bytes=limit),
        cost_estimate=pl.CostEstimate(
            flops=2 * steps * rows * depth * columns,
            bytes_accessed=(steps + loads) * depth * columns * 2 + rows * columns * 8,
            transcendentals=0,
        ),
        name=name,
    )(*operands, weights)


def partials_kernel(owners, grads, weights, *refs):
    outs, (held, sems) = refs[:-2], refs[-2:]
    order = [(o, i) for o, out in enumerate(outs) for i in range(out.shape[0])]
    depth = held.shape[1]

    def fetch(step):
        start = pl.multiple_of(owners[step] * depth, depth)
        slot = step % WEIGHT_SLOTS
        return pltpu.make_async_copy(
            weights.at[pl.ds(start, depth), :], held.at[slot], sems.at[slot]
        )

    for step in range(min(WEIGHT_SLOTS, len(order))):
        fetch(step).start()
    for step, (o, i) in enumerate(order):
        fetch(step).wait()
        term = lax.dot_general(
            grads[...],
            held[step % WEIGHT_SLOTS],
            (((1,), (1,)), ((), ())),
            preferred_element_type=F32,
        )
        outs[o][i] = term.astype(outs[o].dtype)
        if step + WEIGHT_SLOTS < len(order):
            fetch(step + WEIGHT_SLOTS).start()


def partials(grads, weights, high, low):
    me = lax.axis_index("col")
    h, l = me // low, me % low
    owners = [((h + j) % high) * low + (l ^ flip) for flip in flipped_low(low) for j in range(high)]
    rows, features = grads.shape
    depth = weights.shape[0] // (high * low)
    counts = [high] + [high << step for step in range(low.bit_length() - 1)]
    return pl.pallas_call(
        partials_kernel,
        out_shape=[jax.ShapeDtypeStruct((count, rows, depth), BF16) for count in counts],
        in_specs=[SMEM_SPEC, VMEM_SPEC, HBM_SPEC],
        out_specs=[VMEM_SPEC] * len(counts),
        scratch_shapes=[
            pltpu.VMEM((WEIGHT_SLOTS, depth, features), weights.dtype),
            pltpu.SemaphoreType.DMA((WEIGHT_SLOTS,)),
        ],
        compiler_params=pltpu.CompilerParams(vmem_limit_bytes=VMEM_LIMIT),
        cost_estimate=pl.CostEstimate(
            flops=2 * rows * features * weights.shape[0],
            bytes_accessed=2 * weights.shape[0] * (features + rows),
            transcendentals=0,
        ),
        name="grad_partials",
    )(jnp.stack(owners).astype(jnp.int32), grads, weights)


def halves(value):
    top = value.astype(BF16)
    return top, (value - top.astype(F32)).astype(BF16)


def band_kernel(taps, table):
    rows, span = table.shape[1:]
    for g in range(table.shape[0]):
        spreadout = jnp.broadcast_to(taps[g : g + 1, :], (rows, span))
        band = pltpu.roll(spreadout, 0, 1, stride=1, stride_axis=0)
        table[g] = band.astype(table.dtype)


def band_table(mr_filter):
    groups, taps = mr_filter.shape
    first = jnp.concatenate(
        [jnp.zeros((groups, 1), F32), mr_filter[:, ::-1], jnp.zeros((groups, taps - 1), F32)], 1
    )
    shape = jax.ShapeDtypeStruct((groups, taps, 2 * taps), BF16)
    return pl.pallas_call(
        band_kernel,
        out_shape=shape,
        in_specs=[VMEM_SPEC],
        out_specs=VMEM_SPEC,
        compiler_params=pltpu.CompilerParams(vmem_limit_bytes=SMALL_LIMIT),
        name="band_table",
    )(first)


def mixing_kernel(groups, earlier, projected, order, filters, bands, skip, gated, query, mixed):
    rows = projected.shape[0]
    channels = skip.shape[1]
    taps = bands.shape[1]
    span = 2 * taps
    extended = jnp.concatenate([earlier[...].astype(F32), projected[...].astype(F32)], 0).astype(BF16)
    lines = jnp.dot(extended, order[...], preferred_element_type=F32)
    short = (
        filters[0:1, :] * lines
        + filters[1:2, :] * pltpu.roll(lines, 1, 0)
        + filters[2:3, :] * pltpu.roll(lines, 2, 0)
    )
    own_query = short[rows:, :channels]
    both = short[:, channels : 2 * channels] * short[:, 2 * channels :]
    query[...] = own_query
    mixed[...] = both
    both_top, both_rest = halves(both)
    pair = jnp.concatenate([both_top, both_rest], 1)
    lane_group = lax.broadcasted_iota(jnp.int32, (taps, channels), 1) // (channels // groups)
    spare = rows - taps
    first = rows - taps
    body = jnp.zeros((taps, channels), F32)
    tail = jnp.zeros((spare, channels), F32)
    for g in range(groups):
        here = jnp.dot(bands[g], pair[first : first + span], preferred_element_type=F32)
        here = here[:, :channels] + here[:, channels:]
        body = jnp.where(lane_group == g, here, body)
        last = bands[g, taps - spare :]
        after = jnp.dot(last, pair[2 * first :], preferred_element_type=F32)
        after = after[:, :channels] + after[:, channels:]
        tail = jnp.where(lane_group[:spare] == g, after, tail)
    longconv = jnp.concatenate([body, tail], 0)
    gated[...] = (own_query * (longconv + skip[...] * both[rows:])).astype(gated.dtype)


def mixing(earlier, projected, order, filters, bands, skip, groups):
    rows, columns = projected.shape
    channels = columns // 3
    block = order.shape[0] // 3
    steps = channels // block
    per_step = groups // steps
    taps = bands.shape[1]
    ext = 2 * rows
    table = pl.BlockSpec((per_step, taps, 2 * taps), lambda i: (i, 0, 0))
    return pl.pallas_call(
        functools.partial(mixing_kernel, per_step),
        grid=(steps,),
        out_shape=[
            jax.ShapeDtypeStruct((rows, channels), BF16),
            jax.ShapeDtypeStruct((rows, channels), F32),
            jax.ShapeDtypeStruct((ext, channels), F32),
        ],
        in_specs=[
            pl.BlockSpec((rows, 3 * block), lambda i: (0, i)),
            pl.BlockSpec((rows, 3 * block), lambda i: (0, i)),
            pl.BlockSpec((3 * block, 3 * block), lambda i: (0, 0)),
            pl.BlockSpec((3, 3 * block), lambda i: (0, i)),
            table,
            pl.BlockSpec((1, block), lambda i: (0, i)),
        ],
        out_specs=[
            pl.BlockSpec((rows, block), lambda i: (0, i)),
            pl.BlockSpec((rows, block), lambda i: (0, i)),
            pl.BlockSpec((ext, block), lambda i: (0, i)),
        ],
        compiler_params=pltpu.CompilerParams(vmem_limit_bytes=SMALL_LIMIT),
        cost_estimate=pl.CostEstimate(
            flops=2 * 2 * groups * rows * 2 * taps * 2 * block,
            bytes_accessed=4 * ext * channels + 6 * ext * channels + 4 * groups * taps * taps,
            transcendentals=0,
        ),
        name="mixing",
    )(earlier, projected, order, filters, bands, skip)


def tap_grad_kernel(groups, pieces, *refs):
    grads, (query, mixed, taps_out, skip_out) = refs[:pieces], refs[pieces:]
    total = grads[0][...].astype(F32)
    for piece in grads[1:]:
        total = total + piece[...].astype(F32)
    weighted = total * query[...]
    rows, channels = weighted.shape
    taps = taps_out.shape[1]
    span = 2 * taps
    first = rows - taps
    spare = rows - taps
    both = mixed[...]
    skip_out[...] = jnp.sum(weighted * both[rows:], axis=0, keepdims=True)
    both_top = both.astype(BF16)
    flip = jnp.where(
        lax.broadcasted_iota(jnp.int32, (span, span), 0)
        + lax.broadcasted_iota(jnp.int32, (span, span), 1)
        == span - 1,
        1.0,
        0.0,
    ).astype(BF16)

    def backwards(start):
        end = jnp.dot(flip, both_top[start : start + span], preferred_element_type=F32)
        return jnp.concatenate([end.astype(BF16)] * 2, 1)

    near, far = backwards(first), backwards(2 * first)
    parts = jnp.concatenate(halves(weighted), 1)
    lane_group = (lax.broadcasted_iota(jnp.int32, (1, 2 * channels), 1) % channels) // (
        channels // groups
    )
    contract = (((1,), (1,)), ((), ()))
    for g in range(groups):
        sides = parts * jnp.where(lane_group == g, 1.0, 0.0).astype(BF16)
        body = lax.dot_general(sides[:taps], near, contract, preferred_element_type=F32)
        tail = lax.dot_general(sides[taps:], far, contract, preferred_element_type=F32)
        body = jnp.concatenate([body[: taps - spare], body[taps - spare :] + tail], 0)
        skewed = pltpu.roll(body, 0, 1, stride=1, stride_axis=0)
        line = jnp.sum(skewed, axis=0, keepdims=True)
        taps_out[g : g + 1, :] = pltpu.roll(line, span - (taps - 1), 1)[:, :taps]


def tap_grad(grads, query, mixed, groups, taps):
    rows, channels = query.shape
    ext = mixed.shape[0]
    block = 128 if channels % 128 == 0 else channels
    steps = channels // block
    per_step = groups // steps
    span = 2 * taps
    one = pl.BlockSpec((rows, block), lambda i: (0, i))
    return pl.pallas_call(
        functools.partial(tap_grad_kernel, per_step, len(grads)),
        grid=(steps,),
        out_shape=[
            jax.ShapeDtypeStruct((groups, taps), F32),
            jax.ShapeDtypeStruct((1, channels), F32),
        ],
        in_specs=[one] * (len(grads) + 1) + [pl.BlockSpec((ext, block), lambda i: (0, i))],
        out_specs=[
            pl.BlockSpec((per_step, taps), lambda i: (i, 0)),
            pl.BlockSpec((1, block), lambda i: (0, i)),
        ],
        compiler_params=pltpu.CompilerParams(vmem_limit_bytes=SMALL_LIMIT),
        cost_estimate=pl.CostEstimate(
            flops=2 * groups * rows * span * 2 * block,
            bytes_accessed=4 * ext * channels + 6 * rows * channels,
            transcendentals=0,
        ),
        name="tap_grad",
    )(*grads, query, mixed)


def branch_order(block, width):
    to = jnp.arange(3 * block)
    branch, channel = to // block, to % block
    source = 3 * width * (channel // width) + width * branch + channel % width
    return (jnp.arange(3 * block)[:, None] == source[None, :]).astype(BF16)


def local(tokens, w_in, short_filter, mr_filter, skip, w_out, grad_out):
    high, low = split_axis(lax.axis_size("col"))
    row_size = lax.axis_size("row")
    channels = tokens.shape[1]
    groups, taps = mr_filter.shape
    width = channels // groups
    block = 128 if channels % 128 == 0 else channels

    order = branch_order(block, width)
    filters = short_filter.reshape(3, channels // block, block // width, 3, width)
    filters = filters.transpose(0, 1, 3, 2, 4).reshape(3, 3 * channels)
    bands = band_table(mr_filter)
    grad_out, order, filters, bands = lax.optimization_barrier((grad_out, order, filters, bands))

    gather = Gather(tokens, high, low, False)
    parts = partials(grad_out, w_out, high, low)
    gather.pass_on(parts)
    projected = gather.finish(w_in, BF16, "project")
    earlier = lax.ppermute(projected, "row", [(r, r + 1) for r in range(row_size - 1)])
    gated, query, mixed = mixing(earlier, projected, order, filters, bands, skip[None], groups)
    parts = after(parts, gather.total)
    gather = Gather(gated, high, low, False)

    parts = list(parts)
    for step in reversed(range(low.bit_length() - 1)):
        moved = after(swap_low(parts.pop(), high, low, step), gather.near[:2])
        at = 0
        for i, part in enumerate(parts):
            count = part.shape[0]
            total = part.astype(F32) + moved[at : at + count].astype(F32)
            parts[i], at = total.astype(BF16), at + count
    gather.pass_on()
    sums = after([parts[0][j] for j in range(high)], gather.line)
    grads = [sums[0]] + [shift_high(sums[j], high, low, j) for j in range(1, high)]
    block_out = gather.finish(w_out, BF16, "output")
    grads = after(grads, gather.far[1])

    tap_part, skip_part = tap_grad(grads, query, mixed, groups, taps)
    if row_size == 2:
        flat = jnp.concatenate([tap_part.reshape(-1), skip_part.reshape(-1)])
        flat = flat + lax.ppermute(flat, "row", [(0, 1), (1, 0)])
        filter_grad = flat[: groups * taps].reshape(groups, taps)
        skip_grad = flat[groups * taps :]
    else:
        filter_grad, skip_grad = lax.psum((tap_part, skip_part.reshape(-1)), "row")
    return (block_out, filter_grad, skip_grad)


def solution(mesh):
    in_specs = (
        P("row", "col"),
        P(None, "col"),
        P(None, "col"),
        P("col", None),
        P("col"),
        P(None, "col"),
        P("row", "col"),
    )
    out_specs = (P("row", "col"), P("col", None), P("col"))
    return jax.shard_map(local, mesh=mesh, in_specs=in_specs, out_specs=out_specs, check_vma=False)
```

```python
import functools

import jax
import jax.numpy as jnp
import numpy as np
from jax import lax
from jax.experimental import pallas as pl
from jax.experimental.pallas import tpu as pltpu
from jax.sharding import PartitionSpec as P

F32 = jnp.float32
BF16 = jnp.bfloat16
VMEM_SPEC = pl.BlockSpec(memory_space=pltpu.VMEM)
SMEM_SPEC = pl.BlockSpec(memory_space=pltpu.SMEM)
HBM_SPEC = pl.BlockSpec(memory_space=pltpu.HBM)
WEIGHT_SLOTS = 4
VMEM_LIMIT = 47 * 2**20
SMALL_LIMIT = 16 * 2**20


def split_axis(size):
    low = 1
    while low * low < size and size % (low * 2) == 0:
        low *= 2
    return size // low, low


def low_masks(low, parity):
    bits = [1 << i for i in range(low.bit_length() - 1)]
    return bits[::-1] if parity else bits


def swap_low(block, high, low, step):
    rows = lax.axis_size("row")
    size = high * low
    route = []
    for r in range(rows):
        mask = low_masks(low, r % 2)[step]
        route += [(r * size + c, r * size + (c ^ mask)) for c in range(size)]
    return lax.ppermute(block, ("row", "col"), route)


def shift_high(block, high, low, k):
    route = [(h * low + l, ((h + k) % high) * low + l) for h in range(high) for l in range(low)]
    return lax.ppermute(block, "col", route)


def flipped_low(low):
    parity = lax.axis_index("row") % 2
    forward, backward = low_masks(low, 0), low_masks(low, 1)
    flips = [0]
    for one, other in zip(forward, backward):
        mask = jnp.where(parity == 0, one, other)
        flips += [flip + mask for flip in flips]
    return flips


def after(values, *others):
    return lax.optimization_barrier((values, others))[0]


class Gather:
    def __init__(self, block, high, low):
        self.high, self.low, self.block = high, low, block
        self.bits = low.bit_length() - 1
        shifts = [k for k in range(1, high) if 2 * k != high]
        shifts += [k for k in (high // 2,) if 2 * k == high]
        self.shifts = shifts
        self.line = [shift_high(block, high, low, k) for k in shifts]
        near = self.plane([block], self.bits - 1)
        late = after(near, near[1:])
        self.near = near[1:]
        self.late = [swap_low(each, high, low, self.bits - 1) for each in late]

    def plane(self, items, steps):
        for step in range(steps):
            items = items + [swap_low(each, self.high, self.low, step) for each in items]
        return items

    def pass_on(self, *others):
        self.line = after(self.line, self.near, others)
        self.far = self.plane([jnp.stack(self.line)], self.bits - 1)

    def finish(self, weights, out_type, name):
        high, low = self.high, self.low
        me = lax.axis_index("col")
        h, l = me // low, me % low
        flips = flipped_low(low)
        from_high = [(h - k + high) % high for k in self.shifts]
        limit = VMEM_LIMIT if weights.size < 2**23 else 38 * 2**20

        owners = [h * low + (l ^ flip) for flip in flips]
        own = 1 + len(self.near)
        owners, late_owners = owners[:own], owners[own:]
        owners += [f * low + l for f in from_high]
        pieces = [self.block, *self.near, *self.line]
        total, = accumulate(None, pieces, owners, weights, F32, 0, limit, name + "_0")
        hop = after(self.far, total)
        last = [swap_low(each, high, low, self.bits - 1) for each in hop]
        owners = late_owners + [f * low + (l ^ flip) for flip in flips[1:] for f in from_high]
        final = len(last) * len(self.line)
        pieces = [*self.late, *self.far[1:]]
        total, ahead = accumulate(total, pieces, owners, weights, F32, final, limit, name + "_1")
        self.total = total
        owners = owners[len(owners) - final :]
        return accumulate(total, last, owners, ahead, out_type, 0, limit, name + "_2")[0]


def accumulate_kernel(counts, has_total, loads, width, owners, *refs):
    refs = list(refs)
    pieces = [refs.pop(0) for _ in counts]
    total = refs.pop(0) if has_total else None
    weights, out = refs[:2]
    refs = refs[2:]
    ahead = refs.pop(0) if loads else None
    sums, held, sems, ahead_sems = refs
    order = [(p, i) for p, count in enumerate(counts) for i in range(count or 1)]
    resident = len(weights.shape) == 3
    depth = weights.shape[1] if resident else held.shape[1]

    def rows_of(step):
        return weights.at[pl.ds(pl.multiple_of(owners[step] * depth, depth), depth), :]

    def fetch(step):
        slot = step % WEIGHT_SLOTS
        return pltpu.make_async_copy(rows_of(step), held.at[slot], sems.at[slot])

    def load(at):
        return pltpu.make_async_copy(rows_of(len(order) + at), ahead.at[at], ahead_sems.at[at])

    if not resident:
        for step in range(min(WEIGHT_SLOTS, len(order))):
            fetch(step).start()
    for step, (p, i) in enumerate(order):
        if not resident:
            fetch(step).wait()
        slot = step % WEIGHT_SLOTS
        rows = pieces[p][i] if counts[p] else pieces[p][...]
        for at in range(0, out.shape[1], width):
            cols = slice(at, at + width)
            part = weights[step, :, cols] if resident else held[slot, :, cols]
            term = jnp.dot(rows, part, preferred_element_type=F32)
            if step == 0 and total is not None:
                term = term + total[:, cols]
            if step:
                term = term + sums[:, cols]
            if step + 1 == len(order):
                out[:, cols] = term.astype(out.dtype)
            else:
                sums[:, cols] = term
        if not resident and step + WEIGHT_SLOTS < len(order):
            fetch(step + WEIGHT_SLOTS).start()
        if step == max(0, len(order) - 1 - WEIGHT_SLOTS):
            for at in range(loads):
                load(at).start()
    for at in range(loads):
        load(at).wait()


def accumulate(total, pieces, owners, weights, out_type, loads, limit, name):
    counts = tuple(0 if piece.ndim == 2 else piece.shape[0] for piece in pieces)
    rows, depth = pieces[0].shape[-2:]
    columns = weights.shape[-1]
    width = next(w for w in (512, 256, 128, columns) if columns % w == 0)
    resident = weights.ndim == 3
    steps = sum(count or 1 for count in counts)
    operands = [jnp.stack(owners).astype(jnp.int32), *pieces]
    if total is not None:
        operands.append(total)
    out_shape = [jax.ShapeDtypeStruct((rows, columns), out_type)]
    if loads:
        out_shape.append(jax.ShapeDtypeStruct((loads, depth, columns), weights.dtype))
    slots = 1 if resident else WEIGHT_SLOTS
    return pl.pallas_call(
        functools.partial(accumulate_kernel, counts, total is not None, loads, width),
        out_shape=out_shape,
        in_specs=[SMEM_SPEC]
        + [VMEM_SPEC] * (len(operands) - 1)
        + [VMEM_SPEC if resident else HBM_SPEC],
        out_specs=[VMEM_SPEC] * len(out_shape),
        scratch_shapes=[
            pltpu.VMEM((rows, columns), F32),
            pltpu.VMEM((slots, 8 if resident else depth, columns), weights.dtype),
            pltpu.SemaphoreType.DMA((slots,)),
            pltpu.SemaphoreType.DMA((max(1, loads),)),
        ],
        compiler_params=pltpu.CompilerParams(vmem_limit_bytes=limit),
        cost_estimate=pl.CostEstimate(
            flops=2 * steps * rows * depth * columns,
            bytes_accessed=(steps + loads) * depth * columns * 2 + rows * columns * 8,
            transcendentals=0,
        ),
        name=name,
    )(*operands, weights)


def partials_kernel(owners, grads, weights, *refs):
    outs, (held, sems) = refs[:-2], refs[-2:]
    order = [(o, i) for o, out in enumerate(outs) for i in range(out.shape[0])]
    depth = held.shape[1]

    def fetch(step):
        start = pl.multiple_of(owners[step] * depth, depth)
        slot = step % WEIGHT_SLOTS
        return pltpu.make_async_copy(
            weights.at[pl.ds(start, depth), :], held.at[slot], sems.at[slot]
        )

    for step in range(min(WEIGHT_SLOTS, len(order))):
        fetch(step).start()
    for step, (o, i) in enumerate(order):
        fetch(step).wait()
        term = lax.dot_general(
            grads[...],
            held[step % WEIGHT_SLOTS],
            (((1,), (1,)), ((), ())),
            preferred_element_type=F32,
        )
        outs[o][i] = term.astype(outs[o].dtype)
        if step + WEIGHT_SLOTS < len(order):
            fetch(step + WEIGHT_SLOTS).start()


def partials(grads, weights, high, low):
    me = lax.axis_index("col")
    h, l = me // low, me % low
    owners = [((h + j) % high) * low + (l ^ flip) for flip in flipped_low(low) for j in range(high)]
    rows, features = grads.shape
    depth = weights.shape[0] // (high * low)
    counts = [high] + [high << step for step in range(low.bit_length() - 1)]
    return pl.pallas_call(
        partials_kernel,
        out_shape=[jax.ShapeDtypeStruct((count, rows, depth), BF16) for count in counts],
        in_specs=[SMEM_SPEC, VMEM_SPEC, HBM_SPEC],
        out_specs=[VMEM_SPEC] * len(counts),
        scratch_shapes=[
            pltpu.VMEM((WEIGHT_SLOTS, depth, features), weights.dtype),
            pltpu.SemaphoreType.DMA((WEIGHT_SLOTS,)),
        ],
        compiler_params=pltpu.CompilerParams(vmem_limit_bytes=VMEM_LIMIT),
        cost_estimate=pl.CostEstimate(
            flops=2 * rows * features * weights.shape[0],
            bytes_accessed=2 * weights.shape[0] * (features + rows),
            transcendentals=0,
        ),
        name="grad_partials",
    )(jnp.stack(owners).astype(jnp.int32), grads, weights)


def halves(value):
    top = value.astype(BF16)
    return top, (value - top.astype(F32)).astype(BF16)


def prepare_kernel(mr_filter, short_filter, order, table, filters):
    taps, span = table.shape[1:]
    ends = lax.broadcasted_iota(jnp.int32, (taps, span), 0) + lax.broadcasted_iota(
        jnp.int32, (taps, span), 1
    )
    flip = jnp.where(ends == taps, 1.0, 0.0).astype(BF16)
    first = jnp.dot(mr_filter[...].astype(BF16), flip, preferred_element_type=F32)
    for g in range(table.shape[0]):
        spreadout = jnp.broadcast_to(first[g : g + 1, :], (taps, span))
        table[g] = pltpu.roll(spreadout, 0, 1, stride=1, stride_axis=0).astype(table.dtype)
    size = order.shape[0]
    for at in range(0, filters.shape[1], size):
        left = short_filter[:, at : at + size]
        moved = jnp.zeros(left.shape, F32)
        for _ in range(3):
            part = left.astype(BF16)
            moved = moved + jnp.dot(part, order[...], preferred_element_type=F32)
            left = left - part.astype(F32)
        filters[:, at : at + size] = moved


def prepare(mr_filter, short_filter, order):
    groups, taps = mr_filter.shape
    return pl.pallas_call(
        prepare_kernel,
        out_shape=[
            jax.ShapeDtypeStruct((groups, taps, 2 * taps), BF16),
            jax.ShapeDtypeStruct(short_filter.shape, F32),
        ],
        in_specs=[VMEM_SPEC] * 3,
        out_specs=[VMEM_SPEC] * 2,
        compiler_params=pltpu.CompilerParams(vmem_limit_bytes=SMALL_LIMIT),
        name="prepare",
    )(mr_filter, short_filter, order)


def mixing_kernel(groups, earlier, projected, order, filters, bands, skip, gated, query, mixed):
    rows = projected.shape[0]
    channels = skip.shape[1]
    taps = bands.shape[1]
    span = 2 * taps
    extended = jnp.concatenate([earlier[...].astype(F32), projected[...].astype(F32)], 0).astype(BF16)
    lines = jnp.dot(extended, order[...], preferred_element_type=F32)
    short = (
        filters[0:1, :] * lines
        + filters[1:2, :] * pltpu.roll(lines, 1, 0)
        + filters[2:3, :] * pltpu.roll(lines, 2, 0)
    )
    own_query = short[rows:, :channels]
    both = short[:, channels : 2 * channels] * short[:, 2 * channels :]
    query[...] = own_query
    mixed[...] = both
    both_top, both_rest = halves(both)
    pair = jnp.concatenate([both_top, both_rest], 1)
    lane_group = lax.broadcasted_iota(jnp.int32, (taps, channels), 1) // (channels // groups)
    first = spare = rows - taps
    whole = bands[...].reshape(groups * taps, span)
    ends = bands[:, taps - spare :, :].reshape(groups * spare, span)
    bodies = jnp.dot(whole, pair[first : first + span], preferred_element_type=F32)
    tails = jnp.dot(ends, pair[2 * first :], preferred_element_type=F32)
    bodies = bodies[:, :channels] + bodies[:, channels:]
    tails = tails[:, :channels] + tails[:, channels:]
    body, tail = bodies[:taps], tails[:spare]
    for g in range(1, groups):
        body = jnp.where(lane_group == g, bodies[g * taps : (g + 1) * taps], body)
        tail = jnp.where(lane_group[:spare] == g, tails[g * spare : (g + 1) * spare], tail)
    longconv = jnp.concatenate([body, tail], 0)
    gated[...] = (own_query * (longconv + skip[...] * both[rows:])).astype(gated.dtype)


def mixing(earlier, projected, order, filters, bands, skip, groups):
    rows, columns = projected.shape
    channels = columns // 3
    block = order.shape[0] // 3
    steps = channels // block
    per_step = groups // steps
    taps = bands.shape[1]
    ext = 2 * rows
    table = pl.BlockSpec((per_step, taps, 2 * taps), lambda i: (i, 0, 0))
    return pl.pallas_call(
        functools.partial(mixing_kernel, per_step),
        grid=(steps,),
        out_shape=[
            jax.ShapeDtypeStruct((rows, channels), BF16),
            jax.ShapeDtypeStruct((rows, channels), F32),
            jax.ShapeDtypeStruct((ext, channels), F32),
        ],
        in_specs=[
            pl.BlockSpec((rows, 3 * block), lambda i: (0, i)),
            pl.BlockSpec((rows, 3 * block), lambda i: (0, i)),
            pl.BlockSpec((3 * block, 3 * block), lambda i: (0, 0)),
            pl.BlockSpec((3, 3 * block), lambda i: (0, i)),
            table,
            pl.BlockSpec((1, block), lambda i: (0, i)),
        ],
        out_specs=[
            pl.BlockSpec((rows, block), lambda i: (0, i)),
            pl.BlockSpec((rows, block), lambda i: (0, i)),
            pl.BlockSpec((ext, block), lambda i: (0, i)),
        ],
        compiler_params=pltpu.CompilerParams(vmem_limit_bytes=SMALL_LIMIT),
        cost_estimate=pl.CostEstimate(
            flops=2 * 2 * groups * rows * 2 * taps * 2 * block,
            bytes_accessed=4 * ext * channels + 6 * ext * channels + 4 * groups * taps * taps,
            transcendentals=0,
        ),
        name="mixing",
    )(earlier, projected, order, filters, bands, skip)


def tap_grad_kernel(groups, pieces, *refs):
    grads, (query, mixed, taps_out, skip_out) = refs[:pieces], refs[pieces:]
    total = grads[0][...].astype(F32)
    for piece in grads[1:]:
        total = total + piece[...].astype(F32)
    weighted = total * query[...]
    rows, channels = weighted.shape
    taps = taps_out.shape[1]
    span = 2 * taps
    first = rows - taps
    spare = rows - taps
    both = mixed[...]
    skip_out[...] = jnp.sum(weighted * both[rows:], axis=0, keepdims=True)
    both_top = both.astype(BF16)
    flip = jnp.where(
        lax.broadcasted_iota(jnp.int32, (span, span), 0)
        + lax.broadcasted_iota(jnp.int32, (span, span), 1)
        == span - 1,
        1.0,
        0.0,
    ).astype(BF16)

    def backwards(start):
        end = jnp.dot(flip, both_top[start : start + span], preferred_element_type=F32)
        return jnp.concatenate([end.astype(BF16)] * 2, 1)

    near, far = backwards(first), backwards(2 * first)
    parts = jnp.concatenate(halves(weighted), 1)
    lane_group = (lax.broadcasted_iota(jnp.int32, (1, 2 * channels), 1) % channels) // (
        channels // groups
    )
    contract = (((1,), (1,)), ((), ()))
    masks = [jnp.where(lane_group == g, 1.0, 0.0).astype(BF16) for g in range(groups)]
    sides = jnp.concatenate([parts[:taps] * mask for mask in masks], 0)
    ends = jnp.concatenate([parts[taps:].astype(F32) * mask.astype(F32) for mask in masks], 0)
    bodies = lax.dot_general(sides, near, contract, preferred_element_type=F32)
    tails = lax.dot_general(ends.astype(BF16), far, contract, preferred_element_type=F32)
    for g in range(groups):
        body = bodies[g * taps : (g + 1) * taps]
        tail = tails[g * spare : (g + 1) * spare]
        body = jnp.concatenate([body[: taps - spare], body[taps - spare :] + tail], 0)
        skewed = pltpu.roll(body, 0, 1, stride=1, stride_axis=0)
        line = jnp.sum(skewed, axis=0, keepdims=True)
        taps_out[g : g + 1, :] = pltpu.roll(line, span - (taps - 1), 1)[:, :taps]


def tap_grad(grads, query, mixed, groups, taps):
    rows, channels = query.shape
    ext = mixed.shape[0]
    block = 128 if channels % 128 == 0 else channels
    steps = channels // block
    per_step = groups // steps
    span = 2 * taps
    one = pl.BlockSpec((rows, block), lambda i: (0, i))
    return pl.pallas_call(
        functools.partial(tap_grad_kernel, per_step, len(grads)),
        grid=(steps,),
        out_shape=[
            jax.ShapeDtypeStruct((groups, taps), F32),
            jax.ShapeDtypeStruct((1, channels), F32),
        ],
        in_specs=[one] * (len(grads) + 1) + [pl.BlockSpec((ext, block), lambda i: (0, i))],
        out_specs=[
            pl.BlockSpec((per_step, taps), lambda i: (i, 0)),
            pl.BlockSpec((1, block), lambda i: (0, i)),
        ],
        compiler_params=pltpu.CompilerParams(vmem_limit_bytes=SMALL_LIMIT),
        cost_estimate=pl.CostEstimate(
            flops=2 * groups * rows * span * 2 * block,
            bytes_accessed=4 * ext * channels + 6 * rows * channels,
            transcendentals=0,
        ),
        name="tap_grad",
    )(*grads, query, mixed)


def branch_order(block, width):
    to = np.arange(3 * block)
    branch, channel = to // block, to % block
    source = 3 * width * (channel // width) + width * branch + channel % width
    return jnp.asarray(np.arange(3 * block)[:, None] == source[None, :], BF16)


def local(tokens, w_in, short_filter, mr_filter, skip, w_out, grad_out):
    high, low = split_axis(lax.axis_size("col"))
    row_size = lax.axis_size("row")
    channels = tokens.shape[1]
    groups, taps = mr_filter.shape
    width = channels // groups
    block = 128 if channels % 128 == 0 else channels

    order = branch_order(block, width)
    bands, filters = prepare(mr_filter, short_filter, order)
    grad_out, filters, bands = lax.optimization_barrier((grad_out, filters, bands))

    gather = Gather(tokens, high, low)
    parts = partials(grad_out, w_out, high, low)
    gather.pass_on(parts, gather.late)
    projected = gather.finish(w_in, BF16, "project")
    earlier = lax.ppermute(projected, "row", [(r, r + 1) for r in range(row_size - 1)])
    gated, query, mixed = mixing(earlier, projected, order, filters, bands, skip[None], groups)
    parts = after(parts, gather.total)
    gather = Gather(gated, high, low)

    parts = list(parts)
    for step in reversed(range(low.bit_length() - 1)):
        moved = after(swap_low(parts.pop(), high, low, step), gather.near)
        at = 0
        for i, part in enumerate(parts):
            count = part.shape[0]
            total = part.astype(F32) + moved[at : at + count].astype(F32)
            parts[i], at = total.astype(BF16), at + count
    gather.pass_on()
    sums = after([parts[0][j] for j in range(high)], gather.line)
    grads = [sums[0]] + [shift_high(sums[j], high, low, j) for j in range(1, high)]
    block_out = gather.finish(w_out, BF16, "output")
    grads = after(grads, gather.far[1])

    tap_part, skip_part = tap_grad(grads, query, mixed, groups, taps)
    if row_size == 2:
        flat = jnp.concatenate([tap_part.reshape(-1), skip_part.reshape(-1)])
        flat = flat + lax.ppermute(flat, "row", [(0, 1), (1, 0)])
        filter_grad = flat[: groups * taps].reshape(groups, taps)
        skip_grad = flat[groups * taps :]
    else:
        filter_grad, skip_grad = lax.psum((tap_part, skip_part.reshape(-1)), "row")
    return (block_out, filter_grad, skip_grad)


def solution(mesh):
    in_specs = (
        P("row", "col"),
        P(None, "col"),
        P(None, "col"),
        P("col", None),
        P("col"),
        P(None, "col"),
        P("row", "col"),
    )
    out_specs = (P("row", "col"), P("col", None), P("col"))
    return jax.shard_map(local, mesh=mesh, in_specs=in_specs, out_specs=out_specs, check_vma=False)
```

```python
import functools

import jax
import jax.numpy as jnp
import numpy as np
from jax import lax
from jax.experimental import pallas as pl
from jax.experimental.pallas import tpu as pltpu
from jax.sharding import PartitionSpec as P

F32 = jnp.float32
BF16 = jnp.bfloat16
VMEM_SPEC = pl.BlockSpec(memory_space=pltpu.VMEM)
SMEM_SPEC = pl.BlockSpec(memory_space=pltpu.SMEM)
HBM_SPEC = pl.BlockSpec(memory_space=pltpu.HBM)
WEIGHT_SLOTS = 4
VMEM_LIMIT = 47 * 2**20
SMALL_LIMIT = 16 * 2**20


def split_axis(size):
    low = 1
    while low * low < size and size % (low * 2) == 0:
        low *= 2
    return size // low, low


def low_masks(low, parity):
    bits = [1 << i for i in range(low.bit_length() - 1)]
    return bits[::-1] if parity else bits


def swap_low(block, high, low, step):
    rows = lax.axis_size("row")
    size = high * low
    route = []
    for r in range(rows):
        mask = low_masks(low, r % 2)[step]
        route += [(r * size + c, r * size + (c ^ mask)) for c in range(size)]
    return lax.ppermute(block, ("row", "col"), route)


def shift_high(block, high, low, k):
    route = [(h * low + l, ((h + k) % high) * low + l) for h in range(high) for l in range(low)]
    return lax.ppermute(block, "col", route)


def flipped_low(low):
    parity = lax.axis_index("row") % 2
    forward, backward = low_masks(low, 0), low_masks(low, 1)
    flips = [0]
    for one, other in zip(forward, backward):
        mask = jnp.where(parity == 0, one, other)
        flips += [flip + mask for flip in flips]
    return flips


def after(values, *others):
    return lax.optimization_barrier((values, others))[0]


class Gather:
    def __init__(self, block, high, low):
        self.high, self.low, self.block = high, low, block
        self.bits = low.bit_length() - 1
        shifts = [k for k in range(1, high) if 2 * k != high]
        shifts += [k for k in (high // 2,) if 2 * k == high]
        self.shifts = shifts
        self.line = [shift_high(block, high, low, k) for k in shifts]
        near = self.plane([block], self.bits - 1)
        late = after(near, near[1:])
        self.near = near[1:]
        self.late = [swap_low(each, high, low, self.bits - 1) for each in late]

    def plane(self, items, steps):
        for step in range(steps):
            items = items + [swap_low(each, self.high, self.low, step) for each in items]
        return items

    def pass_on(self, *others):
        self.line = after(self.line, self.near, others)
        self.far = self.plane([jnp.stack(self.line)], self.bits - 1)

    def finish(self, weights, out_type, name, before_hop=()):
        high, low = self.high, self.low
        me = lax.axis_index("col")
        h, l = me // low, me % low
        flips = flipped_low(low)
        from_high = [(h - k + high) % high for k in self.shifts]
        small = weights.size < 2**23
        limit = VMEM_LIMIT if small else 40 * 2**20

        owners = [h * low + (l ^ flip) for flip in flips]
        own = 1 + len(self.near)
        owners, late_owners = owners[:own], owners[own:]
        owners += [f * low + l for f in from_high]
        pieces = [self.block, *self.near, *self.line]
        total, hop = None, self.far
        if small:
            hop = after(hop, before_hop)
        else:
            total, = accumulate(None, pieces, owners, weights, None, F32, 0, limit, name + "_0")
            hop = after(hop, before_hop, total)
            pieces, owners = [], []
        last = [swap_low(each, high, low, self.bits - 1) for each in hop]
        owners += late_owners + [f * low + (l ^ flip) for flip in flips[1:] for f in from_high]
        final = len(last) * len(self.line)
        loads = final if small else final // 2
        pieces += [*self.late, *self.far[1:]]
        total, ahead = accumulate(
            total, pieces, owners, weights, None, F32, loads, limit, name + "_1"
        )
        self.total = total
        owners = owners[len(owners) - final :]
        return accumulate(total, last, owners, weights, ahead, out_type, 0, limit, name + "_2")[0]


def accumulate_kernel(counts, has_total, ready, loads, width, owners, *refs):
    refs = list(refs)
    pieces = [refs.pop(0) for _ in counts]
    total = refs.pop(0) if has_total else None
    here = refs.pop(0) if ready else None
    weights, out = refs[:2]
    refs = refs[2:]
    ahead = refs.pop(0) if loads else None
    sums, held, sems, ahead_sems = refs
    order = [(p, i) for p, count in enumerate(counts) for i in range(count or 1)]
    depth = held.shape[1]

    def rows_of(step):
        return weights.at[pl.ds(pl.multiple_of(owners[step] * depth, depth), depth), :]

    def fetch(step):
        slot = step % WEIGHT_SLOTS
        return pltpu.make_async_copy(rows_of(step), held.at[slot], sems.at[slot])

    def load(at):
        return pltpu.make_async_copy(rows_of(len(order) + at), ahead.at[at], ahead_sems.at[at])

    for step in range(ready, min(ready + WEIGHT_SLOTS, len(order))):
        fetch(step).start()
    for step, (p, i) in enumerate(order):
        if step >= ready:
            fetch(step).wait()
        slot = step % WEIGHT_SLOTS
        rows = pieces[p][i] if counts[p] else pieces[p][...]
        for at in range(0, out.shape[1], width):
            cols = slice(at, at + width)
            part = here[step, :, cols] if step < ready else held[slot, :, cols]
            term = jnp.dot(rows, part, preferred_element_type=F32)
            if step == 0 and total is not None:
                term = term + total[:, cols]
            if step:
                term = term + sums[:, cols]
            if step + 1 == len(order):
                out[:, cols] = term.astype(out.dtype)
            else:
                sums[:, cols] = term
        if step >= ready and step + WEIGHT_SLOTS < len(order):
            fetch(step + WEIGHT_SLOTS).start()
        if step == max(0, len(order) - 1 - WEIGHT_SLOTS):
            for at in range(loads):
                load(at).start()
    for at in range(loads):
        load(at).wait()


def accumulate(total, pieces, owners, weights, here, out_type, loads, limit, name):
    counts = tuple(0 if piece.ndim == 2 else piece.shape[0] for piece in pieces)
    rows, depth = pieces[0].shape[-2:]
    columns = weights.shape[-1]
    width = next(w for w in (512, 256, 128, columns) if columns % w == 0)
    steps = sum(count or 1 for count in counts)
    ready = 0 if here is None else here.shape[0]
    operands = [jnp.stack(owners).astype(jnp.int32), *pieces]
    operands += [extra for extra in (total, here) if extra is not None]
    out_shape = [jax.ShapeDtypeStruct((rows, columns), out_type)]
    if loads:
        out_shape.append(jax.ShapeDtypeStruct((loads, depth, columns), weights.dtype))
    return pl.pallas_call(
        functools.partial(accumulate_kernel, counts, total is not None, ready, loads, width),
        out_shape=out_shape,
        in_specs=[SMEM_SPEC] + [VMEM_SPEC] * (len(operands) - 1) + [HBM_SPEC],
        out_specs=[VMEM_SPEC] * len(out_shape),
        scratch_shapes=[
            pltpu.VMEM((rows, columns), F32),
            pltpu.VMEM((WEIGHT_SLOTS, depth, columns), weights.dtype),
            pltpu.SemaphoreType.DMA((WEIGHT_SLOTS,)),
            pltpu.SemaphoreType.DMA((max(1, loads),)),
        ],
        compiler_params=pltpu.CompilerParams(vmem_limit_bytes=limit),
        cost_estimate=pl.CostEstimate(
            flops=2 * steps * rows * depth * columns,
            bytes_accessed=(steps + loads) * depth * columns * 2 + rows * columns * 8,
            transcendentals=0,
        ),
        name=name,
    )(*operands, weights)


def partials_kernel(owners, grads, weights, *refs):
    outs, (held, sems) = refs[:-2], refs[-2:]
    order = [(o, i) for o, out in enumerate(outs) for i in range(out.shape[0])]
    depth = held.shape[1]

    def fetch(step):
        start = pl.multiple_of(owners[step] * depth, depth)
        slot = step % WEIGHT_SLOTS
        return pltpu.make_async_copy(
            weights.at[pl.ds(start, depth), :], held.at[slot], sems.at[slot]
        )

    for step in range(min(WEIGHT_SLOTS, len(order))):
        fetch(step).start()
    for step, (o, i) in enumerate(order):
        fetch(step).wait()
        term = lax.dot_general(
            grads[...],
            held[step % WEIGHT_SLOTS],
            (((1,), (1,)), ((), ())),
            preferred_element_type=F32,
        )
        outs[o][i] = term.astype(outs[o].dtype)
        if step + WEIGHT_SLOTS < len(order):
            fetch(step + WEIGHT_SLOTS).start()


def partials(grads, weights, high, low):
    l = lax.axis_index("col") % low
    owners = [j * low + (l ^ flip) for flip in flipped_low(low) for j in range(high)]
    rows, features = grads.shape
    depth = weights.shape[0] // (high * low)
    counts = [high] + [high << step for step in range(low.bit_length() - 1)]
    return pl.pallas_call(
        partials_kernel,
        out_shape=[jax.ShapeDtypeStruct((count, rows, depth), BF16) for count in counts],
        in_specs=[SMEM_SPEC, VMEM_SPEC, HBM_SPEC],
        out_specs=[VMEM_SPEC] * len(counts),
        scratch_shapes=[
            pltpu.VMEM((WEIGHT_SLOTS, depth, features), weights.dtype),
            pltpu.SemaphoreType.DMA((WEIGHT_SLOTS,)),
        ],
        compiler_params=pltpu.CompilerParams(vmem_limit_bytes=VMEM_LIMIT),
        cost_estimate=pl.CostEstimate(
            flops=2 * rows * features * weights.shape[0],
            bytes_accessed=2 * weights.shape[0] * (features + rows),
            transcendentals=0,
        ),
        name="grad_partials",
    )(jnp.stack(owners).astype(jnp.int32), grads, weights)


def halves(value):
    top = value.astype(BF16)
    return top, (value - top.astype(F32)).astype(BF16)


def prepare_kernel(mr_filter, short_filter, order, table, filters):
    taps, span = table.shape[1:]
    ends = lax.broadcasted_iota(jnp.int32, (taps, span), 0) + lax.broadcasted_iota(
        jnp.int32, (taps, span), 1
    )
    flip = jnp.where(ends == taps, 1.0, 0.0).astype(BF16)
    first = jnp.dot(mr_filter[...].astype(BF16), flip, preferred_element_type=F32)
    for g in range(table.shape[0]):
        spreadout = jnp.broadcast_to(first[g : g + 1, :], (taps, span))
        table[g] = pltpu.roll(spreadout, 0, 1, stride=1, stride_axis=0).astype(table.dtype)
    size = order.shape[0]
    for at in range(0, filters.shape[1], size):
        left = short_filter[:, at : at + size]
        moved = jnp.zeros(left.shape, F32)
        for _ in range(3):
            part = left.astype(BF16)
            moved = moved + jnp.dot(part, order[...], preferred_element_type=F32)
            left = left - part.astype(F32)
        filters[:, at : at + size] = moved


def prepare(mr_filter, short_filter, order):
    groups, taps = mr_filter.shape
    return pl.pallas_call(
        prepare_kernel,
        out_shape=[
            jax.ShapeDtypeStruct((groups, taps, 2 * taps), BF16),
            jax.ShapeDtypeStruct(short_filter.shape, F32),
        ],
        in_specs=[VMEM_SPEC] * 3,
        out_specs=[VMEM_SPEC] * 2,
        compiler_params=pltpu.CompilerParams(vmem_limit_bytes=SMALL_LIMIT),
        name="prepare",
    )(mr_filter, short_filter, order)


def mixing_kernel(groups, earlier, projected, order, filters, bands, skip, gated, query, mixed):
    rows = projected.shape[0]
    channels = skip.shape[1]
    taps = bands.shape[1]
    span = 2 * taps
    extended = jnp.concatenate([earlier[...].astype(F32), projected[...].astype(F32)], 0).astype(BF16)
    lines = jnp.dot(extended, order[...], preferred_element_type=F32)
    short = (
        filters[0:1, :] * lines
        + filters[1:2, :] * pltpu.roll(lines, 1, 0)
        + filters[2:3, :] * pltpu.roll(lines, 2, 0)
    )
    own_query = short[rows:, :channels]
    both = short[:, channels : 2 * channels] * short[:, 2 * channels :]
    query[...] = own_query
    mixed[...] = both
    both_top, both_rest = halves(both)
    pair = jnp.concatenate([both_top, both_rest], 1)
    lane_group = lax.broadcasted_iota(jnp.int32, (taps, channels), 1) // (channels // groups)
    first = spare = rows - taps
    whole = bands[...].reshape(groups * taps, span)
    ends = bands[:, taps - spare :, :].reshape(groups * spare, span)
    bodies = jnp.dot(whole, pair[first : first + span], preferred_element_type=F32)
    tails = jnp.dot(ends, pair[2 * first :], preferred_element_type=F32)
    bodies = bodies[:, :channels] + bodies[:, channels:]
    tails = tails[:, :channels] + tails[:, channels:]
    body, tail = bodies[:taps], tails[:spare]
    for g in range(1, groups):
        body = jnp.where(lane_group == g, bodies[g * taps : (g + 1) * taps], body)
        tail = jnp.where(lane_group[:spare] == g, tails[g * spare : (g + 1) * spare], tail)
    longconv = jnp.concatenate([body, tail], 0)
    gated[...] = (own_query * (longconv + skip[...] * both[rows:])).astype(gated.dtype)


def mixing(earlier, projected, order, filters, bands, skip, groups):
    rows, columns = projected.shape
    channels = columns // 3
    block = order.shape[0] // 3
    steps = channels // block
    per_step = groups // steps
    taps = bands.shape[1]
    ext = 2 * rows
    table = pl.BlockSpec((per_step, taps, 2 * taps), lambda i: (i, 0, 0))
    return pl.pallas_call(
        functools.partial(mixing_kernel, per_step),
        grid=(steps,),
        out_shape=[
            jax.ShapeDtypeStruct((rows, channels), BF16),
            jax.ShapeDtypeStruct((rows, channels), F32),
            jax.ShapeDtypeStruct((ext, channels), F32),
        ],
        in_specs=[
            pl.BlockSpec((rows, 3 * block), lambda i: (0, i)),
            pl.BlockSpec((rows, 3 * block), lambda i: (0, i)),
            pl.BlockSpec((3 * block, 3 * block), lambda i: (0, 0)),
            pl.BlockSpec((3, 3 * block), lambda i: (0, i)),
            table,
            pl.BlockSpec((1, block), lambda i: (0, i)),
        ],
        out_specs=[
            pl.BlockSpec((rows, block), lambda i: (0, i)),
            pl.BlockSpec((rows, block), lambda i: (0, i)),
            pl.BlockSpec((ext, block), lambda i: (0, i)),
        ],
        compiler_params=pltpu.CompilerParams(vmem_limit_bytes=SMALL_LIMIT),
        cost_estimate=pl.CostEstimate(
            flops=2 * 2 * groups * rows * 2 * taps * 2 * block,
            bytes_accessed=4 * ext * channels + 6 * ext * channels + 4 * groups * taps * taps,
            transcendentals=0,
        ),
        name="mixing",
    )(earlier, projected, order, filters, bands, skip)


def tap_grad_kernel(groups, grads, query, mixed, taps_out, skip_out):
    total = grads[0].astype(F32)
    for at in range(1, grads.shape[0]):
        total = total + grads[at].astype(F32)
    weighted = total * query[...]
    rows, channels = weighted.shape
    taps = taps_out.shape[1]
    span = 2 * taps
    first = rows - taps
    spare = rows - taps
    both = mixed[...]
    skip_out[...] = jnp.sum(weighted * both[rows:], axis=0, keepdims=True)
    both_top = both.astype(BF16)
    flip = jnp.where(
        lax.broadcasted_iota(jnp.int32, (span, span), 0)
        + lax.broadcasted_iota(jnp.int32, (span, span), 1)
        == span - 1,
        1.0,
        0.0,
    ).astype(BF16)

    def backwards(start):
        end = jnp.dot(flip, both_top[start : start + span], preferred_element_type=F32)
        return jnp.concatenate([end.astype(BF16)] * 2, 1)

    near, far = backwards(first), backwards(2 * first)
    parts = jnp.concatenate(halves(weighted), 1)
    lane_group = (lax.broadcasted_iota(jnp.int32, (1, 2 * channels), 1) % channels) // (
        channels // groups
    )
    contract = (((1,), (1,)), ((), ()))
    masks = [jnp.where(lane_group == g, 1.0, 0.0).astype(BF16) for g in range(groups)]
    sides = jnp.concatenate([parts[:taps] * mask for mask in masks], 0)
    ends = jnp.concatenate([parts[taps:].astype(F32) * mask.astype(F32) for mask in masks], 0)
    bodies = lax.dot_general(sides, near, contract, preferred_element_type=F32)
    tails = lax.dot_general(ends.astype(BF16), far, contract, preferred_element_type=F32)
    for g in range(groups):
        body = bodies[g * taps : (g + 1) * taps]
        tail = tails[g * spare : (g + 1) * spare]
        body = jnp.concatenate([body[: taps - spare], body[taps - spare :] + tail], 0)
        skewed = pltpu.roll(body, 0, 1, stride=1, stride_axis=0)
        line = jnp.sum(skewed, axis=0, keepdims=True)
        taps_out[g : g + 1, :] = pltpu.roll(line, span - (taps - 1), 1)[:, :taps]


def tap_grad(grads, query, mixed, groups, taps):
    rows, channels = query.shape
    ext = mixed.shape[0]
    block = 128 if channels % 128 == 0 else channels
    steps = channels // block
    per_step = groups // steps
    span = 2 * taps
    one = pl.BlockSpec((rows, block), lambda i: (0, i))
    return pl.pallas_call(
        functools.partial(tap_grad_kernel, per_step),
        grid=(steps,),
        out_shape=[
            jax.ShapeDtypeStruct((groups, taps), F32),
            jax.ShapeDtypeStruct((1, channels), F32),
        ],
        in_specs=[
            pl.BlockSpec((grads.shape[0], rows, block), lambda i: (0, 0, i)),
            one,
            pl.BlockSpec((ext, block), lambda i: (0, i)),
        ],
        out_specs=[
            pl.BlockSpec((per_step, taps), lambda i: (i, 0)),
            pl.BlockSpec((1, block), lambda i: (0, i)),
        ],
        compiler_params=pltpu.CompilerParams(vmem_limit_bytes=SMALL_LIMIT),
        cost_estimate=pl.CostEstimate(
            flops=2 * groups * rows * span * 2 * block,
            bytes_accessed=4 * ext * channels + 6 * rows * channels,
            transcendentals=0,
        ),
        name="tap_grad",
    )(grads, query, mixed)


def branch_order(block, width):
    to = np.arange(3 * block)
    branch, channel = to // block, to % block
    source = 3 * width * (channel // width) + width * branch + channel % width
    return jnp.asarray(np.arange(3 * block)[:, None] == source[None, :], BF16)


def local(tokens, w_in, short_filter, mr_filter, skip, w_out, grad_out):
    high, low = split_axis(lax.axis_size("col"))
    row_size = lax.axis_size("row")
    channels = tokens.shape[1]
    groups, taps = mr_filter.shape
    width = channels // groups
    block = 128 if channels % 128 == 0 else channels

    order = branch_order(block, width)
    gather = Gather(tokens, high, low)
    parts = partials(grad_out, w_out, high, low)
    gather.pass_on(parts, gather.late)
    bands, filters = prepare(*after((mr_filter, short_filter), gather.line), order)
    projected = gather.finish(w_in, BF16, "project", (bands, filters))
    earlier = lax.ppermute(projected, "row", [(r, r + 1) for r in range(row_size - 1)])
    gated, query, mixed = mixing(earlier, projected, order, filters, bands, skip[None], groups)
    parts = list(after(parts, gather.total))
    gather = Gather(gated, high, low)

    for step in reversed(range(low.bit_length() - 1)):
        moved = after(swap_low(parts.pop(), high, low, step), gather.near)
        at = 0
        for i, part in enumerate(parts):
            count = part.shape[0]
            total = part.astype(F32) + moved[at : at + count].astype(F32)
            parts[i], at = total.astype(BF16), at + count
    gather.pass_on()
    sums = after(parts[0], gather.line)
    lines = [[h * low + l for h in range(high)] for l in range(low)]
    grads = lax.all_to_all(sums, "col", 0, 0, axis_index_groups=lines, tiled=True)
    block_out = gather.finish(w_out, BF16, "output", (sums,))
    grads = after(grads, gather.far[1])

    tap_part, skip_part = tap_grad(grads, query, mixed, groups, taps)
    if row_size == 2:
        flat = jnp.concatenate([tap_part.reshape(-1), skip_part.reshape(-1)])
        flat = flat + lax.ppermute(flat, "row", [(0, 1), (1, 0)])
        filter_grad = flat[: groups * taps].reshape(groups, taps)
        skip_grad = flat[groups * taps :]
    else:
        filter_grad, skip_grad = lax.psum((tap_part, skip_part.reshape(-1)), "row")
    return (block_out, filter_grad, skip_grad)


def solution(mesh):
    in_specs = (
        P("row", "col"),
        P(None, "col"),
        P(None, "col"),
        P("col", None),
        P("col"),
        P(None, "col"),
        P("row", "col"),
    )
    out_specs = (P("row", "col"), P("col", None), P("col"))
    return jax.shard_map(local, mesh=mesh, in_specs=in_specs, out_specs=out_specs, check_vma=False)
```

```python
import functools

import jax
import jax.numpy as jnp
import numpy as np
from jax import lax
from jax.experimental import pallas as pl
from jax.experimental.pallas import tpu as pltpu
from jax.sharding import PartitionSpec as P

F32 = jnp.float32
BF16 = jnp.bfloat16
VMEM_SPEC = pl.BlockSpec(memory_space=pltpu.VMEM)
SMEM_SPEC = pl.BlockSpec(memory_space=pltpu.SMEM)
HBM_SPEC = pl.BlockSpec(memory_space=pltpu.HBM)
WEIGHT_SLOTS = 4
VMEM_LIMIT = 47 * 2**20
SMALL_LIMIT = 16 * 2**20


def split_axis(size):
    low = 1
    while low * low < size and size % (low * 2) == 0:
        low *= 2
    return size // low, low


def low_masks(low, parity):
    bits = [1 << i for i in range(low.bit_length() - 1)]
    return bits[::-1] if parity else bits


def swap_low(block, high, low, step):
    rows = lax.axis_size("row")
    size = high * low
    route = []
    for r in range(rows):
        mask = low_masks(low, r % 2)[step]
        route += [(r * size + c, r * size + (c ^ mask)) for c in range(size)]
    return lax.ppermute(block, ("row", "col"), route)


def shift_high(block, high, low, k):
    route = [(h * low + l, ((h + k) % high) * low + l) for h in range(high) for l in range(low)]
    return lax.ppermute(block, "col", route)


def flipped_low(low):
    parity = lax.axis_index("row") % 2
    forward, backward = low_masks(low, 0), low_masks(low, 1)
    flips = [0]
    for one, other in zip(forward, backward):
        mask = jnp.where(parity == 0, one, other)
        flips += [flip + mask for flip in flips]
    return flips


def after(values, *others):
    return lax.optimization_barrier((values, others))[0]


class Gather:
    def __init__(self, block, high, low):
        self.high, self.low, self.block = high, low, block
        self.bits = low.bit_length() - 1
        shifts = [k for k in range(1, high) if 2 * k != high]
        shifts += [k for k in (high // 2,) if 2 * k == high]
        self.shifts = shifts
        lines = [[h * low + l for h in range(high)] for l in range(low)]
        self.line = lax.all_gather(block, "col", axis_index_groups=lines)
        items = self.plane([block], self.bits - 1)
        self.near = items[1:]
        items = after(items, self.near)
        self.late = [swap_low(each, high, low, self.bits - 1) for each in items]

    def plane(self, items, steps):
        for step in range(steps):
            items = items + [swap_low(each, self.high, self.low, step) for each in items]
        return items

    def pass_on(self, *others):
        self.line = after(self.line, self.near, others)
        h = lax.axis_index("col") // self.low
        places = [(h - k + self.high) % self.high for k in self.shifts]
        blocks = [lax.dynamic_index_in_dim(self.line, place, 0, False) for place in places]
        self.far = self.plane([jnp.stack(blocks)], self.bits - 1)

    def finish(self, weights, out_type, name, before_hop=()):
        high, low = self.high, self.low
        me = lax.axis_index("col")
        h, l = me // low, me % low
        flips = flipped_low(low)
        from_high = [(h - k + high) % high for k in self.shifts]
        small = weights.size < 2**23
        limit = VMEM_LIMIT if small else 34 * 2**20

        near_owners = [h * low + (l ^ flip) for flip in flips]
        own = 1 + len(self.near)
        owners = [f * low + l for f in range(high)] + near_owners[1:own]
        pieces = [self.line, *self.near]
        total, = accumulate(None, pieces, owners, weights, None, F32, 0, limit, name + "_0")
        hop = after(self.far, before_hop, total)
        last = [swap_low(each, high, low, self.bits - 1) for each in hop]
        self.last = last
        owners = near_owners[own:]
        owners += [f * low + (l ^ flip) for flip in flips[1:] for f in from_high]
        final = len(last) * len(from_high)
        loads = final if small else final // 2
        pieces = [*self.late, *self.far[1:]]
        total, ahead = accumulate(
            total, pieces, owners, weights, None, F32, loads, limit, name + "_1"
        )
        self.total = total
        owners = owners[len(owners) - final :]
        return accumulate(total, last, owners, weights, ahead, out_type, 0, limit, name + "_2")[0]


def accumulate_kernel(counts, has_total, ready, loads, width, owners, *refs):
    refs = list(refs)
    pieces = [refs.pop(0) for _ in counts]
    total = refs.pop(0) if has_total else None
    here = refs.pop(0) if ready else None
    weights, out = refs[:2]
    refs = refs[2:]
    ahead = refs.pop(0) if loads else None
    sums, held, sems, ahead_sems = refs
    order = [(p, i) for p, count in enumerate(counts) for i in range(count or 1)]
    depth = held.shape[1]

    def rows_of(step):
        return weights.at[pl.ds(pl.multiple_of(owners[step] * depth, depth), depth), :]

    def fetch(step):
        slot = step % WEIGHT_SLOTS
        return pltpu.make_async_copy(rows_of(step), held.at[slot], sems.at[slot])

    def load(at):
        return pltpu.make_async_copy(rows_of(len(order) + at), ahead.at[at], ahead_sems.at[at])

    for step in range(ready, min(ready + WEIGHT_SLOTS, len(order))):
        fetch(step).start()
    for step, (p, i) in enumerate(order):
        if step >= ready:
            fetch(step).wait()
        slot = step % WEIGHT_SLOTS
        rows = pieces[p][i] if counts[p] else pieces[p][...]
        for at in range(0, out.shape[1], width):
            cols = slice(at, at + width)
            part = here[step, :, cols] if step < ready else held[slot, :, cols]
            term = jnp.dot(rows, part, preferred_element_type=F32)
            if step == 0 and total is not None:
                term = term + total[:, cols]
            if step:
                term = term + sums[:, cols]
            if step + 1 == len(order):
                out[:, cols] = term.astype(out.dtype)
            else:
                sums[:, cols] = term
        if step >= ready and step + WEIGHT_SLOTS < len(order):
            fetch(step + WEIGHT_SLOTS).start()
        if step == max(0, len(order) - 1 - WEIGHT_SLOTS):
            for at in range(loads):
                load(at).start()
    for at in range(loads):
        load(at).wait()


def accumulate(total, pieces, owners, weights, here, out_type, loads, limit, name):
    counts = tuple(0 if piece.ndim == 2 else piece.shape[0] for piece in pieces)
    rows, depth = pieces[0].shape[-2:]
    columns = weights.shape[-1]
    width = next(w for w in (512, 256, 128, columns) if columns % w == 0)
    steps = sum(count or 1 for count in counts)
    ready = 0 if here is None else here.shape[0]
    operands = [jnp.stack(owners).astype(jnp.int32), *pieces]
    operands += [extra for extra in (total, here) if extra is not None]
    out_shape = [jax.ShapeDtypeStruct((rows, columns), out_type)]
    if loads:
        out_shape.append(jax.ShapeDtypeStruct((loads, depth, columns), weights.dtype))
    return pl.pallas_call(
        functools.partial(accumulate_kernel, counts, total is not None, ready, loads, width),
        out_shape=out_shape,
        in_specs=[SMEM_SPEC] + [VMEM_SPEC] * (len(operands) - 1) + [HBM_SPEC],
        out_specs=[VMEM_SPEC] * len(out_shape),
        scratch_shapes=[
            pltpu.VMEM((rows, columns), F32),
            pltpu.VMEM((WEIGHT_SLOTS, depth, columns), weights.dtype),
            pltpu.SemaphoreType.DMA((WEIGHT_SLOTS,)),
            pltpu.SemaphoreType.DMA((max(1, loads),)),
        ],
        compiler_params=pltpu.CompilerParams(vmem_limit_bytes=limit),
        cost_estimate=pl.CostEstimate(
            flops=2 * steps * rows * depth * columns,
            bytes_accessed=(steps + loads) * depth * columns * 2 + rows * columns * 8,
            transcendentals=0,
        ),
        name=name,
    )(*operands, weights)


def partials_kernel(owners, grads, weights, *refs):
    outs, (held, sems) = refs[:-2], refs[-2:]
    order = [(o, i) for o, out in enumerate(outs) for i in range(out.shape[0])]
    depth = held.shape[1]

    def fetch(step):
        start = pl.multiple_of(owners[step] * depth, depth)
        slot = step % WEIGHT_SLOTS
        return pltpu.make_async_copy(
            weights.at[pl.ds(start, depth), :], held.at[slot], sems.at[slot]
        )

    for step in range(min(WEIGHT_SLOTS, len(order))):
        fetch(step).start()
    for step, (o, i) in enumerate(order):
        fetch(step).wait()
        term = lax.dot_general(
            grads[...],
            held[step % WEIGHT_SLOTS],
            (((1,), (1,)), ((), ())),
            preferred_element_type=F32,
        )
        outs[o][i] = term.astype(outs[o].dtype)
        if step + WEIGHT_SLOTS < len(order):
            fetch(step + WEIGHT_SLOTS).start()


def partials(grads, weights, high, low):
    me = lax.axis_index("col")
    h, l = me // low, me % low
    owners = [((h + j) % high) * low + (l ^ flip) for flip in flipped_low(low) for j in range(high)]
    rows, features = grads.shape
    depth = weights.shape[0] // (high * low)
    counts = [high] + [high << step for step in range(low.bit_length() - 1)]
    return pl.pallas_call(
        partials_kernel,
        out_shape=[jax.ShapeDtypeStruct((count, rows, depth), BF16) for count in counts],
        in_specs=[SMEM_SPEC, VMEM_SPEC, HBM_SPEC],
        out_specs=[VMEM_SPEC] * len(counts),
        scratch_shapes=[
            pltpu.VMEM((WEIGHT_SLOTS, depth, features), weights.dtype),
            pltpu.SemaphoreType.DMA((WEIGHT_SLOTS,)),
        ],
        compiler_params=pltpu.CompilerParams(vmem_limit_bytes=VMEM_LIMIT),
        cost_estimate=pl.CostEstimate(
            flops=2 * rows * features * weights.shape[0],
            bytes_accessed=2 * weights.shape[0] * (features + rows),
            transcendentals=0,
        ),
        name="grad_partials",
    )(jnp.stack(owners).astype(jnp.int32), grads, weights)


def halves(value):
    top = value.astype(BF16)
    return top, (value - top.astype(F32)).astype(BF16)


def prepare_kernel(mr_filter, short_filter, order, table, filters):
    taps, span = table.shape[1:]
    ends = lax.broadcasted_iota(jnp.int32, (taps, span), 0) + lax.broadcasted_iota(
        jnp.int32, (taps, span), 1
    )
    flip = jnp.where(ends == taps, 1.0, 0.0).astype(BF16)
    first = jnp.dot(mr_filter[...].astype(BF16), flip, preferred_element_type=F32)
    for g in range(table.shape[0]):
        spreadout = jnp.broadcast_to(first[g : g + 1, :], (taps, span))
        table[g] = pltpu.roll(spreadout, 0, 1, stride=1, stride_axis=0).astype(table.dtype)
    size = order.shape[0]
    for at in range(0, filters.shape[1], size):
        left = short_filter[:, at : at + size]
        moved = jnp.zeros(left.shape, F32)
        for _ in range(3):
            part = left.astype(BF16)
            moved = moved + jnp.dot(part, order[...], preferred_element_type=F32)
            left = left - part.astype(F32)
        filters[:, at : at + size] = moved


def prepare(mr_filter, short_filter, order):
    groups, taps = mr_filter.shape
    return pl.pallas_call(
        prepare_kernel,
        out_shape=[
            jax.ShapeDtypeStruct((groups, taps, 2 * taps), BF16),
            jax.ShapeDtypeStruct(short_filter.shape, F32),
        ],
        in_specs=[VMEM_SPEC] * 3,
        out_specs=[VMEM_SPEC] * 2,
        compiler_params=pltpu.CompilerParams(vmem_limit_bytes=SMALL_LIMIT),
        name="prepare",
    )(mr_filter, short_filter, order)


def mixing_kernel(groups, earlier, projected, order, filters, bands, skip, gated, query, mixed):
    rows = projected.shape[0]
    channels = skip.shape[1]
    taps = bands.shape[1]
    span = 2 * taps
    extended = jnp.concatenate([earlier[...].astype(F32), projected[...].astype(F32)], 0).astype(BF16)
    lines = jnp.dot(extended, order[...], preferred_element_type=F32)
    short = (
        filters[0:1, :] * lines
        + filters[1:2, :] * pltpu.roll(lines, 1, 0)
        + filters[2:3, :] * pltpu.roll(lines, 2, 0)
    )
    own_query = short[rows:, :channels]
    both = short[:, channels : 2 * channels] * short[:, 2 * channels :]
    query[...] = own_query
    mixed[...] = both
    both_top, both_rest = halves(both)
    pair = jnp.concatenate([both_top, both_rest], 1)
    lane_group = lax.broadcasted_iota(jnp.int32, (taps, channels), 1) // (channels // groups)
    first = spare = rows - taps
    whole = bands[...].reshape(groups * taps, span)
    ends = bands[:, taps - spare :, :].reshape(groups * spare, span)
    bodies = jnp.dot(whole, pair[first : first + span], preferred_element_type=F32)
    tails = jnp.dot(ends, pair[2 * first :], preferred_element_type=F32)
    bodies = bodies[:, :channels] + bodies[:, channels:]
    tails = tails[:, :channels] + tails[:, channels:]
    body, tail = bodies[:taps], tails[:spare]
    for g in range(1, groups):
        body = jnp.where(lane_group == g, bodies[g * taps : (g + 1) * taps], body)
        tail = jnp.where(lane_group[:spare] == g, tails[g * spare : (g + 1) * spare], tail)
    longconv = jnp.concatenate([body, tail], 0)
    gated[...] = (own_query * (longconv + skip[...] * both[rows:])).astype(gated.dtype)


def mixing(earlier, projected, order, filters, bands, skip, groups):
    rows, columns = projected.shape
    channels = columns // 3
    block = order.shape[0] // 3
    steps = channels // block
    per_step = groups // steps
    taps = bands.shape[1]
    ext = 2 * rows
    table = pl.BlockSpec((per_step, taps, 2 * taps), lambda i: (i, 0, 0))
    return pl.pallas_call(
        functools.partial(mixing_kernel, per_step),
        grid=(steps,),
        out_shape=[
            jax.ShapeDtypeStruct((rows, channels), BF16),
            jax.ShapeDtypeStruct((rows, channels), F32),
            jax.ShapeDtypeStruct((ext, channels), F32),
        ],
        in_specs=[
            pl.BlockSpec((rows, 3 * block), lambda i: (0, i)),
            pl.BlockSpec((rows, 3 * block), lambda i: (0, i)),
            pl.BlockSpec((3 * block, 3 * block), lambda i: (0, 0)),
            pl.BlockSpec((3, 3 * block), lambda i: (0, i)),
            table,
            pl.BlockSpec((1, block), lambda i: (0, i)),
        ],
        out_specs=[
            pl.BlockSpec((rows, block), lambda i: (0, i)),
            pl.BlockSpec((rows, block), lambda i: (0, i)),
            pl.BlockSpec((ext, block), lambda i: (0, i)),
        ],
        compiler_params=pltpu.CompilerParams(vmem_limit_bytes=SMALL_LIMIT),
        cost_estimate=pl.CostEstimate(
            flops=2 * 2 * groups * rows * 2 * taps * 2 * block,
            bytes_accessed=4 * ext * channels + 6 * ext * channels + 4 * groups * taps * taps,
            transcendentals=0,
        ),
        name="mixing",
    )(earlier, projected, order, filters, bands, skip)


def tap_grad_kernel(groups, pieces, *refs):
    grads, (query, mixed, taps_out, skip_out) = refs[:pieces], refs[pieces:]
    total = grads[0][...].astype(F32)
    for piece in grads[1:]:
        total = total + piece[...].astype(F32)
    weighted = total * query[...]
    rows, channels = weighted.shape
    taps = taps_out.shape[1]
    span = 2 * taps
    first = rows - taps
    spare = rows - taps
    both = mixed[...]
    skip_out[...] = jnp.sum(weighted * both[rows:], axis=0, keepdims=True)
    both_top = both.astype(BF16)
    flip = jnp.where(
        lax.broadcasted_iota(jnp.int32, (span, span), 0)
        + lax.broadcasted_iota(jnp.int32, (span, span), 1)
        == span - 1,
        1.0,
        0.0,
    ).astype(BF16)

    def backwards(start):
        end = jnp.dot(flip, both_top[start : start + span], preferred_element_type=F32)
        return jnp.concatenate([end.astype(BF16)] * 2, 1)

    near, far = backwards(first), backwards(2 * first)
    parts = jnp.concatenate(halves(weighted), 1)
    lane_group = (lax.broadcasted_iota(jnp.int32, (1, 2 * channels), 1) % channels) // (
        channels // groups
    )
    contract = (((1,), (1,)), ((), ()))
    masks = [jnp.where(lane_group == g, 1.0, 0.0).astype(BF16) for g in range(groups)]
    sides = jnp.concatenate([parts[:taps] * mask for mask in masks], 0)
    ends = jnp.concatenate([parts[taps:].astype(F32) * mask.astype(F32) for mask in masks], 0)
    bodies = lax.dot_general(sides, near, contract, preferred_element_type=F32)
    tails = lax.dot_general(ends.astype(BF16), far, contract, preferred_element_type=F32)
    for g in range(groups):
        body = bodies[g * taps : (g + 1) * taps]
        tail = tails[g * spare : (g + 1) * spare]
        body = jnp.concatenate([body[: taps - spare], body[taps - spare :] + tail], 0)
        skewed = pltpu.roll(body, 0, 1, stride=1, stride_axis=0)
        line = jnp.sum(skewed, axis=0, keepdims=True)
        taps_out[g : g + 1, :] = pltpu.roll(line, span - (taps - 1), 1)[:, :taps]


def tap_grad(grads, query, mixed, groups, taps):
    rows, channels = query.shape
    ext = mixed.shape[0]
    block = 128 if channels % 128 == 0 else channels
    steps = channels // block
    per_step = groups // steps
    span = 2 * taps
    one = pl.BlockSpec((rows, block), lambda i: (0, i))
    return pl.pallas_call(
        functools.partial(tap_grad_kernel, per_step, len(grads)),
        grid=(steps,),
        out_shape=[
            jax.ShapeDtypeStruct((groups, taps), F32),
            jax.ShapeDtypeStruct((1, channels), F32),
        ],
        in_specs=[one] * (len(grads) + 1) + [pl.BlockSpec((ext, block), lambda i: (0, i))],
        out_specs=[
            pl.BlockSpec((per_step, taps), lambda i: (i, 0)),
            pl.BlockSpec((1, block), lambda i: (0, i)),
        ],
        compiler_params=pltpu.CompilerParams(vmem_limit_bytes=SMALL_LIMIT),
        cost_estimate=pl.CostEstimate(
            flops=2 * groups * rows * span * 2 * block,
            bytes_accessed=4 * ext * channels + 6 * rows * channels,
            transcendentals=0,
        ),
        name="tap_grad",
    )(*grads, query, mixed)


def branch_order(block, width):
    to = np.arange(3 * block)
    branch, channel = to // block, to % block
    source = 3 * width * (channel // width) + width * branch + channel % width
    return jnp.asarray(np.arange(3 * block)[:, None] == source[None, :], BF16)


def local(tokens, w_in, short_filter, mr_filter, skip, w_out, grad_out):
    high, low = split_axis(lax.axis_size("col"))
    row_size = lax.axis_size("row")
    channels = tokens.shape[1]
    groups, taps = mr_filter.shape
    width = channels // groups
    block = 128 if channels % 128 == 0 else channels

    order = branch_order(block, width)
    gather = Gather(tokens, high, low)
    parts = partials(grad_out, w_out, high, low)
    gather.pass_on(parts, gather.late)
    bands, filters = prepare(*after((mr_filter, short_filter), gather.line), order)
    projected = gather.finish(w_in, BF16, "project", (bands, filters))
    earlier = lax.ppermute(projected, "row", [(r, r + 1) for r in range(row_size - 1)])
    gated, query, mixed = mixing(earlier, projected, order, filters, bands, skip[None], groups)
    parts = list(after(parts, gather.total))
    gather = Gather(gated, high, low)

    for step in reversed(range(low.bit_length() - 1)):
        moved = after(swap_low(parts.pop(), high, low, step), gather.near)
        at = 0
        for i, part in enumerate(parts):
            count = part.shape[0]
            total = part.astype(F32) + moved[at : at + count].astype(F32)
            parts[i], at = total.astype(BF16), at + count
    gather.pass_on(gather.late)
    sums = after([parts[0][j] for j in range(high)], gather.line)
    grads = [sums[0]] + [shift_high(sums[j], high, low, j) for j in range(1, high)]
    block_out = gather.finish(w_out, BF16, "output")
    grads = after(grads, gather.last[0], gather.total)

    tap_part, skip_part = tap_grad(grads, query, mixed, groups, taps)
    if row_size == 2:
        flat = jnp.concatenate([tap_part.reshape(-1), skip_part.reshape(-1)])
        flat = flat + lax.ppermute(flat, "row", [(0, 1), (1, 0)])
        filter_grad = flat[: groups * taps].reshape(groups, taps)
        skip_grad = flat[groups * taps :]
    else:
        filter_grad, skip_grad = lax.psum((tap_part, skip_part.reshape(-1)), "row")
    return (block_out, filter_grad, skip_grad)


def solution(mesh):
    in_specs = (
        P("row", "col"),
        P(None, "col"),
        P(None, "col"),
        P("col", None),
        P("col"),
        P(None, "col"),
        P("row", "col"),
    )
    out_specs = (P("row", "col"), P("col", None), P("col"))
    return jax.shard_map(local, mesh=mesh, in_specs=in_specs, out_specs=out_specs, check_vma=False)
```

```python
import functools

import jax
import jax.numpy as jnp
import numpy as np
from jax import lax
from jax.experimental import pallas as pl
from jax.experimental.pallas import tpu as pltpu
from jax.sharding import PartitionSpec as P

F32 = jnp.float32
BF16 = jnp.bfloat16
VMEM_SPEC = pl.BlockSpec(memory_space=pltpu.VMEM)
SMEM_SPEC = pl.BlockSpec(memory_space=pltpu.SMEM)
HBM_SPEC = pl.BlockSpec(memory_space=pltpu.HBM)
WEIGHT_SLOTS = 4
VMEM_LIMIT = 47 * 2**20
SMALL_LIMIT = 16 * 2**20


def split_axis(size):
    low = 1
    while low * low < size and size % (low * 2) == 0:
        low *= 2
    return size // low, low


def low_masks(low, parity):
    bits = [1 << i for i in range(low.bit_length() - 1)]
    return bits[::-1] if parity else bits


def swap_low(block, high, low, step):
    rows = lax.axis_size("row")
    size = high * low
    route = []
    for r in range(rows):
        mask = low_masks(low, r % 2)[step]
        route += [(r * size + c, r * size + (c ^ mask)) for c in range(size)]
    return lax.ppermute(block, ("row", "col"), route)


def shift_high(block, high, low, k):
    route = [(h * low + l, ((h + k) % high) * low + l) for h in range(high) for l in range(low)]
    return lax.ppermute(block, "col", route)


def flipped_low(low):
    parity = lax.axis_index("row") % 2
    forward, backward = low_masks(low, 0), low_masks(low, 1)
    flips = [0]
    for one, other in zip(forward, backward):
        mask = jnp.where(parity == 0, one, other)
        flips += [flip + mask for flip in flips]
    return flips


def after(values, *others):
    return lax.optimization_barrier((values, others))[0]


class Gather:
    def __init__(self, block, high, low):
        self.high, self.low, self.block = high, low, block
        self.bits = low.bit_length() - 1
        shifts = [k for k in range(1, high) if 2 * k != high]
        shifts += [k for k in (high // 2,) if 2 * k == high]
        self.shifts = shifts
        self.line = [shift_high(block, high, low, k) for k in shifts]
        near = self.plane([block], self.bits - 1)
        late = after(near, near[1:])
        self.near = near[1:]
        self.late = [swap_low(each, high, low, self.bits - 1) for each in late]

    def plane(self, items, steps):
        for step in range(steps):
            items = items + [swap_low(each, self.high, self.low, step) for each in items]
        return items

    def pass_on(self, *others):
        self.line = after(self.line, self.near, others)
        self.far = self.plane([jnp.stack(self.line)], self.bits - 1)

    def finish(self, weights, out_type, name, before_hop=()):
        high, low = self.high, self.low
        me = lax.axis_index("col")
        h, l = me // low, me % low
        flips = flipped_low(low)
        from_high = [(h - k + high) % high for k in self.shifts]
        small = weights.size < 2**23
        limit = VMEM_LIMIT if small else 34 * 2**20

        owners = [h * low + (l ^ flip) for flip in flips]
        own = 1 + len(self.near)
        owners, late_owners = owners[:own], owners[own:]
        owners += [f * low + l for f in from_high]
        pieces = [self.block, *self.near, *self.line]
        total, = accumulate(None, pieces, owners, weights, None, F32, 0, limit, name + "_0")
        hop = after(self.far, total, before_hop)
        last = [swap_low(each, high, low, self.bits - 1) for each in hop]
        self.last = last
        owners = late_owners + [f * low + (l ^ flip) for flip in flips[1:] for f in from_high]
        final = len(last) * len(self.line)
        loads = final if small else final // 2
        pieces = [*self.late, *self.far[1:]]
        total, ahead = accumulate(
            total, pieces, owners, weights, None, F32, loads, limit, name + "_1"
        )
        self.total = total
        owners = owners[len(owners) - final :]
        return accumulate(total, last, owners, weights, ahead, out_type, 0, limit, name + "_2")[0]


def accumulate_kernel(counts, has_total, ready, loads, width, owners, *refs):
    refs = list(refs)
    pieces = [refs.pop(0) for _ in counts]
    total = refs.pop(0) if has_total else None
    here = refs.pop(0) if ready else None
    weights, out = refs[:2]
    refs = refs[2:]
    ahead = refs.pop(0) if loads else None
    sums, held, sems, ahead_sems = refs
    order = [(p, i) for p, count in enumerate(counts) for i in range(count or 1)]
    depth = held.shape[1]

    def rows_of(step):
        return weights.at[pl.ds(pl.multiple_of(owners[step] * depth, depth), depth), :]

    def fetch(step):
        slot = step % WEIGHT_SLOTS
        return pltpu.make_async_copy(rows_of(step), held.at[slot], sems.at[slot])

    def load(at):
        return pltpu.make_async_copy(rows_of(len(order) + at), ahead.at[at], ahead_sems.at[at])

    for step in range(ready, min(ready + WEIGHT_SLOTS, len(order))):
        fetch(step).start()
    for step, (p, i) in enumerate(order):
        if step >= ready:
            fetch(step).wait()
        slot = step % WEIGHT_SLOTS
        rows = pieces[p][i] if counts[p] else pieces[p][...]
        for at in range(0, out.shape[1], width):
            cols = slice(at, at + width)
            part = here[step, :, cols] if step < ready else held[slot, :, cols]
            term = jnp.dot(rows, part, preferred_element_type=F32)
            if step == 0 and total is not None:
                term = term + total[:, cols]
            if step:
                term = term + sums[:, cols]
            if step + 1 == len(order):
                out[:, cols] = term.astype(out.dtype)
            else:
                sums[:, cols] = term
        if step >= ready and step + WEIGHT_SLOTS < len(order):
            fetch(step + WEIGHT_SLOTS).start()
        if step == max(0, len(order) - 1 - WEIGHT_SLOTS):
            for at in range(loads):
                load(at).start()
    for at in range(loads):
        load(at).wait()


def accumulate(total, pieces, owners, weights, here, out_type, loads, limit, name):
    counts = tuple(0 if piece.ndim == 2 else piece.shape[0] for piece in pieces)
    rows, depth = pieces[0].shape[-2:]
    columns = weights.shape[-1]
    width = next(w for w in (512, 256, 128, columns) if columns % w == 0)
    steps = sum(count or 1 for count in counts)
    ready = 0 if here is None else here.shape[0]
    operands = [jnp.stack(owners).astype(jnp.int32), *pieces]
    operands += [extra for extra in (total, here) if extra is not None]
    out_shape = [jax.ShapeDtypeStruct((rows, columns), out_type)]
    if loads:
        out_shape.append(jax.ShapeDtypeStruct((loads, depth, columns), weights.dtype))
    return pl.pallas_call(
        functools.partial(accumulate_kernel, counts, total is not None, ready, loads, width),
        out_shape=out_shape,
        in_specs=[SMEM_SPEC] + [VMEM_SPEC] * (len(operands) - 1) + [HBM_SPEC],
        out_specs=[VMEM_SPEC] * len(out_shape),
        scratch_shapes=[
            pltpu.VMEM((rows, columns), F32),
            pltpu.VMEM((WEIGHT_SLOTS, depth, columns), weights.dtype),
            pltpu.SemaphoreType.DMA((WEIGHT_SLOTS,)),
            pltpu.SemaphoreType.DMA((max(1, loads),)),
        ],
        compiler_params=pltpu.CompilerParams(vmem_limit_bytes=limit),
        cost_estimate=pl.CostEstimate(
            flops=2 * steps * rows * depth * columns,
            bytes_accessed=(steps + loads) * depth * columns * 2 + rows * columns * 8,
            transcendentals=0,
        ),
        name=name,
    )(*operands, weights)


def partials_kernel(owners, grads, weights, *refs):
    outs, (held, sems) = refs[:-2], refs[-2:]
    order = [(o, i) for o, out in enumerate(outs) for i in range(out.shape[0])]
    depth = held.shape[1]

    def fetch(step):
        start = pl.multiple_of(owners[step] * depth, depth)
        slot = step % WEIGHT_SLOTS
        return pltpu.make_async_copy(
            weights.at[pl.ds(start, depth), :], held.at[slot], sems.at[slot]
        )

    for step in range(min(WEIGHT_SLOTS, len(order))):
        fetch(step).start()
    for step, (o, i) in enumerate(order):
        fetch(step).wait()
        term = lax.dot_general(
            grads[...],
            held[step % WEIGHT_SLOTS],
            (((1,), (1,)), ((), ())),
            preferred_element_type=F32,
        )
        outs[o][i] = term.astype(outs[o].dtype)
        if step + WEIGHT_SLOTS < len(order):
            fetch(step + WEIGHT_SLOTS).start()


def partials(grads, weights, high, low):
    me = lax.axis_index("col")
    h, l = me // low, me % low
    owners = [((h + j) % high) * low + (l ^ flip) for flip in flipped_low(low) for j in range(high)]
    rows, features = grads.shape
    depth = weights.shape[0] // (high * low)
    counts = [high] + [high << step for step in range(low.bit_length() - 1)]
    return pl.pallas_call(
        partials_kernel,
        out_shape=[jax.ShapeDtypeStruct((count, rows, depth), BF16) for count in counts],
        in_specs=[SMEM_SPEC, VMEM_SPEC, HBM_SPEC],
        out_specs=[VMEM_SPEC] * len(counts),
        scratch_shapes=[
            pltpu.VMEM((WEIGHT_SLOTS, depth, features), weights.dtype),
            pltpu.SemaphoreType.DMA((WEIGHT_SLOTS,)),
        ],
        compiler_params=pltpu.CompilerParams(vmem_limit_bytes=VMEM_LIMIT),
        cost_estimate=pl.CostEstimate(
            flops=2 * rows * features * weights.shape[0],
            bytes_accessed=2 * weights.shape[0] * (features + rows),
            transcendentals=0,
        ),
        name="grad_partials",
    )(jnp.stack(owners).astype(jnp.int32), grads, weights)


def halves(value):
    top = value.astype(BF16)
    return top, (value - top.astype(F32)).astype(BF16)


def prepare_kernel(mr_filter, short_filter, order, table, filters):
    taps, span = table.shape[1:]
    ends = lax.broadcasted_iota(jnp.int32, (taps, span), 0) + lax.broadcasted_iota(
        jnp.int32, (taps, span), 1
    )
    flip = jnp.where(ends == taps, 1.0, 0.0).astype(BF16)
    first = jnp.dot(mr_filter[...].astype(BF16), flip, preferred_element_type=F32)
    for g in range(table.shape[0]):
        spreadout = jnp.broadcast_to(first[g : g + 1, :], (taps, span))
        table[g] = pltpu.roll(spreadout, 0, 1, stride=1, stride_axis=0).astype(table.dtype)
    size = order.shape[0]
    for at in range(0, filters.shape[1], size):
        left = short_filter[:, at : at + size]
        moved = jnp.zeros(left.shape, F32)
        for _ in range(3):
            part = left.astype(BF16)
            moved = moved + jnp.dot(part, order[...], preferred_element_type=F32)
            left = left - part.astype(F32)
        filters[:, at : at + size] = moved


def prepare(mr_filter, short_filter, order):
    groups, taps = mr_filter.shape
    return pl.pallas_call(
        prepare_kernel,
        out_shape=[
            jax.ShapeDtypeStruct((groups, taps, 2 * taps), BF16),
            jax.ShapeDtypeStruct(short_filter.shape, F32),
        ],
        in_specs=[VMEM_SPEC] * 3,
        out_specs=[VMEM_SPEC] * 2,
        compiler_params=pltpu.CompilerParams(vmem_limit_bytes=SMALL_LIMIT),
        name="prepare",
    )(mr_filter, short_filter, order)


def mixing_kernel(groups, earlier, projected, order, filters, bands, skip, gated, query, mixed):
    rows = projected.shape[0]
    channels = skip.shape[1]
    taps = bands.shape[1]
    span = 2 * taps
    extended = jnp.concatenate([earlier[...].astype(F32), projected[...].astype(F32)], 0).astype(BF16)
    lines = jnp.dot(extended, order[...], preferred_element_type=F32)
    short = (
        filters[0:1, :] * lines
        + filters[1:2, :] * pltpu.roll(lines, 1, 0)
        + filters[2:3, :] * pltpu.roll(lines, 2, 0)
    )
    own_query = short[rows:, :channels]
    both = short[:, channels : 2 * channels] * short[:, 2 * channels :]
    query[...] = own_query
    mixed[...] = both
    both_top, both_rest = halves(both)
    pair = jnp.concatenate([both_top, both_rest], 1)
    lane_group = lax.broadcasted_iota(jnp.int32, (taps, channels), 1) // (channels // groups)
    first = spare = rows - taps
    whole = bands[...].reshape(groups * taps, span)
    ends = bands[:, taps - spare :, :].reshape(groups * spare, span)
    bodies = jnp.dot(whole, pair[first : first + span], preferred_element_type=F32)
    tails = jnp.dot(ends, pair[2 * first :], preferred_element_type=F32)
    bodies = bodies[:, :channels] + bodies[:, channels:]
    tails = tails[:, :channels] + tails[:, channels:]
    body, tail = bodies[:taps], tails[:spare]
    for g in range(1, groups):
        body = jnp.where(lane_group == g, bodies[g * taps : (g + 1) * taps], body)
        tail = jnp.where(lane_group[:spare] == g, tails[g * spare : (g + 1) * spare], tail)
    longconv = jnp.concatenate([body, tail], 0)
    gated[...] = (own_query * (longconv + skip[...] * both[rows:])).astype(gated.dtype)


def mixing(earlier, projected, order, filters, bands, skip, groups):
    rows, columns = projected.shape
    channels = columns // 3
    block = order.shape[0] // 3
    steps = channels // block
    per_step = groups // steps
    taps = bands.shape[1]
    ext = 2 * rows
    table = pl.BlockSpec((per_step, taps, 2 * taps), lambda i: (i, 0, 0))
    return pl.pallas_call(
        functools.partial(mixing_kernel, per_step),
        grid=(steps,),
        out_shape=[
            jax.ShapeDtypeStruct((rows, channels), BF16),
            jax.ShapeDtypeStruct((rows, channels), F32),
            jax.ShapeDtypeStruct((ext, channels), F32),
        ],
        in_specs=[
            pl.BlockSpec((rows, 3 * block), lambda i: (0, i)),
            pl.BlockSpec((rows, 3 * block), lambda i: (0, i)),
            pl.BlockSpec((3 * block, 3 * block), lambda i: (0, 0)),
            pl.BlockSpec((3, 3 * block), lambda i: (0, i)),
            table,
            pl.BlockSpec((1, block), lambda i: (0, i)),
        ],
        out_specs=[
            pl.BlockSpec((rows, block), lambda i: (0, i)),
            pl.BlockSpec((rows, block), lambda i: (0, i)),
            pl.BlockSpec((ext, block), lambda i: (0, i)),
        ],
        compiler_params=pltpu.CompilerParams(vmem_limit_bytes=SMALL_LIMIT),
        cost_estimate=pl.CostEstimate(
            flops=2 * 2 * groups * rows * 2 * taps * 2 * block,
            bytes_accessed=4 * ext * channels + 6 * ext * channels + 4 * groups * taps * taps,
            transcendentals=0,
        ),
        name="mixing",
    )(earlier, projected, order, filters, bands, skip)


def tap_grad_kernel(groups, pieces, *refs):
    grads, (query, mixed, taps_out, skip_out) = refs[:pieces], refs[pieces:]
    total = grads[0][...].astype(F32)
    for piece in grads[1:]:
        total = total + piece[...].astype(F32)
    weighted = total * query[...]
    rows, channels = weighted.shape
    taps = taps_out.shape[1]
    span = 2 * taps
    first = rows - taps
    spare = rows - taps
    both = mixed[...]
    skip_out[...] = jnp.sum(weighted * both[rows:], axis=0, keepdims=True)
    both_top = both.astype(BF16)
    flip = jnp.where(
        lax.broadcasted_iota(jnp.int32, (span, span), 0)
        + lax.broadcasted_iota(jnp.int32, (span, span), 1)
        == span - 1,
        1.0,
        0.0,
    ).astype(BF16)

    def backwards(start):
        end = jnp.dot(flip, both_top[start : start + span], preferred_element_type=F32)
        return jnp.concatenate([end.astype(BF16)] * 2, 1)

    near, far = backwards(first), backwards(2 * first)
    parts = jnp.concatenate(halves(weighted), 1)
    lane_group = (lax.broadcasted_iota(jnp.int32, (1, 2 * channels), 1) % channels) // (
        channels // groups
    )
    contract = (((1,), (1,)), ((), ()))
    masks = [jnp.where(lane_group == g, 1.0, 0.0).astype(BF16) for g in range(groups)]
    sides = jnp.concatenate([parts[:taps] * mask for mask in masks], 0)
    ends = jnp.concatenate([parts[taps:].astype(F32) * mask.astype(F32) for mask in masks], 0)
    bodies = lax.dot_general(sides, near, contract, preferred_element_type=F32)
    tails = lax.dot_general(ends.astype(BF16), far, contract, preferred_element_type=F32)
    for g in range(groups):
        body = bodies[g * taps : (g + 1) * taps]
        tail = tails[g * spare : (g + 1) * spare]
        body = jnp.concatenate([body[: taps - spare], body[taps - spare :] + tail], 0)
        skewed = pltpu.roll(body, 0, 1, stride=1, stride_axis=0)
        line = jnp.sum(skewed, axis=0, keepdims=True)
        taps_out[g : g + 1, :] = pltpu.roll(line, span - (taps - 1), 1)[:, :taps]


def tap_grad(grads, query, mixed, groups, taps):
    rows, channels = query.shape
    ext = mixed.shape[0]
    block = 128 if channels % 128 == 0 else channels
    steps = channels // block
    per_step = groups // steps
    span = 2 * taps
    one = pl.BlockSpec((rows, block), lambda i: (0, i))
    return pl.pallas_call(
        functools.partial(tap_grad_kernel, per_step, len(grads)),
        grid=(steps,),
        out_shape=[
            jax.ShapeDtypeStruct((groups, taps), F32),
            jax.ShapeDtypeStruct((1, channels), F32),
        ],
        in_specs=[one] * (len(grads) + 1) + [pl.BlockSpec((ext, block), lambda i: (0, i))],
        out_specs=[
            pl.BlockSpec((per_step, taps), lambda i: (i, 0)),
            pl.BlockSpec((1, block), lambda i: (0, i)),
        ],
        compiler_params=pltpu.CompilerParams(vmem_limit_bytes=SMALL_LIMIT),
        cost_estimate=pl.CostEstimate(
            flops=2 * groups * rows * span * 2 * block,
            bytes_accessed=4 * ext * channels + 6 * rows * channels,
            transcendentals=0,
        ),
        name="tap_grad",
    )(*grads, query, mixed)


def branch_order(block, width):
    to = np.arange(3 * block)
    branch, channel = to // block, to % block
    source = 3 * width * (channel // width) + width * branch + channel % width
    return jnp.asarray(np.arange(3 * block)[:, None] == source[None, :], BF16)


def local(tokens, w_in, short_filter, mr_filter, skip, w_out, grad_out):
    high, low = split_axis(lax.axis_size("col"))
    row_size = lax.axis_size("row")
    channels = tokens.shape[1]
    groups, taps = mr_filter.shape
    width = channels // groups
    block = 128 if channels % 128 == 0 else channels

    order = branch_order(block, width)
    gather = Gather(tokens, high, low)
    parts = partials(grad_out, w_out, high, low)
    gather.pass_on(parts, gather.late)
    bands, filters = prepare(*after((mr_filter, short_filter), gather.line), order)
    projected = gather.finish(w_in, BF16, "project", (bands, filters))
    earlier = lax.ppermute(projected, "row", [(r, r + 1) for r in range(row_size - 1)])
    gated, query, mixed = mixing(earlier, projected, order, filters, bands, skip[None], groups)
    parts = after(parts, gather.total)
    gather = Gather(gated, high, low)

    parts = list(parts)
    for step in reversed(range(low.bit_length() - 1)):
        moved = after(swap_low(parts.pop(), high, low, step), gather.near)
        at = 0
        for i, part in enumerate(parts):
            count = part.shape[0]
            total = part.astype(F32) + moved[at : at + count].astype(F32)
            parts[i], at = total.astype(BF16), at + count
    gather.pass_on()
    sums = after([parts[0][j] for j in range(high)], gather.line)
    grads = [sums[0]] + [shift_high(sums[j], high, low, j) for j in range(1, high)]
    block_out = gather.finish(w_out, BF16, "output", ())
    grads = after(grads, (gather.last[0], gather.total))

    tap_part, skip_part = tap_grad(grads, query, mixed, groups, taps)
    if row_size == 2:
        swap = [(0, 1), (1, 0)]
        filter_grad = tap_part + lax.ppermute(tap_part, "row", swap)
        skip_grad = (skip_part + lax.ppermute(skip_part, "row", swap)).reshape(-1)
    else:
        filter_grad, skip_grad = lax.psum((tap_part, skip_part.reshape(-1)), "row")
    return (block_out, filter_grad, skip_grad)


def solution(mesh):
    in_specs = (
        P("row", "col"),
        P(None, "col"),
        P(None, "col"),
        P("col", None),
        P("col"),
        P(None, "col"),
        P("row", "col"),
    )
    out_specs = (P("row", "col"), P("col", None), P("col"))
    return jax.shard_map(local, mesh=mesh, in_specs=in_specs, out_specs=out_specs, check_vma=False)
```

```python
import functools

import jax
import jax.numpy as jnp
import numpy as np
from jax import lax
from jax.experimental import pallas as pl
from jax.experimental.pallas import tpu as pltpu
from jax.sharding import PartitionSpec as P

F32 = jnp.float32
BF16 = jnp.bfloat16
VMEM_SPEC = pl.BlockSpec(memory_space=pltpu.VMEM)
SMEM_SPEC = pl.BlockSpec(memory_space=pltpu.SMEM)
HBM_SPEC = pl.BlockSpec(memory_space=pltpu.HBM)
WEIGHT_SLOTS = 4
VMEM_LIMIT = 47 * 2**20
SMALL_LIMIT = 16 * 2**20


def split_axis(size):
    low = 1
    while low * low < size and size % (low * 2) == 0:
        low *= 2
    return size // low, low


def low_masks(low, parity):
    bits = [1 << i for i in range(low.bit_length() - 1)]
    return bits[::-1] if parity else bits


def swap_low(block, high, low, step):
    rows = lax.axis_size("row")
    size = high * low
    route = []
    for r in range(rows):
        mask = low_masks(low, r % 2)[step]
        route += [(r * size + c, r * size + (c ^ mask)) for c in range(size)]
    return lax.ppermute(block, ("row", "col"), route)


def shift_high(block, high, low, k):
    route = [(h * low + l, ((h + k) % high) * low + l) for h in range(high) for l in range(low)]
    return lax.ppermute(block, "col", route)


def flipped_low(low):
    parity = lax.axis_index("row") % 2
    forward, backward = low_masks(low, 0), low_masks(low, 1)
    flips = [0]
    for one, other in zip(forward, backward):
        mask = jnp.where(parity == 0, one, other)
        flips += [flip + mask for flip in flips]
    return flips


def after(values, *others):
    return lax.optimization_barrier((values, others))[0]


class Gather:
    def __init__(self, block, high, low, apart):
        self.high, self.low, self.block = high, low, block
        self.bits = low.bit_length() - 1
        shifts = sorted(range(1, high), key=lambda k: -min(k, high - k))
        self.shifts = shifts
        self.line = [shift_high(block, high, low, k) for k in shifts]
        self.near, self.late = [], []
        if apart:
            items = self.plane([block], self.bits - 1)
            self.near = items[1:]
            items = after(items, self.near)
            self.late = [swap_low(each, high, low, self.bits - 1) for each in items]

    def plane(self, items, steps):
        for step in range(steps):
            items = items + [swap_low(each, self.high, self.low, step) for each in items]
        return items

    def pass_on(self, *others):
        self.line = after(self.line, self.near, others)
        blocks = self.line if self.late else [self.block, *self.line]
        self.far = self.plane([jnp.stack(blocks)], self.bits - 1)

    def finish(self, weights, out_type, name, before_hop=()):
        high, low = self.high, self.low
        me = lax.axis_index("col")
        h, l = me // low, me % low
        flips = flipped_low(low)
        from_high = [(h - k + high) % high for k in self.shifts]
        small = weights.size < 2**23
        limit = VMEM_LIMIT if small else 34 * 2**20

        owners = [h * low + (l ^ flip) for flip in flips]
        own = 1 + len(self.near)
        owners, late_owners = owners[:own], owners[own:]
        owners += [f * low + l for f in from_high]
        pieces = [self.block, *self.near, *self.line]
        total, = accumulate(None, pieces, owners, weights, None, F32, 0, limit, name + "_0")
        hop = after(self.far, total, before_hop)
        last = [swap_low(each, high, low, self.bits - 1) for each in hop]
        self.last = last
        if not self.late:
            late_owners, from_high = [], [h, *from_high]
        owners = late_owners + [f * low + (l ^ flip) for flip in flips[1:] for f in from_high]
        final = len(last) * len(from_high)
        loads = final if small else 0
        pieces = [*self.late, *self.far[1:]]
        total, *ahead = accumulate(
            total, pieces, owners, weights, None, F32, loads, limit, name + "_1"
        )
        ahead = ahead[0] if loads else None
        self.total = total
        owners = owners[len(owners) - final :]
        return accumulate(total, last, owners, weights, ahead, out_type, 0, limit, name + "_2")[0]


def accumulate_kernel(counts, has_total, ready, loads, width, owners, *refs):
    refs = list(refs)
    pieces = [refs.pop(0) for _ in counts]
    total = refs.pop(0) if has_total else None
    here = refs.pop(0) if ready else None
    weights, out = refs[:2]
    refs = refs[2:]
    ahead = refs.pop(0) if loads else None
    sums, held, sems, ahead_sems = refs
    order = [(p, i) for p, count in enumerate(counts) for i in range(count or 1)]
    depth = held.shape[1]

    def rows_of(step):
        return weights.at[pl.ds(pl.multiple_of(owners[step] * depth, depth), depth), :]

    def fetch(step):
        slot = step % WEIGHT_SLOTS
        return pltpu.make_async_copy(rows_of(step), held.at[slot], sems.at[slot])

    def load(at):
        return pltpu.make_async_copy(rows_of(len(order) + at), ahead.at[at], ahead_sems.at[at])

    for step in range(ready, min(ready + WEIGHT_SLOTS, len(order))):
        fetch(step).start()
    for step, (p, i) in enumerate(order):
        if step >= ready:
            fetch(step).wait()
        slot = step % WEIGHT_SLOTS
        rows = pieces[p][i] if counts[p] else pieces[p][...]
        for at in range(0, out.shape[1], width):
            cols = slice(at, at + width)
            part = here[step, :, cols] if step < ready else held[slot, :, cols]
            term = jnp.dot(rows, part, preferred_element_type=F32)
            if step == 0 and total is not None:
                term = term + total[:, cols]
            if step:
                term = term + sums[:, cols]
            if step + 1 == len(order):
                out[:, cols] = term.astype(out.dtype)
            else:
                sums[:, cols] = term
        if step >= ready and step + WEIGHT_SLOTS < len(order):
            fetch(step + WEIGHT_SLOTS).start()
        if step == max(0, len(order) - 1 - WEIGHT_SLOTS):
            for at in range(loads):
                load(at).start()
    for at in range(loads):
        load(at).wait()


def accumulate(total, pieces, owners, weights, here, out_type, loads, limit, name):
    counts = tuple(0 if piece.ndim == 2 else piece.shape[0] for piece in pieces)
    rows, depth = pieces[0].shape[-2:]
    columns = weights.shape[-1]
    width = next(w for w in (512, 256, 128, columns) if columns % w == 0)
    steps = sum(count or 1 for count in counts)
    ready = 0 if here is None else here.shape[0]
    operands = [jnp.stack(owners).astype(jnp.int32), *pieces]
    operands += [extra for extra in (total, here) if extra is not None]
    out_shape = [jax.ShapeDtypeStruct((rows, columns), out_type)]
    if loads:
        out_shape.append(jax.ShapeDtypeStruct((loads, depth, columns), weights.dtype))
    return pl.pallas_call(
        functools.partial(accumulate_kernel, counts, total is not None, ready, loads, width),
        out_shape=out_shape,
        in_specs=[SMEM_SPEC] + [VMEM_SPEC] * (len(operands) - 1) + [HBM_SPEC],
        out_specs=[VMEM_SPEC] * len(out_shape),
        scratch_shapes=[
            pltpu.VMEM((rows, columns), F32),
            pltpu.VMEM((WEIGHT_SLOTS, depth, columns), weights.dtype),
            pltpu.SemaphoreType.DMA((WEIGHT_SLOTS,)),
            pltpu.SemaphoreType.DMA((max(1, loads),)),
        ],
        compiler_params=pltpu.CompilerParams(vmem_limit_bytes=limit),
        cost_estimate=pl.CostEstimate(
            flops=2 * steps * rows * depth * columns,
            bytes_accessed=(steps + loads) * depth * columns * 2 + rows * columns * 8,
            transcendentals=0,
        ),
        name=name,
    )(*operands, weights)


def partials_kernel(owners, grads, weights, *refs):
    outs, (held, sems) = refs[:-2], refs[-2:]
    order = [(o, i) for o, out in enumerate(outs) for i in range(out.shape[0])]
    depth = held.shape[1]

    def fetch(step):
        start = pl.multiple_of(owners[step] * depth, depth)
        slot = step % WEIGHT_SLOTS
        return pltpu.make_async_copy(
            weights.at[pl.ds(start, depth), :], held.at[slot], sems.at[slot]
        )

    for step in range(min(WEIGHT_SLOTS, len(order))):
        fetch(step).start()
    for step, (o, i) in enumerate(order):
        fetch(step).wait()
        term = lax.dot_general(
            grads[...],
            held[step % WEIGHT_SLOTS],
            (((1,), (1,)), ((), ())),
            preferred_element_type=F32,
        )
        outs[o][i] = term.astype(outs[o].dtype)
        if step + WEIGHT_SLOTS < len(order):
            fetch(step + WEIGHT_SLOTS).start()


def partials(grads, weights, high, low):
    me = lax.axis_index("col")
    h, l = me // low, me % low
    owners = [((h + j) % high) * low + (l ^ flip) for flip in flipped_low(low) for j in range(high)]
    rows, features = grads.shape
    depth = weights.shape[0] // (high * low)
    counts = [high] + [high << step for step in range(low.bit_length() - 1)]
    return pl.pallas_call(
        partials_kernel,
        out_shape=[jax.ShapeDtypeStruct((count, rows, depth), BF16) for count in counts],
        in_specs=[SMEM_SPEC, VMEM_SPEC, HBM_SPEC],
        out_specs=[VMEM_SPEC] * len(counts),
        scratch_shapes=[
            pltpu.VMEM((WEIGHT_SLOTS, depth, features), weights.dtype),
            pltpu.SemaphoreType.DMA((WEIGHT_SLOTS,)),
        ],
        compiler_params=pltpu.CompilerParams(vmem_limit_bytes=VMEM_LIMIT),
        cost_estimate=pl.CostEstimate(
            flops=2 * rows * features * weights.shape[0],
            bytes_accessed=2 * weights.shape[0] * (features + rows),
            transcendentals=0,
        ),
        name="grad_partials",
    )(jnp.stack(owners).astype(jnp.int32), grads, weights)


def halves(value):
    top = value.astype(BF16)
    return top, (value - top.astype(F32)).astype(BF16)


def prepare_kernel(mr_filter, short_filter, order, table, filters):
    taps, span = table.shape[1:]
    ends = lax.broadcasted_iota(jnp.int32, (taps, span), 0) + lax.broadcasted_iota(
        jnp.int32, (taps, span), 1
    )
    flip = jnp.where(ends == taps, 1.0, 0.0).astype(BF16)
    first = jnp.dot(mr_filter[...].astype(BF16), flip, preferred_element_type=F32)
    for g in range(table.shape[0]):
        spreadout = jnp.broadcast_to(first[g : g + 1, :], (taps, span))
        table[g] = pltpu.roll(spreadout, 0, 1, stride=1, stride_axis=0).astype(table.dtype)
    size = order.shape[0]
    for at in range(0, filters.shape[1], size):
        left = short_filter[:, at : at + size]
        moved = jnp.zeros(left.shape, F32)
        for _ in range(3):
            part = left.astype(BF16)
            moved = moved + jnp.dot(part, order[...], preferred_element_type=F32)
            left = left - part.astype(F32)
        filters[:, at : at + size] = moved


def prepare(mr_filter, short_filter, order):
    groups, taps = mr_filter.shape
    return pl.pallas_call(
        prepare_kernel,
        out_shape=[
            jax.ShapeDtypeStruct((groups, taps, 2 * taps), BF16),
            jax.ShapeDtypeStruct(short_filter.shape, F32),
        ],
        in_specs=[VMEM_SPEC] * 3,
        out_specs=[VMEM_SPEC] * 2,
        compiler_params=pltpu.CompilerParams(vmem_limit_bytes=SMALL_LIMIT),
        name="prepare",
    )(mr_filter, short_filter, order)


def mixing_kernel(groups, earlier, projected, order, filters, bands, skip, gated, query, mixed):
    rows = projected.shape[0]
    channels = skip.shape[1]
    taps = bands.shape[1]
    span = 2 * taps
    extended = jnp.concatenate([earlier[...].astype(F32), projected[...].astype(F32)], 0).astype(BF16)
    lines = jnp.dot(extended, order[...], preferred_element_type=F32)
    short = (
        filters[0:1, :] * lines
        + filters[1:2, :] * pltpu.roll(lines, 1, 0)
        + filters[2:3, :] * pltpu.roll(lines, 2, 0)
    )
    own_query = short[rows:, :channels]
    both = short[:, channels : 2 * channels] * short[:, 2 * channels :]
    query[...] = own_query
    mixed[...] = both
    both_top, both_rest = halves(both)
    pair = jnp.concatenate([both_top, both_rest], 1)
    lane_group = lax.broadcasted_iota(jnp.int32, (taps, channels), 1) // (channels // groups)
    first = spare = rows - taps
    whole = bands[...].reshape(groups * taps, span)
    ends = bands[:, taps - spare :, :].reshape(groups * spare, span)
    bodies = jnp.dot(whole, pair[first : first + span], preferred_element_type=F32)
    tails = jnp.dot(ends, pair[2 * first :], preferred_element_type=F32)
    bodies = bodies[:, :channels] + bodies[:, channels:]
    tails = tails[:, :channels] + tails[:, channels:]
    body, tail = bodies[:taps], tails[:spare]
    for g in range(1, groups):
        body = jnp.where(lane_group == g, bodies[g * taps : (g + 1) * taps], body)
        tail = jnp.where(lane_group[:spare] == g, tails[g * spare : (g + 1) * spare], tail)
    longconv = jnp.concatenate([body, tail], 0)
    gated[...] = (own_query * (longconv + skip[...] * both[rows:])).astype(gated.dtype)


def mixing(earlier, projected, order, filters, bands, skip, groups):
    rows, columns = projected.shape
    channels = columns // 3
    block = order.shape[0] // 3
    steps = channels // block
    per_step = groups // steps
    taps = bands.shape[1]
    ext = 2 * rows
    table = pl.BlockSpec((per_step, taps, 2 * taps), lambda i: (i, 0, 0))
    return pl.pallas_call(
        functools.partial(mixing_kernel, per_step),
        grid=(steps,),
        out_shape=[
            jax.ShapeDtypeStruct((rows, channels), BF16),
            jax.ShapeDtypeStruct((rows, channels), F32),
            jax.ShapeDtypeStruct((ext, channels), F32),
        ],
        in_specs=[
            pl.BlockSpec((rows, 3 * block), lambda i: (0, i)),
            pl.BlockSpec((rows, 3 * block), lambda i: (0, i)),
            pl.BlockSpec((3 * block, 3 * block), lambda i: (0, 0)),
            pl.BlockSpec((3, 3 * block), lambda i: (0, i)),
            table,
            pl.BlockSpec((1, block), lambda i: (0, i)),
        ],
        out_specs=[
            pl.BlockSpec((rows, block), lambda i: (0, i)),
            pl.BlockSpec((rows, block), lambda i: (0, i)),
            pl.BlockSpec((ext, block), lambda i: (0, i)),
        ],
        compiler_params=pltpu.CompilerParams(vmem_limit_bytes=SMALL_LIMIT),
        cost_estimate=pl.CostEstimate(
            flops=2 * 2 * groups * rows * 2 * taps * 2 * block,
            bytes_accessed=4 * ext * channels + 6 * ext * channels + 4 * groups * taps * taps,
            transcendentals=0,
        ),
        name="mixing",
    )(earlier, projected, order, filters, bands, skip)


def tap_grad_kernel(groups, pieces, *refs):
    grads, (query, mixed, taps_out, skip_out) = refs[:pieces], refs[pieces:]
    total = grads[0][...].astype(F32)
    for piece in grads[1:]:
        total = total + piece[...].astype(F32)
    weighted = total * query[...]
    rows, channels = weighted.shape
    taps = taps_out.shape[1]
    span = 2 * taps
    first = rows - taps
    spare = rows - taps
    both = mixed[...]
    skip_out[...] = jnp.sum(weighted * both[rows:], axis=0, keepdims=True)
    both_top = both.astype(BF16)
    flip = jnp.where(
        lax.broadcasted_iota(jnp.int32, (span, span), 0)
        + lax.broadcasted_iota(jnp.int32, (span, span), 1)
        == span - 1,
        1.0,
        0.0,
    ).astype(BF16)

    def backwards(start):
        end = jnp.dot(flip, both_top[start : start + span], preferred_element_type=F32)
        return jnp.concatenate([end.astype(BF16)] * 2, 1)

    near, far = backwards(first), backwards(2 * first)
    parts = jnp.concatenate(halves(weighted), 1)
    lane_group = (lax.broadcasted_iota(jnp.int32, (1, 2 * channels), 1) % channels) // (
        channels // groups
    )
    contract = (((1,), (1,)), ((), ()))
    masks = [jnp.where(lane_group == g, 1.0, 0.0).astype(BF16) for g in range(groups)]
    sides = jnp.concatenate([parts[:taps] * mask for mask in masks], 0)
    ends = jnp.concatenate([parts[taps:].astype(F32) * mask.astype(F32) for mask in masks], 0)
    bodies = lax.dot_general(sides, near, contract, preferred_element_type=F32)
    tails = lax.dot_general(ends.astype(BF16), far, contract, preferred_element_type=F32)
    for g in range(groups):
        body = bodies[g * taps : (g + 1) * taps]
        tail = tails[g * spare : (g + 1) * spare]
        body = jnp.concatenate([body[: taps - spare], body[taps - spare :] + tail], 0)
        skewed = pltpu.roll(body, 0, 1, stride=1, stride_axis=0)
        line = jnp.sum(skewed, axis=0, keepdims=True)
        taps_out[g : g + 1, :] = pltpu.roll(line, span - (taps - 1), 1)[:, :taps]


def tap_grad(grads, query, mixed, groups, taps):
    rows, channels = query.shape
    ext = mixed.shape[0]
    block = 128 if channels % 128 == 0 else channels
    steps = channels // block
    per_step = groups // steps
    span = 2 * taps
    one = pl.BlockSpec((rows, block), lambda i: (0, i))
    return pl.pallas_call(
        functools.partial(tap_grad_kernel, per_step, len(grads)),
        grid=(steps,),
        out_shape=[
            jax.ShapeDtypeStruct((groups, taps), F32),
            jax.ShapeDtypeStruct((1, channels), F32),
        ],
        in_specs=[one] * (len(grads) + 1) + [pl.BlockSpec((ext, block), lambda i: (0, i))],
        out_specs=[
            pl.BlockSpec((per_step, taps), lambda i: (i, 0)),
            pl.BlockSpec((1, block), lambda i: (0, i)),
        ],
        compiler_params=pltpu.CompilerParams(vmem_limit_bytes=SMALL_LIMIT),
        cost_estimate=pl.CostEstimate(
            flops=2 * groups * rows * span * 2 * block,
            bytes_accessed=4 * ext * channels + 6 * rows * channels,
            transcendentals=0,
        ),
        name="tap_grad",
    )(*grads, query, mixed)


def branch_order(block, width):
    to = np.arange(3 * block)
    branch, channel = to // block, to % block
    source = 3 * width * (channel // width) + width * branch + channel % width
    return jnp.asarray(np.arange(3 * block)[:, None] == source[None, :], BF16)


def local(tokens, w_in, short_filter, mr_filter, skip, w_out, grad_out):
    high, low = split_axis(lax.axis_size("col"))
    row_size = lax.axis_size("row")
    channels = tokens.shape[1]
    groups, taps = mr_filter.shape
    width = channels // groups
    block = 128 if channels % 128 == 0 else channels

    order = branch_order(block, width)
    gather = Gather(tokens, high, low, True)
    parts = partials(grad_out, w_out, high, low)
    gather.pass_on(parts, gather.late)
    bands, filters = prepare(*after((mr_filter, short_filter), gather.line), order)
    projected = gather.finish(w_in, BF16, "project", (bands, filters))
    earlier = lax.ppermute(projected, "row", [(r, r + 1) for r in range(row_size - 1)])
    gated, query, mixed = mixing(earlier, projected, order, filters, bands, skip[None], groups)
    parts = after(parts, gather.total)
    gather = Gather(gated, high, low, True)

    parts = list(parts)
    for step in reversed(range(low.bit_length() - 1)):
        moved = after(swap_low(parts.pop(), high, low, step), gated)
        at = 0
        for i, part in enumerate(parts):
            count = part.shape[0]
            total = part.astype(F32) + moved[at : at + count].astype(F32)
            parts[i], at = total.astype(BF16), at + count
    sums = after([parts[0][j] for j in range(high)], gather.near)
    gather.pass_on(gather.late, sums)
    grads = [sums[0]] + [shift_high(sums[j], high, low, j) for j in range(1, high)]
    block_out = gather.finish(w_out, BF16, "output", (grads[1:2],))
    grads = after(grads, gather.far[1])

    tap_part, skip_part = tap_grad(grads, query, mixed, groups, taps)
    if row_size == 2:
        swap = [(0, 1), (1, 0)]
        filter_grad = tap_part + lax.ppermute(tap_part, "row", swap)
        skip_grad = (skip_part + lax.ppermute(skip_part, "row", swap)).reshape(-1)
    else:
        filter_grad, skip_grad = lax.psum((tap_part, skip_part.reshape(-1)), "row")
    return (block_out, filter_grad, skip_grad)


def solution(mesh):
    in_specs = (
        P("row", "col"),
        P(None, "col"),
        P(None, "col"),
        P("col", None),
        P("col"),
        P(None, "col"),
        P("row", "col"),
    )
    out_specs = (P("row", "col"), P("col", None), P("col"))
    return jax.shard_map(local, mesh=mesh, in_specs=in_specs, out_specs=out_specs, check_vma=False)
```

```python
import functools

import jax
import jax.numpy as jnp
import numpy as np
from jax import lax
from jax.experimental import pallas as pl
from jax.experimental.pallas import tpu as pltpu
from jax.sharding import PartitionSpec as P

F32 = jnp.float32
BF16 = jnp.bfloat16
VMEM_SPEC = pl.BlockSpec(memory_space=pltpu.VMEM)
SMEM_SPEC = pl.BlockSpec(memory_space=pltpu.SMEM)
HBM_SPEC = pl.BlockSpec(memory_space=pltpu.HBM)
WEIGHT_SLOTS = 4
VMEM_LIMIT = 47 * 2**20
SMALL_LIMIT = 16 * 2**20


def split_axis(size):
    low = 1
    while low * low < size and size % (low * 2) == 0:
        low *= 2
    return size // low, low


def low_masks(low, parity):
    bits = [1 << i for i in range(low.bit_length() - 1)]
    return bits[::-1] if parity else bits


def swap_low(block, high, low, step):
    rows = lax.axis_size("row")
    size = high * low
    route = []
    for r in range(rows):
        mask = low_masks(low, r % 2)[step]
        route += [(r * size + c, r * size + (c ^ mask)) for c in range(size)]
    return lax.ppermute(block, ("row", "col"), route)


def shift_high(block, high, low, k):
    route = [(h * low + l, ((h + k) % high) * low + l) for h in range(high) for l in range(low)]
    return lax.ppermute(block, "col", route)


def flipped_low(low):
    parity = lax.axis_index("row") % 2
    forward, backward = low_masks(low, 0), low_masks(low, 1)
    flips = [0]
    for one, other in zip(forward, backward):
        mask = jnp.where(parity == 0, one, other)
        flips += [flip + mask for flip in flips]
    return flips


def after(values, *others):
    return lax.optimization_barrier((values, others))[0]


class Gather:
    def __init__(self, block, high, low, apart):
        self.high, self.low, self.block = high, low, block
        self.bits = low.bit_length() - 1
        shifts = list(range(1, high))
        self.shifts = shifts
        self.line = [shift_high(block, high, low, k) for k in shifts]
        self.near, self.late = [], []
        if apart:
            items = self.plane([block], self.bits - 1)
            self.near = items[1:]
            items = after(items, self.near)
            self.late = [swap_low(each, high, low, self.bits - 1) for each in items]

    def plane(self, items, steps):
        for step in range(steps):
            items = items + [swap_low(each, self.high, self.low, step) for each in items]
        return items

    def pass_on(self, *others):
        self.line = after(self.line, self.near, others)
        blocks = self.line if self.late else [self.block, *self.line]
        self.far = self.plane([jnp.stack(blocks)], self.bits - 1)

    def finish(self, weights, out_type, name, before_hop=()):
        high, low = self.high, self.low
        me = lax.axis_index("col")
        h, l = me // low, me % low
        flips = flipped_low(low)
        from_high = [(h - k + high) % high for k in self.shifts]
        small = weights.size < 2**23
        limit = VMEM_LIMIT if small else 34 * 2**20

        owners = [h * low + (l ^ flip) for flip in flips]
        own = 1 + len(self.near)
        owners, late_owners = owners[:own], owners[own:]
        owners += [f * low + l for f in from_high]
        pieces = [self.block, *self.near, *self.line]
        total, = accumulate(None, pieces, owners, weights, None, F32, 0, limit, name + "_0")
        hop = after(self.far, total, before_hop)
        last = [swap_low(each, high, low, self.bits - 1) for each in hop]
        self.last = last
        if not self.late:
            late_owners, from_high = [], [h, *from_high]
        owners = late_owners + [f * low + (l ^ flip) for flip in flips[1:] for f in from_high]
        final = len(last) * len(from_high)
        loads = final if small else 0
        pieces = [*self.late, *self.far[1:]]
        total, *ahead = accumulate(
            total, pieces, owners, weights, None, F32, loads, limit, name + "_1"
        )
        ahead = ahead[0] if loads else None
        self.total = total
        owners = owners[len(owners) - final :]
        return accumulate(total, last, owners, weights, ahead, out_type, 0, limit, name + "_2")[0]


def accumulate_kernel(counts, has_total, ready, loads, width, owners, *refs):
    refs = list(refs)
    pieces = [refs.pop(0) for _ in counts]
    total = refs.pop(0) if has_total else None
    here = refs.pop(0) if ready else None
    weights, out = refs[:2]
    refs = refs[2:]
    ahead = refs.pop(0) if loads else None
    sums, held, sems, ahead_sems = refs
    order = [(p, i) for p, count in enumerate(counts) for i in range(count or 1)]
    depth = held.shape[1]

    def rows_of(step):
        return weights.at[pl.ds(pl.multiple_of(owners[step] * depth, depth), depth), :]

    def fetch(step):
        slot = step % WEIGHT_SLOTS
        return pltpu.make_async_copy(rows_of(step), held.at[slot], sems.at[slot])

    def load(at):
        return pltpu.make_async_copy(rows_of(len(order) + at), ahead.at[at], ahead_sems.at[at])

    for step in range(ready, min(ready + WEIGHT_SLOTS, len(order))):
        fetch(step).start()
    for step, (p, i) in enumerate(order):
        if step >= ready:
            fetch(step).wait()
        slot = step % WEIGHT_SLOTS
        rows = pieces[p][i] if counts[p] else pieces[p][...]
        for at in range(0, out.shape[1], width):
            cols = slice(at, at + width)
            part = here[step, :, cols] if step < ready else held[slot, :, cols]
            term = jnp.dot(rows, part, preferred_element_type=F32)
            if step == 0 and total is not None:
                term = term + total[:, cols]
            if step:
                term = term + sums[:, cols]
            if step + 1 == len(order):
                out[:, cols] = term.astype(out.dtype)
            else:
                sums[:, cols] = term
        if step >= ready and step + WEIGHT_SLOTS < len(order):
            fetch(step + WEIGHT_SLOTS).start()
        if step == max(0, len(order) - 1 - WEIGHT_SLOTS):
            for at in range(loads):
                load(at).start()
    for at in range(loads):
        load(at).wait()


def accumulate(total, pieces, owners, weights, here, out_type, loads, limit, name):
    counts = tuple(0 if piece.ndim == 2 else piece.shape[0] for piece in pieces)
    rows, depth = pieces[0].shape[-2:]
    columns = weights.shape[-1]
    width = next(w for w in (512, 256, 128, columns) if columns % w == 0)
    steps = sum(count or 1 for count in counts)
    ready = 0 if here is None else here.shape[0]
    operands = [jnp.stack(owners).astype(jnp.int32), *pieces]
    operands += [extra for extra in (total, here) if extra is not None]
    out_shape = [jax.ShapeDtypeStruct((rows, columns), out_type)]
    if loads:
        out_shape.append(jax.ShapeDtypeStruct((loads, depth, columns), weights.dtype))
    return pl.pallas_call(
        functools.partial(accumulate_kernel, counts, total is not None, ready, loads, width),
        out_shape=out_shape,
        in_specs=[SMEM_SPEC] + [VMEM_SPEC] * (len(operands) - 1) + [HBM_SPEC],
        out_specs=[VMEM_SPEC] * len(out_shape),
        scratch_shapes=[
            pltpu.VMEM((rows, columns), F32),
            pltpu.VMEM((WEIGHT_SLOTS, depth, columns), weights.dtype),
            pltpu.SemaphoreType.DMA((WEIGHT_SLOTS,)),
            pltpu.SemaphoreType.DMA((max(1, loads),)),
        ],
        compiler_params=pltpu.CompilerParams(vmem_limit_bytes=limit),
        cost_estimate=pl.CostEstimate(
            flops=2 * steps * rows * depth * columns,
            bytes_accessed=(steps + loads) * depth * columns * 2 + rows * columns * 8,
            transcendentals=0,
        ),
        name=name,
    )(*operands, weights)


def partials_kernel(owners, grads, weights, *refs):
    outs, (held, sems) = refs[:-2], refs[-2:]
    order = [(o, i) for o, out in enumerate(outs) for i in range(out.shape[0])]
    depth = held.shape[1]

    def fetch(step):
        start = pl.multiple_of(owners[step] * depth, depth)
        slot = step % WEIGHT_SLOTS
        return pltpu.make_async_copy(
            weights.at[pl.ds(start, depth), :], held.at[slot], sems.at[slot]
        )

    for step in range(min(WEIGHT_SLOTS, len(order))):
        fetch(step).start()
    for step, (o, i) in enumerate(order):
        fetch(step).wait()
        term = lax.dot_general(
            grads[...],
            held[step % WEIGHT_SLOTS],
            (((1,), (1,)), ((), ())),
            preferred_element_type=F32,
        )
        outs[o][i] = term.astype(outs[o].dtype)
        if step + WEIGHT_SLOTS < len(order):
            fetch(step + WEIGHT_SLOTS).start()


def partials(grads, weights, high, low):
    me = lax.axis_index("col")
    h, l = me // low, me % low
    owners = [((h + j) % high) * low + (l ^ flip) for flip in flipped_low(low) for j in range(high)]
    rows, features = grads.shape
    depth = weights.shape[0] // (high * low)
    counts = [high] + [high << step for step in range(low.bit_length() - 1)]
    return pl.pallas_call(
        partials_kernel,
        out_shape=[jax.ShapeDtypeStruct((count, rows, depth), BF16) for count in counts],
        in_specs=[SMEM_SPEC, VMEM_SPEC, HBM_SPEC],
        out_specs=[VMEM_SPEC] * len(counts),
        scratch_shapes=[
            pltpu.VMEM((WEIGHT_SLOTS, depth, features), weights.dtype),
            pltpu.SemaphoreType.DMA((WEIGHT_SLOTS,)),
        ],
        compiler_params=pltpu.CompilerParams(vmem_limit_bytes=VMEM_LIMIT),
        cost_estimate=pl.CostEstimate(
            flops=2 * rows * features * weights.shape[0],
            bytes_accessed=2 * weights.shape[0] * (features + rows),
            transcendentals=0,
        ),
        name="grad_partials",
    )(jnp.stack(owners).astype(jnp.int32), grads, weights)


def halves(value):
    top = value.astype(BF16)
    return top, (value - top.astype(F32)).astype(BF16)


def prepare_kernel(mr_filter, short_filter, order, table, filters):
    taps, span = table.shape[1:]
    ends = lax.broadcasted_iota(jnp.int32, (taps, span), 0) + lax.broadcasted_iota(
        jnp.int32, (taps, span), 1
    )
    flip = jnp.where(ends == taps, 1.0, 0.0).astype(BF16)
    first = jnp.dot(mr_filter[...].astype(BF16), flip, preferred_element_type=F32)
    for g in range(table.shape[0]):
        spreadout = jnp.broadcast_to(first[g : g + 1, :], (taps, span))
        table[g] = pltpu.roll(spreadout, 0, 1, stride=1, stride_axis=0).astype(table.dtype)
    size = order.shape[0]
    for at in range(0, filters.shape[1], size):
        left = short_filter[:, at : at + size]
        moved = jnp.zeros(left.shape, F32)
        for _ in range(3):
            part = left.astype(BF16)
            moved = moved + jnp.dot(part, order[...], preferred_element_type=F32)
            left = left - part.astype(F32)
        filters[:, at : at + size] = moved


def prepare(mr_filter, short_filter, order):
    groups, taps = mr_filter.shape
    return pl.pallas_call(
        prepare_kernel,
        out_shape=[
            jax.ShapeDtypeStruct((groups, taps, 2 * taps), BF16),
            jax.ShapeDtypeStruct(short_filter.shape, F32),
        ],
        in_specs=[VMEM_SPEC] * 3,
        out_specs=[VMEM_SPEC] * 2,
        compiler_params=pltpu.CompilerParams(vmem_limit_bytes=SMALL_LIMIT),
        name="prepare",
    )(mr_filter, short_filter, order)


def mixing_kernel(groups, earlier, projected, order, filters, bands, skip, gated, query, mixed):
    rows = projected.shape[0]
    channels = skip.shape[1]
    taps = bands.shape[1]
    span = 2 * taps
    extended = jnp.concatenate([earlier[...].astype(F32), projected[...].astype(F32)], 0).astype(BF16)
    lines = jnp.dot(extended, order[...], preferred_element_type=F32)
    short = (
        filters[0:1, :] * lines
        + filters[1:2, :] * pltpu.roll(lines, 1, 0)
        + filters[2:3, :] * pltpu.roll(lines, 2, 0)
    )
    own_query = short[rows:, :channels]
    both = short[:, channels : 2 * channels] * short[:, 2 * channels :]
    query[...] = own_query
    mixed[...] = both
    both_top, both_rest = halves(both)
    pair = jnp.concatenate([both_top, both_rest], 1)
    lane_group = lax.broadcasted_iota(jnp.int32, (taps, channels), 1) // (channels // groups)
    first = spare = rows - taps
    whole = bands[...].reshape(groups * taps, span)
    ends = bands[:, taps - spare :, :].reshape(groups * spare, span)
    bodies = jnp.dot(whole, pair[first : first + span], preferred_element_type=F32)
    tails = jnp.dot(ends, pair[2 * first :], preferred_element_type=F32)
    bodies = bodies[:, :channels] + bodies[:, channels:]
    tails = tails[:, :channels] + tails[:, channels:]
    body, tail = bodies[:taps], tails[:spare]
    for g in range(1, groups):
        body = jnp.where(lane_group == g, bodies[g * taps : (g + 1) * taps], body)
        tail = jnp.where(lane_group[:spare] == g, tails[g * spare : (g + 1) * spare], tail)
    longconv = jnp.concatenate([body, tail], 0)
    gated[...] = (own_query * (longconv + skip[...] * both[rows:])).astype(gated.dtype)


def mixing(earlier, projected, order, filters, bands, skip, groups):
    rows, columns = projected.shape
    channels = columns // 3
    block = order.shape[0] // 3
    steps = channels // block
    per_step = groups // steps
    taps = bands.shape[1]
    ext = 2 * rows
    table = pl.BlockSpec((per_step, taps, 2 * taps), lambda i: (i, 0, 0))
    return pl.pallas_call(
        functools.partial(mixing_kernel, per_step),
        grid=(steps,),
        out_shape=[
            jax.ShapeDtypeStruct((rows, channels), BF16),
            jax.ShapeDtypeStruct((rows, channels), F32),
            jax.ShapeDtypeStruct((ext, channels), F32),
        ],
        in_specs=[
            pl.BlockSpec((rows, 3 * block), lambda i: (0, i)),
            pl.BlockSpec((rows, 3 * block), lambda i: (0, i)),
            pl.BlockSpec((3 * block, 3 * block), lambda i: (0, 0)),
            pl.BlockSpec((3, 3 * block), lambda i: (0, i)),
            table,
            pl.BlockSpec((1, block), lambda i: (0, i)),
        ],
        out_specs=[
            pl.BlockSpec((rows, block), lambda i: (0, i)),
            pl.BlockSpec((rows, block), lambda i: (0, i)),
            pl.BlockSpec((ext, block), lambda i: (0, i)),
        ],
        compiler_params=pltpu.CompilerParams(vmem_limit_bytes=SMALL_LIMIT),
        cost_estimate=pl.CostEstimate(
            flops=2 * 2 * groups * rows * 2 * taps * 2 * block,
            bytes_accessed=4 * ext * channels + 6 * ext * channels + 4 * groups * taps * taps,
            transcendentals=0,
        ),
        name="mixing",
    )(earlier, projected, order, filters, bands, skip)


def tap_grad_kernel(groups, pieces, *refs):
    grads, (query, mixed, taps_out, skip_out) = refs[:pieces], refs[pieces:]
    total = grads[0][...].astype(F32)
    for piece in grads[1:]:
        total = total + piece[...].astype(F32)
    weighted = total * query[...]
    rows, channels = weighted.shape
    taps = taps_out.shape[1]
    span = 2 * taps
    first = rows - taps
    spare = rows - taps
    both = mixed[...]
    skip_out[...] = jnp.sum(weighted * both[rows:], axis=0, keepdims=True)
    both_top = both.astype(BF16)
    flip = jnp.where(
        lax.broadcasted_iota(jnp.int32, (span, span), 0)
        + lax.broadcasted_iota(jnp.int32, (span, span), 1)
        == span - 1,
        1.0,
        0.0,
    ).astype(BF16)

    def backwards(start):
        end = jnp.dot(flip, both_top[start : start + span], preferred_element_type=F32)
        return jnp.concatenate([end.astype(BF16)] * 2, 1)

    near, far = backwards(first), backwards(2 * first)
    parts = jnp.concatenate(halves(weighted), 1)
    lane_group = (lax.broadcasted_iota(jnp.int32, (1, 2 * channels), 1) % channels) // (
        channels // groups
    )
    contract = (((1,), (1,)), ((), ()))
    masks = [jnp.where(lane_group == g, 1.0, 0.0).astype(BF16) for g in range(groups)]
    sides = jnp.concatenate([parts[:taps] * mask for mask in masks], 0)
    ends = jnp.concatenate([parts[taps:].astype(F32) * mask.astype(F32) for mask in masks], 0)
    bodies = lax.dot_general(sides, near, contract, preferred_element_type=F32)
    tails = lax.dot_general(ends.astype(BF16), far, contract, preferred_element_type=F32)
    for g in range(groups):
        body = bodies[g * taps : (g + 1) * taps]
        tail = tails[g * spare : (g + 1) * spare]
        body = jnp.concatenate([body[: taps - spare], body[taps - spare :] + tail], 0)
        skewed = pltpu.roll(body, 0, 1, stride=1, stride_axis=0)
        line = jnp.sum(skewed, axis=0, keepdims=True)
        taps_out[g : g + 1, :] = pltpu.roll(line, span - (taps - 1), 1)[:, :taps]


def tap_grad(grads, query, mixed, groups, taps):
    rows, channels = query.shape
    ext = mixed.shape[0]
    block = 128 if channels % 128 == 0 else channels
    steps = channels // block
    per_step = groups // steps
    span = 2 * taps
    one = pl.BlockSpec((rows, block), lambda i: (0, i))
    return pl.pallas_call(
        functools.partial(tap_grad_kernel, per_step, len(grads)),
        grid=(steps,),
        out_shape=[
            jax.ShapeDtypeStruct((groups, taps), F32),
            jax.ShapeDtypeStruct((1, channels), F32),
        ],
        in_specs=[one] * (len(grads) + 1) + [pl.BlockSpec((ext, block), lambda i: (0, i))],
        out_specs=[
            pl.BlockSpec((per_step, taps), lambda i: (i, 0)),
            pl.BlockSpec((1, block), lambda i: (0, i)),
        ],
        compiler_params=pltpu.CompilerParams(vmem_limit_bytes=SMALL_LIMIT),
        cost_estimate=pl.CostEstimate(
            flops=2 * groups * rows * span * 2 * block,
            bytes_accessed=4 * ext * channels + 6 * rows * channels,
            transcendentals=0,
        ),
        name="tap_grad",
    )(*grads, query, mixed)


def branch_order(block, width):
    to = np.arange(3 * block)
    branch, channel = to // block, to % block
    source = 3 * width * (channel // width) + width * branch + channel % width
    return jnp.asarray(np.arange(3 * block)[:, None] == source[None, :], BF16)


def local(tokens, w_in, short_filter, mr_filter, skip, w_out, grad_out):
    high, low = split_axis(lax.axis_size("col"))
    row_size = lax.axis_size("row")
    channels = tokens.shape[1]
    groups, taps = mr_filter.shape
    width = channels // groups
    block = 128 if channels % 128 == 0 else channels

    order = branch_order(block, width)
    gather = Gather(tokens, high, low, True)
    parts = partials(grad_out, w_out, high, low)
    gather.pass_on(parts, gather.late)
    bands, filters = prepare(*after((mr_filter, short_filter), gather.line), order)
    gather.line = after(gather.line, bands, filters)
    projected = gather.finish(w_in, BF16, "project")
    earlier = lax.ppermute(projected, "row", [(r, r + 1) for r in range(row_size - 1)])
    gated, query, mixed = mixing(earlier, projected, order, filters, bands, skip[None], groups)
    parts = after(parts, gather.total)
    gather = Gather(gated, high, low, True)

    parts = list(parts)
    for step in reversed(range(low.bit_length() - 1)):
        moved = after(swap_low(parts.pop(), high, low, step), gather.near)
        at = 0
        for i, part in enumerate(parts):
            count = part.shape[0]
            total = part.astype(F32) + moved[at : at + count].astype(F32)
            parts[i], at = total.astype(BF16), at + count
    gather.pass_on(gather.late)
    sums = after([parts[0][j] for j in range(high)], gather.line)
    grads = [sums[0]] + [shift_high(sums[j], high, low, j) for j in range(1, high)]
    block_out = gather.finish(w_out, BF16, "output", ())
    grads = after(grads, gather.total)

    tap_part, skip_part = tap_grad(grads, query, mixed, groups, taps)
    if row_size == 2:
        swap = [(0, 1), (1, 0)]
        filter_grad = tap_part + lax.ppermute(tap_part, "row", swap)
        skip_grad = (skip_part + lax.ppermute(skip_part, "row", swap)).reshape(-1)
    else:
        filter_grad, skip_grad = lax.psum((tap_part, skip_part.reshape(-1)), "row")
    return (block_out, filter_grad, skip_grad)


def solution(mesh):
    in_specs = (
        P("row", "col"),
        P(None, "col"),
        P(None, "col"),
        P("col", None),
        P("col"),
        P(None, "col"),
        P("row", "col"),
    )
    out_specs = (P("row", "col"), P("col", None), P("col"))
    return jax.shard_map(local, mesh=mesh, in_specs=in_specs, out_specs=out_specs, check_vma=False)
```

```python
import functools

import jax
import jax.numpy as jnp
import numpy as np
from jax import lax
from jax.experimental import pallas as pl
from jax.experimental.pallas import tpu as pltpu
from jax.sharding import PartitionSpec as P

F32 = jnp.float32
BF16 = jnp.bfloat16
VMEM_SPEC = pl.BlockSpec(memory_space=pltpu.VMEM)
SMEM_SPEC = pl.BlockSpec(memory_space=pltpu.SMEM)
HBM_SPEC = pl.BlockSpec(memory_space=pltpu.HBM)
WEIGHT_SLOTS = 4
VMEM_LIMIT = 47 * 2**20
SMALL_LIMIT = 16 * 2**20


def split_axis(size):
    low = 1
    while low * low < size and size % (low * 2) == 0:
        low *= 2
    return size // low, low


def low_masks(low, parity):
    bits = [1 << i for i in range(low.bit_length() - 1)]
    return bits[::-1] if parity else bits


def swap_low(block, high, low, step):
    rows = lax.axis_size("row")
    size = high * low
    route = []
    for r in range(rows):
        mask = low_masks(low, r % 2)[step]
        route += [(r * size + c, r * size + (c ^ mask)) for c in range(size)]
    return lax.ppermute(block, ("row", "col"), route)


def shift_high(block, high, low, k):
    route = [(h * low + l, ((h + k) % high) * low + l) for h in range(high) for l in range(low)]
    return lax.ppermute(block, "col", route)


def flipped_low(low):
    parity = lax.axis_index("row") % 2
    forward, backward = low_masks(low, 0), low_masks(low, 1)
    flips = [0]
    for one, other in zip(forward, backward):
        mask = jnp.where(parity == 0, one, other)
        flips += [flip + mask for flip in flips]
    return flips


def after(values, *others):
    return lax.optimization_barrier((values, others))[0]


class Gather:
    def __init__(self, block, high, low, apart):
        self.high, self.low, self.block = high, low, block
        self.bits = low.bit_length() - 1
        shifts = list(range(1, high))
        self.shifts = shifts
        self.line = [shift_high(block, high, low, k) for k in shifts]
        self.near, self.late = [], []
        if apart:
            items = self.plane([block], self.bits - 1)
            self.near = items[1:]
            items = after(items, self.near)
            self.late = [swap_low(each, high, low, self.bits - 1) for each in items]

    def plane(self, items, steps):
        for step in range(steps):
            items = items + [swap_low(each, self.high, self.low, step) for each in items]
        return items

    def pass_on(self, *others):
        self.line = after(self.line, self.near, others)
        blocks = self.line if self.late else [self.block, *self.line]
        self.far = self.plane([jnp.stack(blocks)], self.bits - 1)

    def finish(self, weights, out_type, name, before_hop=()):
        high, low = self.high, self.low
        me = lax.axis_index("col")
        h, l = me // low, me % low
        flips = flipped_low(low)
        from_high = [(h - k + high) % high for k in self.shifts]
        small = weights.size < 2**23
        limit = VMEM_LIMIT if small else 34 * 2**20

        owners = [h * low + (l ^ flip) for flip in flips]
        own = 1 + len(self.near)
        owners, late_owners = owners[:own], owners[own:]
        owners += [f * low + l for f in from_high]
        pieces = [self.block, *self.near, *self.line]
        total, = accumulate(None, pieces, owners, weights, None, F32, 0, limit, name + "_0")
        hop = after(self.far, total, before_hop)
        last = [swap_low(each, high, low, self.bits - 1) for each in hop]
        self.last = last
        if not self.late:
            late_owners, from_high = [], [h, *from_high]
        owners = late_owners + [f * low + (l ^ flip) for flip in flips[1:] for f in from_high]
        final = len(last) * len(from_high)
        loads = final if small else 0
        pieces = [*self.late, *self.far[1:]]
        total, *ahead = accumulate(
            total, pieces, owners, weights, None, F32, loads, limit, name + "_1"
        )
        ahead = ahead[0] if loads else None
        self.total = total
        owners = owners[len(owners) - final :]
        return accumulate(total, last, owners, weights, ahead, out_type, 0, limit, name + "_2")[0]


def accumulate_kernel(counts, has_total, ready, loads, width, owners, *refs):
    refs = list(refs)
    pieces = [refs.pop(0) for _ in counts]
    total = refs.pop(0) if has_total else None
    here = refs.pop(0) if ready else None
    weights, out = refs[:2]
    refs = refs[2:]
    ahead = refs.pop(0) if loads else None
    sums, held, sems, ahead_sems = refs
    order = [(p, i) for p, count in enumerate(counts) for i in range(count or 1)]
    depth = held.shape[1]

    def rows_of(step):
        return weights.at[pl.ds(pl.multiple_of(owners[step] * depth, depth), depth), :]

    def fetch(step):
        slot = step % WEIGHT_SLOTS
        return pltpu.make_async_copy(rows_of(step), held.at[slot], sems.at[slot])

    def load(at):
        return pltpu.make_async_copy(rows_of(len(order) + at), ahead.at[at], ahead_sems.at[at])

    for step in range(ready, min(ready + WEIGHT_SLOTS, len(order))):
        fetch(step).start()
    for step, (p, i) in enumerate(order):
        if step >= ready:
            fetch(step).wait()
        slot = step % WEIGHT_SLOTS
        rows = pieces[p][i] if counts[p] else pieces[p][...]
        for at in range(0, out.shape[1], width):
            cols = slice(at, at + width)
            part = here[step, :, cols] if step < ready else held[slot, :, cols]
            term = jnp.dot(rows, part, preferred_element_type=F32)
            if step == 0 and total is not None:
                term = term + total[:, cols]
            if step:
                term = term + sums[:, cols]
            if step + 1 == len(order):
                out[:, cols] = term.astype(out.dtype)
            else:
                sums[:, cols] = term
        if step >= ready and step + WEIGHT_SLOTS < len(order):
            fetch(step + WEIGHT_SLOTS).start()
        if step == max(0, len(order) - 1 - WEIGHT_SLOTS):
            for at in range(loads):
                load(at).start()
    for at in range(loads):
        load(at).wait()


def accumulate(total, pieces, owners, weights, here, out_type, loads, limit, name):
    counts = tuple(0 if piece.ndim == 2 else piece.shape[0] for piece in pieces)
    rows, depth = pieces[0].shape[-2:]
    columns = weights.shape[-1]
    width = next(w for w in (512, 256, 128, columns) if columns % w == 0)
    steps = sum(count or 1 for count in counts)
    ready = 0 if here is None else here.shape[0]
    operands = [jnp.stack(owners).astype(jnp.int32), *pieces]
    operands += [extra for extra in (total, here) if extra is not None]
    out_shape = [jax.ShapeDtypeStruct((rows, columns), out_type)]
    if loads:
        out_shape.append(jax.ShapeDtypeStruct((loads, depth, columns), weights.dtype))
    return pl.pallas_call(
        functools.partial(accumulate_kernel, counts, total is not None, ready, loads, width),
        out_shape=out_shape,
        in_specs=[SMEM_SPEC] + [VMEM_SPEC] * (len(operands) - 1) + [HBM_SPEC],
        out_specs=[VMEM_SPEC] * len(out_shape),
        scratch_shapes=[
            pltpu.VMEM((rows, columns), F32),
            pltpu.VMEM((WEIGHT_SLOTS, depth, columns), weights.dtype),
            pltpu.SemaphoreType.DMA((WEIGHT_SLOTS,)),
            pltpu.SemaphoreType.DMA((max(1, loads),)),
        ],
        compiler_params=pltpu.CompilerParams(vmem_limit_bytes=limit),
        cost_estimate=pl.CostEstimate(
            flops=2 * steps * rows * depth * columns,
            bytes_accessed=(steps + loads) * depth * columns * 2 + rows * columns * 8,
            transcendentals=0,
        ),
        name=name,
    )(*operands, weights)


def partials_kernel(owners, grads, weights, *refs):
    outs, (held, sems) = refs[:-2], refs[-2:]
    order = [(o, i) for o, out in enumerate(outs) for i in range(out.shape[0])]
    depth = held.shape[1]

    def fetch(step):
        start = pl.multiple_of(owners[step] * depth, depth)
        slot = step % WEIGHT_SLOTS
        return pltpu.make_async_copy(
            weights.at[pl.ds(start, depth), :], held.at[slot], sems.at[slot]
        )

    for step in range(min(WEIGHT_SLOTS, len(order))):
        fetch(step).start()
    for step, (o, i) in enumerate(order):
        fetch(step).wait()
        term = lax.dot_general(
            grads[...],
            held[step % WEIGHT_SLOTS],
            (((1,), (1,)), ((), ())),
            preferred_element_type=F32,
        )
        outs[o][i] = term.astype(outs[o].dtype)
        if step + WEIGHT_SLOTS < len(order):
            fetch(step + WEIGHT_SLOTS).start()


def partials(grads, weights, high, low):
    me = lax.axis_index("col")
    h, l = me // low, me % low
    owners = [((h + j) % high) * low + (l ^ flip) for flip in flipped_low(low) for j in range(high)]
    rows, features = grads.shape
    depth = weights.shape[0] // (high * low)
    counts = [high] + [high << step for step in range(low.bit_length() - 1)]
    return pl.pallas_call(
        partials_kernel,
        out_shape=[jax.ShapeDtypeStruct((count, rows, depth), BF16) for count in counts],
        in_specs=[SMEM_SPEC, VMEM_SPEC, HBM_SPEC],
        out_specs=[VMEM_SPEC] * len(counts),
        scratch_shapes=[
            pltpu.VMEM((WEIGHT_SLOTS, depth, features), weights.dtype),
            pltpu.SemaphoreType.DMA((WEIGHT_SLOTS,)),
        ],
        compiler_params=pltpu.CompilerParams(vmem_limit_bytes=VMEM_LIMIT),
        cost_estimate=pl.CostEstimate(
            flops=2 * rows * features * weights.shape[0],
            bytes_accessed=2 * weights.shape[0] * (features + rows),
            transcendentals=0,
        ),
        name="grad_partials",
    )(jnp.stack(owners).astype(jnp.int32), grads, weights)


def halves(value):
    top = value.astype(BF16)
    return top, (value - top.astype(F32)).astype(BF16)


def prepare_kernel(mr_filter, short_filter, order, table, filters):
    taps, span = table.shape[1:]
    ends = lax.broadcasted_iota(jnp.int32, (taps, span), 0) + lax.broadcasted_iota(
        jnp.int32, (taps, span), 1
    )
    flip = jnp.where(ends == taps, 1.0, 0.0).astype(BF16)
    first = jnp.dot(mr_filter[...].astype(BF16), flip, preferred_element_type=F32)
    for g in range(table.shape[0]):
        spreadout = jnp.broadcast_to(first[g : g + 1, :], (taps, span))
        table[g] = pltpu.roll(spreadout, 0, 1, stride=1, stride_axis=0).astype(table.dtype)
    size = order.shape[0]
    for at in range(0, filters.shape[1], size):
        left = short_filter[:, at : at + size]
        moved = jnp.zeros(left.shape, F32)
        for _ in range(3):
            part = left.astype(BF16)
            moved = moved + jnp.dot(part, order[...], preferred_element_type=F32)
            left = left - part.astype(F32)
        filters[:, at : at + size] = moved


def prepare(mr_filter, short_filter, order):
    groups, taps = mr_filter.shape
    return pl.pallas_call(
        prepare_kernel,
        out_shape=[
            jax.ShapeDtypeStruct((groups, taps, 2 * taps), BF16),
            jax.ShapeDtypeStruct(short_filter.shape, F32),
        ],
        in_specs=[VMEM_SPEC] * 3,
        out_specs=[VMEM_SPEC] * 2,
        compiler_params=pltpu.CompilerParams(vmem_limit_bytes=SMALL_LIMIT),
        name="prepare",
    )(mr_filter, short_filter, order)


def mixing_kernel(groups, earlier, projected, order, filters, bands, skip, gated, query, mixed):
    rows = projected.shape[0]
    channels = skip.shape[1]
    taps = bands.shape[1]
    span = 2 * taps
    extended = jnp.concatenate([earlier[...].astype(F32), projected[...].astype(F32)], 0).astype(BF16)
    lines = jnp.dot(extended, order[...], preferred_element_type=F32)
    short = (
        filters[0:1, :] * lines
        + filters[1:2, :] * pltpu.roll(lines, 1, 0)
        + filters[2:3, :] * pltpu.roll(lines, 2, 0)
    )
    own_query = short[rows:, :channels]
    both = short[:, channels : 2 * channels] * short[:, 2 * channels :]
    query[...] = own_query
    mixed[...] = both
    both_top, both_rest = halves(both)
    pair = jnp.concatenate([both_top, both_rest], 1)
    lane_group = lax.broadcasted_iota(jnp.int32, (taps, channels), 1) // (channels // groups)
    first = spare = rows - taps
    whole = bands[...].reshape(groups * taps, span)
    ends = bands[:, taps - spare :, :].reshape(groups * spare, span)
    bodies = jnp.dot(whole, pair[first : first + span], preferred_element_type=F32)
    tails = jnp.dot(ends, pair[2 * first :], preferred_element_type=F32)
    bodies = bodies[:, :channels] + bodies[:, channels:]
    tails = tails[:, :channels] + tails[:, channels:]
    body, tail = bodies[:taps], tails[:spare]
    for g in range(1, groups):
        body = jnp.where(lane_group == g, bodies[g * taps : (g + 1) * taps], body)
        tail = jnp.where(lane_group[:spare] == g, tails[g * spare : (g + 1) * spare], tail)
    longconv = jnp.concatenate([body, tail], 0)
    gated[...] = (own_query * (longconv + skip[...] * both[rows:])).astype(gated.dtype)


def mixing(earlier, projected, order, filters, bands, skip, groups):
    rows, columns = projected.shape
    channels = columns // 3
    block = order.shape[0] // 3
    steps = channels // block
    per_step = groups // steps
    taps = bands.shape[1]
    ext = 2 * rows
    table = pl.BlockSpec((per_step, taps, 2 * taps), lambda i: (i, 0, 0))
    return pl.pallas_call(
        functools.partial(mixing_kernel, per_step),
        grid=(steps,),
        out_shape=[
            jax.ShapeDtypeStruct((rows, channels), BF16),
            jax.ShapeDtypeStruct((rows, channels), F32),
            jax.ShapeDtypeStruct((ext, channels), F32),
        ],
        in_specs=[
            pl.BlockSpec((rows, 3 * block), lambda i: (0, i)),
            pl.BlockSpec((rows, 3 * block), lambda i: (0, i)),
            pl.BlockSpec((3 * block, 3 * block), lambda i: (0, 0)),
            pl.BlockSpec((3, 3 * block), lambda i: (0, i)),
            table,
            pl.BlockSpec((1, block), lambda i: (0, i)),
        ],
        out_specs=[
            pl.BlockSpec((rows, block), lambda i: (0, i)),
            pl.BlockSpec((rows, block), lambda i: (0, i)),
            pl.BlockSpec((ext, block), lambda i: (0, i)),
        ],
        compiler_params=pltpu.CompilerParams(vmem_limit_bytes=SMALL_LIMIT),
        cost_estimate=pl.CostEstimate(
            flops=2 * 2 * groups * rows * 2 * taps * 2 * block,
            bytes_accessed=4 * ext * channels + 6 * ext * channels + 4 * groups * taps * taps,
            transcendentals=0,
        ),
        name="mixing",
    )(earlier, projected, order, filters, bands, skip)


def tap_grad_kernel(groups, pieces, *refs):
    grads, (query, mixed, taps_out, skip_out) = refs[:pieces], refs[pieces:]
    total = grads[0][...].astype(F32)
    for piece in grads[1:]:
        total = total + piece[...].astype(F32)
    weighted = total * query[...]
    rows, channels = weighted.shape
    taps = taps_out.shape[1]
    span = 2 * taps
    first = rows - taps
    spare = rows - taps
    both = mixed[...]
    skip_out[...] = jnp.sum(weighted * both[rows:], axis=0, keepdims=True)
    both_top = both.astype(BF16)
    flip = jnp.where(
        lax.broadcasted_iota(jnp.int32, (span, span), 0)
        + lax.broadcasted_iota(jnp.int32, (span, span), 1)
        == span - 1,
        1.0,
        0.0,
    ).astype(BF16)

    def backwards(start):
        end = jnp.dot(flip, both_top[start : start + span], preferred_element_type=F32)
        return jnp.concatenate([end.astype(BF16)] * 2, 1)

    near, far = backwards(first), backwards(2 * first)
    parts = jnp.concatenate(halves(weighted), 1)
    lane_group = (lax.broadcasted_iota(jnp.int32, (1, 2 * channels), 1) % channels) // (
        channels // groups
    )
    contract = (((1,), (1,)), ((), ()))
    masks = [jnp.where(lane_group == g, 1.0, 0.0).astype(BF16) for g in range(groups)]
    sides = jnp.concatenate([parts[:taps] * mask for mask in masks], 0)
    ends = jnp.concatenate([parts[taps:].astype(F32) * mask.astype(F32) for mask in masks], 0)
    bodies = lax.dot_general(sides, near, contract, preferred_element_type=F32)
    tails = lax.dot_general(ends.astype(BF16), far, contract, preferred_element_type=F32)
    for g in range(groups):
        body = bodies[g * taps : (g + 1) * taps]
        tail = tails[g * spare : (g + 1) * spare]
        body = jnp.concatenate([body[: taps - spare], body[taps - spare :] + tail], 0)
        skewed = pltpu.roll(body, 0, 1, stride=1, stride_axis=0)
        line = jnp.sum(skewed, axis=0, keepdims=True)
        taps_out[g : g + 1, :] = pltpu.roll(line, span - (taps - 1), 1)[:, :taps]


def tap_grad(grads, query, mixed, groups, taps):
    rows, channels = query.shape
    ext = mixed.shape[0]
    block = 128 if channels % 128 == 0 else channels
    steps = channels // block
    per_step = groups // steps
    span = 2 * taps
    one = pl.BlockSpec((rows, block), lambda i: (0, i))
    return pl.pallas_call(
        functools.partial(tap_grad_kernel, per_step, len(grads)),
        grid=(steps,),
        out_shape=[
            jax.ShapeDtypeStruct((groups, taps), F32),
            jax.ShapeDtypeStruct((1, channels), F32),
        ],
        in_specs=[one] * (len(grads) + 1) + [pl.BlockSpec((ext, block), lambda i: (0, i))],
        out_specs=[
            pl.BlockSpec((per_step, taps), lambda i: (i, 0)),
            pl.BlockSpec((1, block), lambda i: (0, i)),
        ],
        compiler_params=pltpu.CompilerParams(vmem_limit_bytes=SMALL_LIMIT),
        cost_estimate=pl.CostEstimate(
            flops=2 * groups * rows * span * 2 * block,
            bytes_accessed=4 * ext * channels + 6 * rows * channels,
            transcendentals=0,
        ),
        name="tap_grad",
    )(*grads, query, mixed)


def add_pairs_kernel(*refs):
    count = len(refs) // 3
    for one, other, out in zip(refs[:count], refs[count : 2 * count], refs[2 * count :]):
        out[...] = one[...] + other[...]


def add_pairs(ones, others):
    return pl.pallas_call(
        add_pairs_kernel,
        out_shape=[jax.ShapeDtypeStruct(one.shape, one.dtype) for one in ones],
        in_specs=[VMEM_SPEC] * (2 * len(ones)),
        out_specs=[VMEM_SPEC] * len(ones),
        compiler_params=pltpu.CompilerParams(vmem_limit_bytes=SMALL_LIMIT),
        name="add_pairs",
    )(*ones, *others)


def branch_order(block, width):
    to = np.arange(3 * block)
    branch, channel = to // block, to % block
    source = 3 * width * (channel // width) + width * branch + channel % width
    return jnp.asarray(np.arange(3 * block)[:, None] == source[None, :], BF16)


def local(tokens, w_in, short_filter, mr_filter, skip, w_out, grad_out):
    high, low = split_axis(lax.axis_size("col"))
    row_size = lax.axis_size("row")
    channels = tokens.shape[1]
    groups, taps = mr_filter.shape
    width = channels // groups
    block = 128 if channels % 128 == 0 else channels

    order = branch_order(block, width)
    gather = Gather(tokens, high, low, True)
    parts = partials(grad_out, w_out, high, low)
    gather.pass_on(parts, gather.late)
    bands, filters = prepare(*after((mr_filter, short_filter), gather.line), order)
    gather.line = after(gather.line, bands, filters)
    projected = gather.finish(w_in, BF16, "project")
    earlier = lax.ppermute(projected, "row", [(r, r + 1) for r in range(row_size - 1)])
    gated, query, mixed = mixing(earlier, projected, order, filters, bands, skip[None], groups)
    parts = after(parts, gather.total)
    gather = Gather(gated, high, low, True)

    parts = list(parts)
    for step in reversed(range(low.bit_length() - 1)):
        moved = after(swap_low(parts.pop(), high, low, step), gather.near)
        at = 0
        for i, part in enumerate(parts):
            count = part.shape[0]
            total = part.astype(F32) + moved[at : at + count].astype(F32)
            parts[i], at = total.astype(BF16), at + count
    gather.pass_on(gather.late)
    sums = after([parts[0][j] for j in range(high)], gather.line)
    grads = [sums[0]] + [shift_high(sums[j], high, low, j) for j in range(1, high)]
    block_out = gather.finish(w_out, BF16, "output", ())
    grads = after(grads, block_out)

    tap_part, skip_part = tap_grad(grads, query, mixed, groups, taps)
    if row_size == 2:
        swap = [(0, 1), (1, 0)]
        other = [lax.ppermute(part, "row", swap) for part in (tap_part, skip_part)]
        filter_grad, skip_grad = add_pairs((tap_part, skip_part), other)
        skip_grad = skip_grad.reshape(-1)
    else:
        filter_grad, skip_grad = lax.psum((tap_part, skip_part.reshape(-1)), "row")
    return (block_out, filter_grad, skip_grad)


def solution(mesh):
    in_specs = (
        P("row", "col"),
        P(None, "col"),
        P(None, "col"),
        P("col", None),
        P("col"),
        P(None, "col"),
        P("row", "col"),
    )
    out_specs = (P("row", "col"), P("col", None), P("col"))
    return jax.shard_map(local, mesh=mesh, in_specs=in_specs, out_specs=out_specs, check_vma=False)
```

```python
import functools

import jax
import jax.numpy as jnp
import numpy as np
from jax import lax
from jax.experimental import pallas as pl
from jax.experimental.pallas import tpu as pltpu
from jax.sharding import PartitionSpec as P

F32 = jnp.float32
BF16 = jnp.bfloat16
VMEM_SPEC = pl.BlockSpec(memory_space=pltpu.VMEM)
SMEM_SPEC = pl.BlockSpec(memory_space=pltpu.SMEM)
HBM_SPEC = pl.BlockSpec(memory_space=pltpu.HBM)
WEIGHT_SLOTS = 4
VMEM_LIMIT = 47 * 2**20
SMALL_LIMIT = 16 * 2**20


def split_axis(size):
    low = 1
    while low * low < size and size % (low * 2) == 0:
        low *= 2
    return size // low, low


def low_masks(low, parity):
    bits = [1 << i for i in range(low.bit_length() - 1)]
    return bits[::-1] if parity else bits


def swap_low(block, high, low, step):
    rows = lax.axis_size("row")
    size = high * low
    route = []
    for r in range(rows):
        mask = low_masks(low, r % 2)[step]
        route += [(r * size + c, r * size + (c ^ mask)) for c in range(size)]
    return lax.ppermute(block, ("row", "col"), route)


def shift_high(block, high, low, k):
    route = [(h * low + l, ((h + k) % high) * low + l) for h in range(high) for l in range(low)]
    return lax.ppermute(block, "col", route)


def flipped_low(low):
    parity = lax.axis_index("row") % 2
    forward, backward = low_masks(low, 0), low_masks(low, 1)
    flips = [0]
    for one, other in zip(forward, backward):
        mask = jnp.where(parity == 0, one, other)
        flips += [flip + mask for flip in flips]
    return flips


def after(values, *others):
    return lax.optimization_barrier((values, others))[0]


class Gather:
    def __init__(self, block, high, low, apart):
        self.high, self.low, self.block = high, low, block
        self.bits = low.bit_length() - 1
        shifts = list(range(1, high))
        self.shifts = shifts
        self.line = [shift_high(block, high, low, k) for k in shifts]
        self.near, self.late = [], []
        if apart:
            items = self.plane([block], self.bits - 1)
            self.near = items[1:]
            items = after(items, self.near)
            self.late = [swap_low(each, high, low, self.bits - 1) for each in items]

    def plane(self, items, steps):
        for step in range(steps):
            items = items + [swap_low(each, self.high, self.low, step) for each in items]
        return items

    def pass_on(self, *others):
        self.line = after(self.line, self.near, others)
        blocks = self.line if self.late else [self.block, *self.line]
        self.far = self.plane([jnp.stack(blocks)], self.bits - 1)

    def finish(self, weights, out_type, name, before_hop=()):
        high, low = self.high, self.low
        me = lax.axis_index("col")
        h, l = me // low, me % low
        flips = flipped_low(low)
        from_high = [(h - k + high) % high for k in self.shifts]
        small = weights.size < 2**23
        limit = VMEM_LIMIT if small else 34 * 2**20

        owners = [h * low + (l ^ flip) for flip in flips]
        own = 1 + len(self.near)
        owners, late_owners = owners[:own], owners[own:]
        owners += [f * low + l for f in from_high]
        pieces = [self.block, *self.near, *self.line]
        total, = accumulate(None, pieces, owners, weights, None, F32, 0, limit, name + "_0")
        hop = after(self.far, total, before_hop)
        last = [swap_low(each, high, low, self.bits - 1) for each in hop]
        self.last = last
        if not self.late:
            late_owners, from_high = [], [h, *from_high]
        owners = late_owners + [f * low + (l ^ flip) for flip in flips[1:] for f in from_high]
        final = len(last) * len(from_high)
        loads = final if small else 0
        pieces = [*self.late, *self.far[1:]]
        total, *ahead = accumulate(
            total, pieces, owners, weights, None, F32, loads, limit, name + "_1"
        )
        ahead = ahead[0] if loads else None
        self.total = total
        owners = owners[len(owners) - final :]
        return accumulate(total, last, owners, weights, ahead, out_type, 0, limit, name + "_2")[0]


def accumulate_kernel(counts, has_total, ready, loads, width, owners, *refs):
    refs = list(refs)
    pieces = [refs.pop(0) for _ in counts]
    total = refs.pop(0) if has_total else None
    here = refs.pop(0) if ready else None
    weights, out = refs[:2]
    refs = refs[2:]
    ahead = refs.pop(0) if loads else None
    sums, held, sems, ahead_sems = refs
    order = [(p, i) for p, count in enumerate(counts) for i in range(count or 1)]
    depth = held.shape[1]

    def rows_of(step):
        return weights.at[pl.ds(pl.multiple_of(owners[step] * depth, depth), depth), :]

    def fetch(step):
        slot = step % WEIGHT_SLOTS
        return pltpu.make_async_copy(rows_of(step), held.at[slot], sems.at[slot])

    def load(at):
        return pltpu.make_async_copy(rows_of(len(order) + at), ahead.at[at], ahead_sems.at[at])

    for step in range(ready, min(ready + WEIGHT_SLOTS, len(order))):
        fetch(step).start()
    for step, (p, i) in enumerate(order):
        if step >= ready:
            fetch(step).wait()
        slot = step % WEIGHT_SLOTS
        rows = pieces[p][i] if counts[p] else pieces[p][...]
        for at in range(0, out.shape[1], width):
            cols = slice(at, at + width)
            part = here[step, :, cols] if step < ready else held[slot, :, cols]
            term = jnp.dot(rows, part, preferred_element_type=F32)
            if step == 0 and total is not None:
                term = term + total[:, cols]
            if step:
                term = term + sums[:, cols]
            if step + 1 == len(order):
                out[:, cols] = term.astype(out.dtype)
            else:
                sums[:, cols] = term
        if step >= ready and step + WEIGHT_SLOTS < len(order):
            fetch(step + WEIGHT_SLOTS).start()
        if step == max(0, len(order) - 1 - WEIGHT_SLOTS):
            for at in range(loads):
                load(at).start()
    for at in range(loads):
        load(at).wait()


def accumulate(total, pieces, owners, weights, here, out_type, loads, limit, name):
    counts = tuple(0 if piece.ndim == 2 else piece.shape[0] for piece in pieces)
    rows, depth = pieces[0].shape[-2:]
    columns = weights.shape[-1]
    width = next(w for w in (512, 256, 128, columns) if columns % w == 0)
    steps = sum(count or 1 for count in counts)
    ready = 0 if here is None else here.shape[0]
    operands = [jnp.stack(owners).astype(jnp.int32), *pieces]
    operands += [extra for extra in (total, here) if extra is not None]
    out_shape = [jax.ShapeDtypeStruct((rows, columns), out_type)]
    if loads:
        out_shape.append(jax.ShapeDtypeStruct((loads, depth, columns), weights.dtype))
    return pl.pallas_call(
        functools.partial(accumulate_kernel, counts, total is not None, ready, loads, width),
        out_shape=out_shape,
        in_specs=[SMEM_SPEC] + [VMEM_SPEC] * (len(operands) - 1) + [HBM_SPEC],
        out_specs=[VMEM_SPEC] * len(out_shape),
        scratch_shapes=[
            pltpu.VMEM((rows, columns), F32),
            pltpu.VMEM((WEIGHT_SLOTS, depth, columns), weights.dtype),
            pltpu.SemaphoreType.DMA((WEIGHT_SLOTS,)),
            pltpu.SemaphoreType.DMA((max(1, loads),)),
        ],
        compiler_params=pltpu.CompilerParams(vmem_limit_bytes=limit),
        cost_estimate=pl.CostEstimate(
            flops=2 * steps * rows * depth * columns,
            bytes_accessed=(steps + loads) * depth * columns * 2 + rows * columns * 8,
            transcendentals=0,
        ),
        name=name,
    )(*operands, weights)


def partials_kernel(owners, grads, weights, *refs):
    outs, (held, sems) = refs[:-2], refs[-2:]
    order = [(o, i) for o, out in enumerate(outs) for i in range(out.shape[0])]
    depth = held.shape[1]

    def fetch(step):
        start = pl.multiple_of(owners[step] * depth, depth)
        slot = step % WEIGHT_SLOTS
        return pltpu.make_async_copy(
            weights.at[pl.ds(start, depth), :], held.at[slot], sems.at[slot]
        )

    for step in range(min(WEIGHT_SLOTS, len(order))):
        fetch(step).start()
    for step, (o, i) in enumerate(order):
        fetch(step).wait()
        term = lax.dot_general(
            grads[...],
            held[step % WEIGHT_SLOTS],
            (((1,), (1,)), ((), ())),
            preferred_element_type=F32,
        )
        outs[o][i] = term.astype(outs[o].dtype)
        if step + WEIGHT_SLOTS < len(order):
            fetch(step + WEIGHT_SLOTS).start()


def partials(grads, weights, high, low):
    me = lax.axis_index("col")
    h, l = me // low, me % low
    owners = [((h + j) % high) * low + (l ^ flip) for flip in flipped_low(low) for j in range(high)]
    rows, features = grads.shape
    depth = weights.shape[0] // (high * low)
    counts = [high] + [high << step for step in range(low.bit_length() - 1)]
    return pl.pallas_call(
        partials_kernel,
        out_shape=[jax.ShapeDtypeStruct((count, rows, depth), BF16) for count in counts],
        in_specs=[SMEM_SPEC, VMEM_SPEC, HBM_SPEC],
        out_specs=[VMEM_SPEC] * len(counts),
        scratch_shapes=[
            pltpu.VMEM((WEIGHT_SLOTS, depth, features), weights.dtype),
            pltpu.SemaphoreType.DMA((WEIGHT_SLOTS,)),
        ],
        compiler_params=pltpu.CompilerParams(vmem_limit_bytes=VMEM_LIMIT),
        cost_estimate=pl.CostEstimate(
            flops=2 * rows * features * weights.shape[0],
            bytes_accessed=2 * weights.shape[0] * (features + rows),
            transcendentals=0,
        ),
        name="grad_partials",
    )(jnp.stack(owners).astype(jnp.int32), grads, weights)


def halves(value):
    top = value.astype(BF16)
    return top, (value - top.astype(F32)).astype(BF16)


def prepare_kernel(mr_filter, short_filter, order, table, filters):
    taps, span = table.shape[1:]
    ends = lax.broadcasted_iota(jnp.int32, (taps, span), 0) + lax.broadcasted_iota(
        jnp.int32, (taps, span), 1
    )
    flip = jnp.where(ends == taps, 1.0, 0.0).astype(BF16)
    first = jnp.dot(mr_filter[...].astype(BF16), flip, preferred_element_type=F32)
    for g in range(table.shape[0]):
        spreadout = jnp.broadcast_to(first[g : g + 1, :], (taps, span))
        table[g] = pltpu.roll(spreadout, 0, 1, stride=1, stride_axis=0).astype(table.dtype)
    size = order.shape[0]
    for at in range(0, filters.shape[1], size):
        left = short_filter[:, at : at + size]
        moved = jnp.zeros(left.shape, F32)
        for _ in range(3):
            part = left.astype(BF16)
            moved = moved + jnp.dot(part, order[...], preferred_element_type=F32)
            left = left - part.astype(F32)
        filters[:, at : at + size] = moved


def prepare(mr_filter, short_filter, order):
    groups, taps = mr_filter.shape
    return pl.pallas_call(
        prepare_kernel,
        out_shape=[
            jax.ShapeDtypeStruct((groups, taps, 2 * taps), BF16),
            jax.ShapeDtypeStruct(short_filter.shape, F32),
        ],
        in_specs=[VMEM_SPEC] * 3,
        out_specs=[VMEM_SPEC] * 2,
        compiler_params=pltpu.CompilerParams(vmem_limit_bytes=SMALL_LIMIT),
        name="prepare",
    )(mr_filter, short_filter, order)


def by_blocks(kernel, steps, parts, *refs):
    for step in range(steps):
        views = []
        for ref, part in zip(refs, parts):
            if part is not None:
                size = ref.shape[part] // steps
                cut = [slice(None)] * len(ref.shape)
                cut[part] = pl.ds(step * size, size)
                ref = ref.at[tuple(cut)]
            views.append(ref)
        kernel(*views)


def mixing_kernel(groups, earlier, projected, order, filters, bands, skip, gated, query, mixed):
    rows = projected.shape[0]
    channels = skip.shape[1]
    taps = bands.shape[1]
    span = 2 * taps
    extended = jnp.concatenate([earlier[...].astype(F32), projected[...].astype(F32)], 0).astype(BF16)
    lines = jnp.dot(extended, order[...], preferred_element_type=F32)
    short = (
        filters[0:1, :] * lines
        + filters[1:2, :] * pltpu.roll(lines, 1, 0)
        + filters[2:3, :] * pltpu.roll(lines, 2, 0)
    )
    own_query = short[rows:, :channels]
    both = short[:, channels : 2 * channels] * short[:, 2 * channels :]
    query[...] = own_query
    mixed[...] = both
    both_top, both_rest = halves(both)
    pair = jnp.concatenate([both_top, both_rest], 1)
    lane_group = lax.broadcasted_iota(jnp.int32, (taps, channels), 1) // (channels // groups)
    first = spare = rows - taps
    whole = bands[...].reshape(groups * taps, span)
    ends = bands[:, taps - spare :, :].reshape(groups * spare, span)
    bodies = jnp.dot(whole, pair[first : first + span], preferred_element_type=F32)
    tails = jnp.dot(ends, pair[2 * first :], preferred_element_type=F32)
    bodies = bodies[:, :channels] + bodies[:, channels:]
    tails = tails[:, :channels] + tails[:, channels:]
    body, tail = bodies[:taps], tails[:spare]
    for g in range(1, groups):
        body = jnp.where(lane_group == g, bodies[g * taps : (g + 1) * taps], body)
        tail = jnp.where(lane_group[:spare] == g, tails[g * spare : (g + 1) * spare], tail)
    longconv = jnp.concatenate([body, tail], 0)
    gated[...] = (own_query * (longconv + skip[...] * both[rows:])).astype(gated.dtype)


def mixing(earlier, projected, order, filters, bands, skip, groups):
    rows, columns = projected.shape
    channels = columns // 3
    block = order.shape[0] // 3
    steps = channels // block
    per_step = groups // steps
    taps = bands.shape[1]
    ext = 2 * rows
    parts = (1, 1, None, 1, 0, 1, 1, 1, 1)
    return pl.pallas_call(
        functools.partial(by_blocks, functools.partial(mixing_kernel, per_step), steps, parts),
        out_shape=[
            jax.ShapeDtypeStruct((rows, channels), BF16),
            jax.ShapeDtypeStruct((rows, channels), F32),
            jax.ShapeDtypeStruct((ext, channels), F32),
        ],
        in_specs=[VMEM_SPEC] * 6,
        out_specs=[VMEM_SPEC] * 3,
        compiler_params=pltpu.CompilerParams(vmem_limit_bytes=2 * SMALL_LIMIT),
        cost_estimate=pl.CostEstimate(
            flops=2 * 2 * groups * rows * 2 * taps * 2 * block,
            bytes_accessed=4 * ext * channels + 6 * ext * channels + 4 * groups * taps * taps,
            transcendentals=0,
        ),
        name="mixing",
    )(earlier, projected, order, filters, bands, skip)


def tap_grad_kernel(groups, pieces, *refs):
    grads, (query, mixed, taps_out, skip_out) = refs[:pieces], refs[pieces:]
    total = grads[0][...].astype(F32)
    for piece in grads[1:]:
        total = total + piece[...].astype(F32)
    weighted = total * query[...]
    rows, channels = weighted.shape
    taps = taps_out.shape[1]
    span = 2 * taps
    first = rows - taps
    spare = rows - taps
    both = mixed[...]
    skip_out[...] = jnp.sum(weighted * both[rows:], axis=0, keepdims=True)
    both_top = both.astype(BF16)
    flip = jnp.where(
        lax.broadcasted_iota(jnp.int32, (span, span), 0)
        + lax.broadcasted_iota(jnp.int32, (span, span), 1)
        == span - 1,
        1.0,
        0.0,
    ).astype(BF16)

    def backwards(start):
        end = jnp.dot(flip, both_top[start : start + span], preferred_element_type=F32)
        return jnp.concatenate([end.astype(BF16)] * 2, 1)

    near, far = backwards(first), backwards(2 * first)
    parts = jnp.concatenate(halves(weighted), 1)
    lane_group = (lax.broadcasted_iota(jnp.int32, (1, 2 * channels), 1) % channels) // (
        channels // groups
    )
    contract = (((1,), (1,)), ((), ()))
    masks = [jnp.where(lane_group == g, 1.0, 0.0).astype(BF16) for g in range(groups)]
    sides = jnp.concatenate([parts[:taps] * mask for mask in masks], 0)
    ends = jnp.concatenate([parts[taps:].astype(F32) * mask.astype(F32) for mask in masks], 0)
    bodies = lax.dot_general(sides, near, contract, preferred_element_type=F32)
    tails = lax.dot_general(ends.astype(BF16), far, contract, preferred_element_type=F32)
    for g in range(groups):
        body = bodies[g * taps : (g + 1) * taps]
        tail = tails[g * spare : (g + 1) * spare]
        body = jnp.concatenate([body[: taps - spare], body[taps - spare :] + tail], 0)
        skewed = pltpu.roll(body, 0, 1, stride=1, stride_axis=0)
        line = jnp.sum(skewed, axis=0, keepdims=True)
        taps_out[g : g + 1, :] = pltpu.roll(line, span - (taps - 1), 1)[:, :taps]


def tap_grad(grads, query, mixed, groups, taps):
    rows, channels = query.shape
    ext = mixed.shape[0]
    block = 128 if channels % 128 == 0 else channels
    steps = channels // block
    per_step = groups // steps
    span = 2 * taps
    parts = (1,) * (len(grads) + 2) + (0, 1)
    kernel = functools.partial(tap_grad_kernel, per_step, len(grads))
    return pl.pallas_call(
        functools.partial(by_blocks, kernel, steps, parts),
        out_shape=[
            jax.ShapeDtypeStruct((groups, taps), F32),
            jax.ShapeDtypeStruct((1, channels), F32),
        ],
        in_specs=[VMEM_SPEC] * (len(grads) + 2),
        out_specs=[VMEM_SPEC] * 2,
        compiler_params=pltpu.CompilerParams(vmem_limit_bytes=2 * SMALL_LIMIT),
        cost_estimate=pl.CostEstimate(
            flops=2 * groups * rows * span * 2 * block,
            bytes_accessed=4 * ext * channels + 6 * rows * channels,
            transcendentals=0,
        ),
        name="tap_grad",
    )(*grads, query, mixed)


def add_pairs_kernel(*refs):
    count = len(refs) // 3
    for one, other, out in zip(refs[:count], refs[count : 2 * count], refs[2 * count :]):
        out[...] = one[...] + other[...]


def add_pairs(ones, others):
    return pl.pallas_call(
        add_pairs_kernel,
        out_shape=[jax.ShapeDtypeStruct(one.shape, one.dtype) for one in ones],
        in_specs=[VMEM_SPEC] * (2 * len(ones)),
        out_specs=[VMEM_SPEC] * len(ones),
        compiler_params=pltpu.CompilerParams(vmem_limit_bytes=SMALL_LIMIT),
        name="add_pairs",
    )(*ones, *others)


def branch_order(block, width):
    to = np.arange(3 * block)
    branch, channel = to // block, to % block
    source = 3 * width * (channel // width) + width * branch + channel % width
    return jnp.asarray(np.arange(3 * block)[:, None] == source[None, :], BF16)


def local(tokens, w_in, short_filter, mr_filter, skip, w_out, grad_out):
    high, low = split_axis(lax.axis_size("col"))
    row_size = lax.axis_size("row")
    channels = tokens.shape[1]
    groups, taps = mr_filter.shape
    width = channels // groups
    block = 128 if channels % 128 == 0 else channels

    order = branch_order(block, width)
    gather = Gather(tokens, high, low, True)
    parts = partials(grad_out, w_out, high, low)
    gather.pass_on(parts, gather.late)
    bands, filters = prepare(*after((mr_filter, short_filter), gather.line), order)
    gather.line = after(gather.line, bands, filters)
    projected = gather.finish(w_in, BF16, "project")
    earlier = lax.ppermute(projected, "row", [(r, r + 1) for r in range(row_size - 1)])
    gated, query, mixed = mixing(earlier, projected, order, filters, bands, skip[None], groups)
    parts = after(parts, gather.total)
    gather = Gather(gated, high, low, True)

    parts = list(parts)
    for step in reversed(range(low.bit_length() - 1)):
        moved = after(swap_low(parts.pop(), high, low, step), gather.near)
        at = 0
        for i, part in enumerate(parts):
            count = part.shape[0]
            total = part.astype(F32) + moved[at : at + count].astype(F32)
            parts[i], at = total.astype(BF16), at + count
    gather.pass_on(gather.late)
    sums = after([parts[0][j] for j in range(high)], gather.line)
    grads = [sums[0]] + [shift_high(sums[j], high, low, j) for j in range(1, high)]
    block_out = gather.finish(w_out, BF16, "output", ())
    grads = after(grads, block_out)

    tap_part, skip_part = tap_grad(grads, query, mixed, groups, taps)
    if row_size == 2:
        swap = [(0, 1), (1, 0)]
        other = [lax.ppermute(part, "row", swap) for part in (tap_part, skip_part)]
        filter_grad, skip_grad = add_pairs((tap_part, skip_part), other)
        skip_grad = skip_grad.reshape(-1)
    else:
        filter_grad, skip_grad = lax.psum((tap_part, skip_part.reshape(-1)), "row")
    return (block_out, filter_grad, skip_grad)


def solution(mesh):
    in_specs = (
        P("row", "col"),
        P(None, "col"),
        P(None, "col"),
        P("col", None),
        P("col"),
        P(None, "col"),
        P("row", "col"),
    )
    out_specs = (P("row", "col"), P("col", None), P("col"))
    return jax.shard_map(local, mesh=mesh, in_specs=in_specs, out_specs=out_specs, check_vma=False)
```

```python
import functools

import jax
import jax.numpy as jnp
import numpy as np
from jax import lax
from jax.experimental import pallas as pl
from jax.experimental.pallas import tpu as pltpu
from jax.sharding import PartitionSpec as P

F32 = jnp.float32
BF16 = jnp.bfloat16
VMEM_SPEC = pl.BlockSpec(memory_space=pltpu.VMEM)
SMEM_SPEC = pl.BlockSpec(memory_space=pltpu.SMEM)
HBM_SPEC = pl.BlockSpec(memory_space=pltpu.HBM)
WEIGHT_SLOTS = 6
VMEM_LIMIT = 47 * 2**20
SMALL_LIMIT = 16 * 2**20


def split_axis(size):
    low = 1
    while low * low < size and size % (low * 2) == 0:
        low *= 2
    return size // low, low


def low_masks(low, parity):
    bits = [1 << i for i in range(low.bit_length() - 1)]
    return bits[::-1] if parity else bits


def swap_low(block, high, low, step):
    rows = lax.axis_size("row")
    size = high * low
    route = []
    for r in range(rows):
        mask = low_masks(low, r % 2)[step]
        route += [(r * size + c, r * size + (c ^ mask)) for c in range(size)]
    return lax.ppermute(block, ("row", "col"), route)


def shift_high(block, high, low, k):
    route = [(h * low + l, ((h + k) % high) * low + l) for h in range(high) for l in range(low)]
    return lax.ppermute(block, "col", route)


def flipped_low(low):
    parity = lax.axis_index("row") % 2
    forward, backward = low_masks(low, 0), low_masks(low, 1)
    flips = [0]
    for one, other in zip(forward, backward):
        mask = jnp.where(parity == 0, one, other)
        flips += [flip + mask for flip in flips]
    return flips


def after(values, *others):
    return lax.optimization_barrier((values, others))[0]


class Gather:
    def __init__(self, block, high, low, apart):
        self.high, self.low, self.block = high, low, block
        self.bits = low.bit_length() - 1
        shifts = list(range(1, high))
        self.shifts = shifts
        self.line = [shift_high(block, high, low, k) for k in shifts]
        self.near, self.late = [], []
        if apart:
            items = self.plane([block], self.bits - 1)
            self.near = items[1:]
            items = after(items, self.near)
            self.late = [swap_low(each, high, low, self.bits - 1) for each in items]

    def plane(self, items, steps):
        for step in range(steps):
            items = items + [swap_low(each, self.high, self.low, step) for each in items]
        return items

    def pass_on(self, *others):
        self.line = after(self.line, self.near, others)
        blocks = self.line if self.late else [self.block, *self.line]
        self.far = self.plane([jnp.stack(blocks)], self.bits - 1)

    def finish(self, weights, out_type, name, before_hop=()):
        high, low = self.high, self.low
        me = lax.axis_index("col")
        h, l = me // low, me % low
        flips = flipped_low(low)
        from_high = [(h - k + high) % high for k in self.shifts]
        small = weights.size < 2**23
        limit = VMEM_LIMIT if small else 34 * 2**20

        owners = [h * low + (l ^ flip) for flip in flips]
        own = 1 + len(self.near)
        owners, late_owners = owners[:own], owners[own:]
        owners += [f * low + l for f in from_high]
        pieces = [self.block, *self.near, *self.line]
        total, = accumulate(None, pieces, owners, weights, None, F32, 0, limit, name + "_0")
        hop = after(self.far, total, before_hop)
        last = [swap_low(each, high, low, self.bits - 1) for each in hop]
        self.last = last
        if not self.late:
            late_owners, from_high = [], [h, *from_high]
        owners = late_owners + [f * low + (l ^ flip) for flip in flips[1:] for f in from_high]
        final = len(last) * len(from_high)
        loads = final if small else 0
        pieces = [*self.late, *self.far[1:]]
        total, *ahead = accumulate(
            total, pieces, owners, weights, None, F32, loads, limit, name + "_1"
        )
        ahead = ahead[0] if loads else None
        self.total = total
        owners = owners[len(owners) - final :]
        return accumulate(total, last, owners, weights, ahead, out_type, 0, limit, name + "_2")[0]


def accumulate_kernel(counts, has_total, ready, loads, width, owners, *refs):
    refs = list(refs)
    pieces = [refs.pop(0) for _ in counts]
    total = refs.pop(0) if has_total else None
    here = refs.pop(0) if ready else None
    weights, out = refs[:2]
    refs = refs[2:]
    ahead = refs.pop(0) if loads else None
    sums, held, sems, ahead_sems = refs
    order = [(p, i) for p, count in enumerate(counts) for i in range(count or 1)]
    depth = held.shape[1]

    def rows_of(step):
        return weights.at[pl.ds(pl.multiple_of(owners[step] * depth, depth), depth), :]

    def fetch(step):
        slot = step % WEIGHT_SLOTS
        return pltpu.make_async_copy(rows_of(step), held.at[slot], sems.at[slot])

    def load(at):
        return pltpu.make_async_copy(rows_of(len(order) + at), ahead.at[at], ahead_sems.at[at])

    for step in range(ready, min(ready + WEIGHT_SLOTS, len(order))):
        fetch(step).start()
    for step, (p, i) in enumerate(order):
        if step >= ready:
            fetch(step).wait()
        slot = step % WEIGHT_SLOTS
        rows = pieces[p][i] if counts[p] else pieces[p][...]
        for at in range(0, out.shape[1], width):
            cols = slice(at, at + width)
            part = here[step, :, cols] if step < ready else held[slot, :, cols]
            term = jnp.dot(rows, part, preferred_element_type=F32)
            if step == 0 and total is not None:
                term = term + total[:, cols]
            if step:
                term = term + sums[:, cols]
            if step + 1 == len(order):
                out[:, cols] = term.astype(out.dtype)
            else:
                sums[:, cols] = term
        if step >= ready and step + WEIGHT_SLOTS < len(order):
            fetch(step + WEIGHT_SLOTS).start()
        if step == max(0, len(order) - 1 - WEIGHT_SLOTS):
            for at in range(loads):
                load(at).start()
    for at in range(loads):
        load(at).wait()


def accumulate(total, pieces, owners, weights, here, out_type, loads, limit, name):
    counts = tuple(0 if piece.ndim == 2 else piece.shape[0] for piece in pieces)
    rows, depth = pieces[0].shape[-2:]
    columns = weights.shape[-1]
    width = next(w for w in (512, 256, 128, columns) if columns % w == 0)
    steps = sum(count or 1 for count in counts)
    ready = 0 if here is None else here.shape[0]
    operands = [jnp.stack(owners).astype(jnp.int32), *pieces]
    operands += [extra for extra in (total, here) if extra is not None]
    out_shape = [jax.ShapeDtypeStruct((rows, columns), out_type)]
    if loads:
        out_shape.append(jax.ShapeDtypeStruct((loads, depth, columns), weights.dtype))
    return pl.pallas_call(
        functools.partial(accumulate_kernel, counts, total is not None, ready, loads, width),
        out_shape=out_shape,
        in_specs=[SMEM_SPEC] + [VMEM_SPEC] * (len(operands) - 1) + [HBM_SPEC],
        out_specs=[VMEM_SPEC] * len(out_shape),
        scratch_shapes=[
            pltpu.VMEM((rows, columns), F32),
            pltpu.VMEM((WEIGHT_SLOTS, depth, columns), weights.dtype),
            pltpu.SemaphoreType.DMA((WEIGHT_SLOTS,)),
            pltpu.SemaphoreType.DMA((max(1, loads),)),
        ],
        compiler_params=pltpu.CompilerParams(vmem_limit_bytes=limit),
        cost_estimate=pl.CostEstimate(
            flops=2 * steps * rows * depth * columns,
            bytes_accessed=(steps + loads) * depth * columns * 2 + rows * columns * 8,
            transcendentals=0,
        ),
        name=name,
    )(*operands, weights)


def partials_kernel(owners, grads, weights, *refs):
    outs, (held, sems) = refs[:-2], refs[-2:]
    order = [(o, i) for o, out in enumerate(outs) for i in range(out.shape[0])]
    depth = held.shape[1]

    def fetch(step):
        start = pl.multiple_of(owners[step] * depth, depth)
        slot = step % WEIGHT_SLOTS
        return pltpu.make_async_copy(
            weights.at[pl.ds(start, depth), :], held.at[slot], sems.at[slot]
        )

    for step in range(min(WEIGHT_SLOTS, len(order))):
        fetch(step).start()
    for step, (o, i) in enumerate(order):
        fetch(step).wait()
        term = lax.dot_general(
            grads[...],
            held[step % WEIGHT_SLOTS],
            (((1,), (1,)), ((), ())),
            preferred_element_type=F32,
        )
        outs[o][i] = term.astype(outs[o].dtype)
        if step + WEIGHT_SLOTS < len(order):
            fetch(step + WEIGHT_SLOTS).start()


def partials(grads, weights, high, low):
    me = lax.axis_index("col")
    h, l = me // low, me % low
    owners = [((h + j) % high) * low + (l ^ flip) for flip in flipped_low(low) for j in range(high)]
    rows, features = grads.shape
    depth = weights.shape[0] // (high * low)
    counts = [high] + [high << step for step in range(low.bit_length() - 1)]
    return pl.pallas_call(
        partials_kernel,
        out_shape=[jax.ShapeDtypeStruct((count, rows, depth), BF16) for count in counts],
        in_specs=[SMEM_SPEC, VMEM_SPEC, HBM_SPEC],
        out_specs=[VMEM_SPEC] * len(counts),
        scratch_shapes=[
            pltpu.VMEM((WEIGHT_SLOTS, depth, features), weights.dtype),
            pltpu.SemaphoreType.DMA((WEIGHT_SLOTS,)),
        ],
        compiler_params=pltpu.CompilerParams(vmem_limit_bytes=VMEM_LIMIT),
        cost_estimate=pl.CostEstimate(
            flops=2 * rows * features * weights.shape[0],
            bytes_accessed=2 * weights.shape[0] * (features + rows),
            transcendentals=0,
        ),
        name="grad_partials",
    )(jnp.stack(owners).astype(jnp.int32), grads, weights)


def halves(value):
    top = value.astype(BF16)
    return top, (value - top.astype(F32)).astype(BF16)


def prepare_kernel(mr_filter, short_filter, order, table, filters):
    taps, span = table.shape[1:]
    ends = lax.broadcasted_iota(jnp.int32, (taps, span), 0) + lax.broadcasted_iota(
        jnp.int32, (taps, span), 1
    )
    flip = jnp.where(ends == taps, 1.0, 0.0).astype(BF16)
    first = jnp.dot(mr_filter[...].astype(BF16), flip, preferred_element_type=F32)
    for g in range(table.shape[0]):
        spreadout = jnp.broadcast_to(first[g : g + 1, :], (taps, span))
        table[g] = pltpu.roll(spreadout, 0, 1, stride=1, stride_axis=0).astype(table.dtype)
    size = order.shape[0]
    for at in range(0, filters.shape[1], size):
        left = short_filter[:, at : at + size]
        moved = jnp.zeros(left.shape, F32)
        for _ in range(3):
            part = left.astype(BF16)
            moved = moved + jnp.dot(part, order[...], preferred_element_type=F32)
            left = left - part.astype(F32)
        filters[:, at : at + size] = moved


def prepare(mr_filter, short_filter, order):
    groups, taps = mr_filter.shape
    return pl.pallas_call(
        prepare_kernel,
        out_shape=[
            jax.ShapeDtypeStruct((groups, taps, 2 * taps), BF16),
            jax.ShapeDtypeStruct(short_filter.shape, F32),
        ],
        in_specs=[VMEM_SPEC] * 3,
        out_specs=[VMEM_SPEC] * 2,
        compiler_params=pltpu.CompilerParams(vmem_limit_bytes=SMALL_LIMIT),
        name="prepare",
    )(mr_filter, short_filter, order)


def by_blocks(kernel, steps, parts, *refs):
    for step in range(steps):
        views = []
        for ref, part in zip(refs, parts):
            if part is not None:
                size = ref.shape[part] // steps
                cut = [slice(None)] * len(ref.shape)
                cut[part] = pl.ds(step * size, size)
                ref = ref.at[tuple(cut)]
            views.append(ref)
        kernel(*views)


def mixing_kernel(groups, earlier, projected, order, filters, bands, skip, gated, query, mixed):
    rows = projected.shape[0]
    channels = skip.shape[1]
    taps = bands.shape[1]
    span = 2 * taps
    extended = jnp.concatenate([earlier[...].astype(F32), projected[...].astype(F32)], 0).astype(BF16)
    lines = jnp.dot(extended, order[...], preferred_element_type=F32)
    short = (
        filters[0:1, :] * lines
        + filters[1:2, :] * pltpu.roll(lines, 1, 0)
        + filters[2:3, :] * pltpu.roll(lines, 2, 0)
    )
    own_query = short[rows:, :channels]
    both = short[:, channels : 2 * channels] * short[:, 2 * channels :]
    query[...] = own_query
    mixed[...] = both
    both_top, both_rest = halves(both)
    pair = jnp.concatenate([both_top, both_rest], 1)
    lane_group = lax.broadcasted_iota(jnp.int32, (taps, channels), 1) // (channels // groups)
    first = spare = rows - taps
    whole = bands[...].reshape(groups * taps, span)
    ends = bands[:, taps - spare :, :].reshape(groups * spare, span)
    bodies = jnp.dot(whole, pair[first : first + span], preferred_element_type=F32)
    tails = jnp.dot(ends, pair[2 * first :], preferred_element_type=F32)
    bodies = bodies[:, :channels] + bodies[:, channels:]
    tails = tails[:, :channels] + tails[:, channels:]
    body, tail = bodies[:taps], tails[:spare]
    for g in range(1, groups):
        body = jnp.where(lane_group == g, bodies[g * taps : (g + 1) * taps], body)
        tail = jnp.where(lane_group[:spare] == g, tails[g * spare : (g + 1) * spare], tail)
    longconv = jnp.concatenate([body, tail], 0)
    gated[...] = (own_query * (longconv + skip[...] * both[rows:])).astype(gated.dtype)


def mixing(earlier, projected, order, filters, bands, skip, groups):
    rows, columns = projected.shape
    channels = columns // 3
    block = order.shape[0] // 3
    steps = channels // block
    per_step = groups // steps
    taps = bands.shape[1]
    ext = 2 * rows
    parts = (1, 1, None, 1, 0, 1, 1, 1, 1)
    return pl.pallas_call(
        functools.partial(by_blocks, functools.partial(mixing_kernel, per_step), steps, parts),
        out_shape=[
            jax.ShapeDtypeStruct((rows, channels), BF16),
            jax.ShapeDtypeStruct((rows, channels), F32),
            jax.ShapeDtypeStruct((ext, channels), F32),
        ],
        in_specs=[VMEM_SPEC] * 6,
        out_specs=[VMEM_SPEC] * 3,
        compiler_params=pltpu.CompilerParams(vmem_limit_bytes=2 * SMALL_LIMIT),
        cost_estimate=pl.CostEstimate(
            flops=2 * 2 * groups * rows * 2 * taps * 2 * block,
            bytes_accessed=4 * ext * channels + 6 * ext * channels + 4 * groups * taps * taps,
            transcendentals=0,
        ),
        name="mixing",
    )(earlier, projected, order, filters, bands, skip)


def tap_grad_kernel(groups, pieces, *refs):
    grads, (query, mixed, taps_out, skip_out) = refs[:pieces], refs[pieces:]
    total = grads[0][...].astype(F32)
    for piece in grads[1:]:
        total = total + piece[...].astype(F32)
    weighted = total * query[...]
    rows, channels = weighted.shape
    taps = taps_out.shape[1]
    span = 2 * taps
    first = rows - taps
    spare = rows - taps
    both = mixed[...]
    skip_out[...] = jnp.sum(weighted * both[rows:], axis=0, keepdims=True)
    both_top = both.astype(BF16)
    flip = jnp.where(
        lax.broadcasted_iota(jnp.int32, (span, span), 0)
        + lax.broadcasted_iota(jnp.int32, (span, span), 1)
        == span - 1,
        1.0,
        0.0,
    ).astype(BF16)

    def backwards(start):
        end = jnp.dot(flip, both_top[start : start + span], preferred_element_type=F32)
        return jnp.concatenate([end.astype(BF16)] * 2, 1)

    near, far = backwards(first), backwards(2 * first)
    parts = jnp.concatenate(halves(weighted), 1)
    lane_group = (lax.broadcasted_iota(jnp.int32, (1, 2 * channels), 1) % channels) // (
        channels // groups
    )
    contract = (((1,), (1,)), ((), ()))
    masks = [jnp.where(lane_group == g, 1.0, 0.0).astype(BF16) for g in range(groups)]
    sides = jnp.concatenate([parts[:taps] * mask for mask in masks], 0)
    ends = jnp.concatenate([parts[taps:].astype(F32) * mask.astype(F32) for mask in masks], 0)
    bodies = lax.dot_general(sides, near, contract, preferred_element_type=F32)
    tails = lax.dot_general(ends.astype(BF16), far, contract, preferred_element_type=F32)
    for g in range(groups):
        body = bodies[g * taps : (g + 1) * taps]
        tail = tails[g * spare : (g + 1) * spare]
        body = jnp.concatenate([body[: taps - spare], body[taps - spare :] + tail], 0)
        skewed = pltpu.roll(body, 0, 1, stride=1, stride_axis=0)
        line = jnp.sum(skewed, axis=0, keepdims=True)
        taps_out[g : g + 1, :] = pltpu.roll(line, span - (taps - 1), 1)[:, :taps]


def tap_grad(grads, query, mixed, groups, taps):
    rows, channels = query.shape
    ext = mixed.shape[0]
    block = 128 if channels % 128 == 0 else channels
    steps = channels // block
    per_step = groups // steps
    span = 2 * taps
    parts = (1,) * (len(grads) + 2) + (0, 1)
    kernel = functools.partial(tap_grad_kernel, per_step, len(grads))
    return pl.pallas_call(
        functools.partial(by_blocks, kernel, steps, parts),
        out_shape=[
            jax.ShapeDtypeStruct((groups, taps), F32),
            jax.ShapeDtypeStruct((1, channels), F32),
        ],
        in_specs=[VMEM_SPEC] * (len(grads) + 2),
        out_specs=[VMEM_SPEC] * 2,
        compiler_params=pltpu.CompilerParams(vmem_limit_bytes=2 * SMALL_LIMIT),
        cost_estimate=pl.CostEstimate(
            flops=2 * groups * rows * span * 2 * block,
            bytes_accessed=4 * ext * channels + 6 * rows * channels,
            transcendentals=0,
        ),
        name="tap_grad",
    )(*grads, query, mixed)


def add_pairs_kernel(*refs):
    count = len(refs) // 3
    for one, other, out in zip(refs[:count], refs[count : 2 * count], refs[2 * count :]):
        out[...] = one[...] + other[...]


def add_pairs(ones, others):
    return pl.pallas_call(
        add_pairs_kernel,
        out_shape=[jax.ShapeDtypeStruct(one.shape, one.dtype) for one in ones],
        in_specs=[VMEM_SPEC] * (2 * len(ones)),
        out_specs=[VMEM_SPEC] * len(ones),
        compiler_params=pltpu.CompilerParams(vmem_limit_bytes=SMALL_LIMIT),
        name="add_pairs",
    )(*ones, *others)


def branch_order(block, width):
    to = np.arange(3 * block)
    branch, channel = to // block, to % block
    source = 3 * width * (channel // width) + width * branch + channel % width
    return jnp.asarray(np.arange(3 * block)[:, None] == source[None, :], BF16)


def local(tokens, w_in, short_filter, mr_filter, skip, w_out, grad_out):
    high, low = split_axis(lax.axis_size("col"))
    row_size = lax.axis_size("row")
    channels = tokens.shape[1]
    groups, taps = mr_filter.shape
    width = channels // groups
    block = 128 if channels % 128 == 0 else channels

    order = branch_order(block, width)
    gather = Gather(tokens, high, low, True)
    parts = partials(grad_out, w_out, high, low)
    gather.pass_on(parts, gather.late)
    bands, filters = prepare(*after((mr_filter, short_filter), gather.line), order)
    gather.line = after(gather.line, bands, filters)
    projected = gather.finish(w_in, BF16, "project")
    earlier = lax.ppermute(projected, "row", [(r, r + 1) for r in range(row_size - 1)])
    gated, query, mixed = mixing(earlier, projected, order, filters, bands, skip[None], groups)
    parts = after(parts, gather.total)
    gather = Gather(gated, high, low, True)

    parts = list(parts)
    for step in reversed(range(low.bit_length() - 1)):
        moved = after(swap_low(parts.pop(), high, low, step), gather.near)
        at = 0
        for i, part in enumerate(parts):
            count = part.shape[0]
            total = part.astype(F32) + moved[at : at + count].astype(F32)
            parts[i], at = total.astype(BF16), at + count
    gather.pass_on(gather.late)
    sums = after([parts[0][j] for j in range(high)], gather.line)
    grads = [sums[0]] + [shift_high(sums[j], high, low, j) for j in range(1, high)]
    block_out = gather.finish(w_out, BF16, "output", ())
    grads = after(grads, block_out)

    tap_part, skip_part = tap_grad(grads, query, mixed, groups, taps)
    if row_size == 2:
        swap = [(0, 1), (1, 0)]
        other = [lax.ppermute(part, "row", swap) for part in (tap_part, skip_part)]
        filter_grad, skip_grad = add_pairs((tap_part, skip_part), other)
        skip_grad = skip_grad.reshape(-1)
    else:
        filter_grad, skip_grad = lax.psum((tap_part, skip_part.reshape(-1)), "row")
    return (block_out, filter_grad, skip_grad)


def solution(mesh):
    in_specs = (
        P("row", "col"),
        P(None, "col"),
        P(None, "col"),
        P("col", None),
        P("col"),
        P(None, "col"),
        P("row", "col"),
    )
    out_specs = (P("row", "col"), P("col", None), P("col"))
    return jax.shard_map(local, mesh=mesh, in_specs=in_specs, out_specs=out_specs, check_vma=False)
```
